32 devices in a mesh: groups: 2 (over y), section: 8 (over z, x), tensor: 2 (over core).
Axes of the slice: x: 2, y: 2, z: 4, core: 2. Of those that a mesh axis runs over, the one named last changes fastest.
Arguments:
- text_embed: bfloat16 [4096, 8192], P(('groups', 'section'), 'tensor'), parts along dimension 0, may hold values from -6 to 6
- image_embed: bfloat16 [4096, 8192], P(('groups', 'section'), 'tensor'), parts along dimension 0, may hold values from -6 to 6
- image_count: int32 [16], P(('groups', 'section')), parts along dimension 0, may hold values from 64 to 256, as said below
- prompt_len: int32 [16], P(('groups', 'section')), parts along dimension 0, may hold values from 64 to 256, as said below
- embed_target: int32 [4096], P(('groups', 'section')), parts along dimension 0, may hold values from -1 to 2047, as said below
- kv_weight: bfloat16 [8192, 1024], P('section', 'tensor'), may hold values from -0.0625 to 0.0625
- kv_bias: float32 [1024], P('tensor'), may hold values from -3 to 3
- norm_gain: float32 [8192], replicated, may hold values from 0.25 to 1.75
- queries: bfloat16 [16, 4096], P(('groups', 'section'), 'tensor'), parts along dimension 0, may hold values from -240 to 240
- old_pool: bfloat16 [768, 4, 1024], P(('groups', 'section'), None, 'tensor'), parts along dimension 0, may hold values from -6 to 6
- pool_owner: int32 [768], P(('groups', 'section')), parts along dimension 0, may hold values from -1 to 7, as said below
- pool_fill: int32 [768], P(('groups', 'section')), parts along dimension 0, may hold values from 0 to 4, as said below
- block_owner: int32 [1024], P(('groups', 'section')), parts along dimension 0, may hold values from -1 to 7, as said below
Outputs:
- decode_out: bfloat16 [16, 4096], P(('groups', 'section'), 'tensor'), parts along dimension 0
- fresh_cache: bfloat16 [4096, 1024], P(('groups', 'section'), 'tensor'), parts along dimension 0
The draws below stay inside these ranges and needn't reach their ends.
There are 2 independent parts, one for each index of `groups`. The reference program is written for one: setup_inputs(seed, part) draws one part's arguments, and reference() takes and returns one part's arrays. A program takes and returns all parts, laid end to end along the dimension named above; an argument that names none is the same for every part. Nothing has to cross between parts.
Inputs may be any that keep to these rules, and one draw needn't show every extreme that they name: `image_count`: some prefill index has 256 image tokens. `prompt_len`: at least the index's image_count; some index reaches 256. `embed_target`: prefill index times 256 plus position, or -1 for an unused row; every position below its index's image_count is named by exactly one encode row; at most 32 rows of one encode index name one prefill index, and some pairs reach 32 in every draw. `block_owner`: -1 exactly for blocks wholly at or past prompt_len; at most 8 blocks of one prefill index go to one decode index, reached in every draw. `pool_owner`: -1 for an unused block. `pool_fill`: 0 exactly for unused blocks, 1 or more for used ones.
All inputs are finite; a program needn't handle non-finite values.
Results may differ from the reference program's by a relative error of at most 0.012.
The reference program's roundings to bfloat16 on the way count: a program that leaves them out, or rounds other values in their place, can miss the bound.
Values may be sent and summed in bfloat16 or wider, within the bound.
No kernel may reach another device: no remote copies, remote signals or barrier semaphores. Data moves between devices by JAX's collectives and lax.ppermute only.
A program may use at most 64 MiB of HBM per device.

```python
import jax
import jax.numpy as jnp
from jax import lax

D = 8192
HQ = 32
KVH = 4
HD = 128
BLK = 4
PRE = 256
POOL = 48
KVC = 1024
CAPE = 32
NBLK = 64
CAPB = 8
N_SECTION = 8


def request_layout(key):
    keys = jax.random.split(jax.random.fold_in(key, 101), 4)
    counts = jax.random.randint(keys[0], (N_SECTION,), PRE // 4, PRE + 1)
    chosen = jax.random.randint(keys[1], (), 0, N_SECTION)
    counts = jnp.where(jnp.arange(N_SECTION) == chosen, PRE, counts)
    extra = jax.random.randint(keys[2], (N_SECTION,), 0, PRE + 1)
    lengths = jnp.minimum(counts + extra, PRE)
    offsets = jax.random.randint(keys[3], (N_SECTION,), 0, N_SECTION)
    return (counts.astype(jnp.int32), lengths.astype(jnp.int32), offsets.astype(jnp.int32))


def pool_layout(key):
    keys = jax.random.split(jax.random.fold_in(key, 211), 4)
    owners = jax.random.randint(keys[0], (N_SECTION * POOL,), 0, N_SECTION)
    used = jax.random.randint(keys[1], (N_SECTION * POOL,), 0, 4) > 0
    owners = jnp.where(used, owners, -1)
    partial_fill = jax.random.randint(keys[2], (N_SECTION * POOL,), 1, BLK + 1)
    short = jax.random.randint(keys[3], (N_SECTION * POOL,), 0, 3) == 0
    fills = jnp.where(used, jnp.where(short, partial_fill, BLK), 0)
    return (owners.astype(jnp.int32), fills.astype(jnp.int32))


def draw_image_count(key, part):
    counts, lengths, offsets = request_layout(key)
    return counts


def draw_prompt_len(key, part):
    counts, lengths, offsets = request_layout(key)
    return lengths


def draw_embed_target(key, part):
    counts, lengths, offsets = request_layout(key)
    key = jax.random.fold_in(key, 3)
    encoder = jnp.arange(N_SECTION, dtype=jnp.int32)[:, None]
    slot_row = jnp.arange(PRE, dtype=jnp.int32)[None, :]
    prefill = slot_row // CAPE
    within = slot_row % CAPE
    position = (encoder - offsets[prefill]) % N_SECTION + within * N_SECTION
    target = jnp.where(position < counts[prefill], prefill * PRE + position, -1)
    orders = jax.vmap(lambda one: jax.random.permutation(one, PRE))(jax.random.split(key, N_SECTION))
    target = jnp.take_along_axis(target, orders, axis=1)
    return target.reshape(-1).astype(jnp.int32)


def draw_block_owner(key, part):
    counts, lengths, offsets = request_layout(key)
    key = jax.random.fold_in(key, 5)
    orders = jax.vmap(lambda one: jax.random.permutation(one, N_SECTION))(jax.random.split(key, N_SECTION))
    block_index = jnp.arange(NBLK, dtype=jnp.int32)
    target_index = orders[:, block_index % N_SECTION]
    live = block_index[None, :] * BLK < lengths[:, None]
    owner = jnp.where(live, target_index, -1)
    return owner.reshape(-1).astype(jnp.int32)


def draw_pool_owner(key, part):
    owners, fills = pool_layout(key)
    return owners


def draw_pool_fill(key, part):
    owners, fills = pool_layout(key)
    return fills


def draw_queries(key, part):
    key = jax.random.fold_in(key, 13)
    first = jax.random.fold_in(key, 0)
    base = jnp.clip(jax.random.normal(first, (N_SECTION, HQ * HD), jnp.float32), -6.0, 6.0)
    factor = 2.0
    return (base * factor).astype(jnp.bfloat16)


def block_levels(key, shape, cuts, smallest, top_value):
    def one(axis_at, parts):
        draws = jax.random.uniform(jax.random.fold_in(jax.random.fold_in(key, 6), axis_at), (parts,), jnp.float32, smallest / len(cuts), top_value / len(cuts))
        return jnp.repeat(jnp.exp(draws), shape[axis_at] // parts).reshape((-1,) + (1,) * (len(shape) - axis_at - 1))

    level = one(*cuts[0])
    for cut in cuts[1:]:
        level = level * one(*cut)
    return level


def scatter_about(stream_key, dims, spread, bound, cuts=(), kind=jnp.bfloat16):
    gain = block_levels(stream_key, dims, cuts, -0.22, 0.18) if cuts else 1.0
    result = jax.random.normal(stream_key, dims, jnp.float32) * spread * gain
    return jnp.minimum(jnp.maximum(result, -bound), bound).astype(kind)


def setup_inputs(seed: int = 0, part: int = 0) -> dict:
    arg_keys = jax.random.split(jax.random.key(seed), 14)
    own_keys = jax.random.split(jax.random.fold_in(arg_keys[13], part), 14)
    return {
        "text_embed": scatter_about(own_keys[0], (N_SECTION * PRE, D), 1.0, 6.0, ((0, 8), (1, 2))),
        "image_embed": scatter_about(own_keys[1], (N_SECTION * PRE, D), 1.0, 6.0, ((0, 8), (1, 2))),
        "image_count": draw_image_count(jax.random.fold_in(jax.random.fold_in(arg_keys[13], part), 71), part),
        "prompt_len": draw_prompt_len(jax.random.fold_in(jax.random.fold_in(arg_keys[13], part), 71), part),
        "embed_target": draw_embed_target(jax.random.fold_in(jax.random.fold_in(arg_keys[13], part), 71), part),
        "kv_weight": scatter_about(arg_keys[5], (D, KVC), D ** -0.5, 0.0625, ((0, 8), (1, 2))),
        "kv_bias": scatter_about(arg_keys[6], (KVC,), 0.5, 3.0, ((0, 2),), jnp.float32),
        "norm_gain": jnp.clip(1.0 + 0.15 * jax.random.normal(arg_keys[7], (D,), jnp.float32), 0.25, 1.75),
        "queries": draw_queries(jax.random.fold_in(jax.random.fold_in(arg_keys[13], part), 71), part),
        "old_pool": scatter_about(own_keys[9], (N_SECTION * POOL, BLK, KVC), 1.0, 6.0, ((0, 8), (2, 2))),
        "pool_owner": draw_pool_owner(jax.random.fold_in(jax.random.fold_in(arg_keys[13], part), 71), part),
        "pool_fill": draw_pool_fill(jax.random.fold_in(jax.random.fold_in(arg_keys[13], part), 71), part),
        "block_owner": draw_block_owner(jax.random.fold_in(jax.random.fold_in(arg_keys[13], part), 71), part),
    }


def normalize(rows, norm_gain):
    values = rows.astype(jnp.float32)
    factor = lax.rsqrt(lax.optimization_barrier(jnp.mean(values * values, axis=-1, keepdims=True)) + 1e-06)
    return (values * factor * norm_gain[None, :]).astype(jnp.bfloat16)

def rounded(values):
    return lax.optimization_barrier(values.astype(jnp.bfloat16)).astype(jnp.float32)

def reference(text_embed, image_embed, image_count, prompt_len, embed_target, kv_weight, kv_bias, norm_gain, queries, old_pool, pool_owner, pool_fill, block_owner):
    total_rows = N_SECTION * PRE
    target_row = jnp.where(embed_target >= 0, embed_target, total_rows).astype(jnp.int32)
    placed = jnp.zeros((total_rows, D), jnp.bfloat16).at[target_row].set(image_embed, mode='drop')
    filled = jnp.zeros((total_rows,), jnp.bool_).at[target_row].set(True, mode='drop')
    positions = jnp.arange(total_rows, dtype=jnp.int32)
    owner_index = positions // PRE
    keep = filled & (positions % PRE < image_count[owner_index])
    assembled = jnp.where(keep[:, None], placed, text_embed)

    def prefill(rows):
        normed = normalize(rows, norm_gain)
        product = jnp.dot(normed, kv_weight, preferred_element_type=jnp.float32)
        return (product + kv_bias[None, :]).astype(jnp.bfloat16)
    key_value = lax.map(prefill, assembled.reshape(N_SECTION, PRE, D))
    blocks = key_value.reshape(N_SECTION * NBLK, BLK, KVC)
    live = block_owner >= 0
    destination = jnp.where(live, block_owner, 0).astype(jnp.int32)
    hits = ((destination[:, None] == jnp.arange(N_SECTION, dtype=jnp.int32)[None, :]) & live[:, None]).astype(jnp.int32)
    hits = hits.reshape(N_SECTION, NBLK, N_SECTION)
    slot_rank = lax.optimization_barrier(jnp.sum(hits * (jnp.cumsum(hits, axis=1) - 1), axis=2)).reshape(-1)
    source = jnp.arange(N_SECTION * NBLK, dtype=jnp.int32) // NBLK
    block_index = jnp.arange(N_SECTION * NBLK, dtype=jnp.int32) % NBLK
    slots = N_SECTION * N_SECTION * CAPB
    flat_slot = jnp.where(live, (destination * N_SECTION + source) * CAPB + slot_rank, slots).astype(jnp.int32)
    fresh = jnp.zeros((slots, BLK, KVC), jnp.bfloat16).at[flat_slot].set(blocks, mode='drop')
    valid_rows = jnp.clip(prompt_len[source] - block_index * BLK, 0, BLK).astype(jnp.int32)
    slot_valid = jnp.zeros((slots,), jnp.int32).at[flat_slot].set(valid_rows, mode='drop')
    fresh_keys_all = fresh.reshape(slots * BLK, KVC)
    per_index = N_SECTION * CAPB * BLK
    group = HQ // KVH
    scale = HD ** (-0.5)
    query_heads = queries.astype(jnp.float32).reshape(N_SECTION, KVH, group, HD)
    requests = jnp.arange(N_SECTION, dtype=jnp.int32)

    def partial_value(device):
        device = device.astype(jnp.int32)
        pool = lax.dynamic_slice_in_dim(old_pool, device * POOL, POOL, 0).astype(jnp.float32).reshape(POOL, BLK, KVH, 2, HD)
        owners = lax.dynamic_slice_in_dim(pool_owner, device * POOL, POOL, 0)
        fills = lax.dynamic_slice_in_dim(pool_fill, device * POOL, POOL, 0)
        fresh_here = lax.dynamic_slice_in_dim(fresh_keys_all, device * per_index, per_index, 0).astype(jnp.float32).reshape(N_SECTION, CAPB * BLK, KVH, 2, HD)
        valids = lax.dynamic_slice_in_dim(slot_valid, device * N_SECTION * CAPB, N_SECTION * CAPB, 0).reshape(N_SECTION, CAPB)
        fresh_mask = (jnp.arange(CAPB * BLK, dtype=jnp.int32) % BLK)[None, :] < jnp.repeat(valids, BLK, axis=1)
        fresh_scores = jnp.einsum('phgd,pkhd->phgk', query_heads, fresh_here[:, :, :, 0, :], precision=lax.Precision.HIGHEST) * scale
        fresh_scores = jnp.where(fresh_mask[:, None, None, :], fresh_scores, -jnp.inf)
        safe_owner = jnp.where(owners >= 0, owners, 0).astype(jnp.int32)
        block_query = query_heads[safe_owner]
        old_scores = jnp.einsum('bhgd,bkhd->bhgk', block_query, pool[:, :, :, 0, :], precision=lax.Precision.HIGHEST) * scale
        old_mask = (jnp.arange(BLK, dtype=jnp.int32)[None, :] < fills[:, None]) & (owners >= 0)[:, None]
        old_scores = jnp.where(old_mask[:, None, None, :], old_scores, -jnp.inf)
        onehot = owners[None, :] == requests[:, None]
        block_top = lax.optimization_barrier(jnp.max(old_scores, axis=-1))
        old_top = lax.optimization_barrier(jnp.max(jnp.where(onehot[:, :, None, None], block_top[None], -jnp.inf), axis=1))
        top = jnp.maximum(jnp.maximum(lax.optimization_barrier(jnp.max(fresh_scores, axis=-1)), old_top), -1e+30)
        fresh_expo = jnp.exp(fresh_scores - top[..., None])
        old_expo = jnp.exp(old_scores - top[safe_owner][..., None])
        selector = onehot.astype(jnp.float32)
        total = lax.optimization_barrier(jnp.sum(fresh_expo, axis=-1)) + jnp.einsum('rb,bhg->rhg', selector, lax.optimization_barrier(jnp.sum(old_expo, axis=-1)), precision=lax.Precision.HIGHEST)
        fresh_acc = jnp.einsum('phgk,pkhd->phgd', rounded(fresh_expo), fresh_here[:, :, :, 1, :], precision=lax.Precision.HIGHEST)
        block_acc = jnp.einsum('bhgk,bkhd->bhgd', rounded(old_expo), pool[:, :, :, 1, :], precision=lax.Precision.HIGHEST)
        acc = fresh_acc + jnp.einsum('rb,bhgd->rhgd', selector, block_acc, precision=lax.Precision.HIGHEST)
        return (top, total, acc)

    def fold(carry, device):
        best, total, acc = carry
        top, part_total, part_acc = partial_value(device)
        newest = jnp.maximum(best, top)
        before = jnp.exp(best - newest)
        after = jnp.exp(top - newest)
        return ((newest, total * before + part_total * after, acc * before[..., None] + part_acc * after[..., None]), None)
    start = (jnp.full((N_SECTION, KVH, group), -1e+30, jnp.float32), jnp.zeros((N_SECTION, KVH, group), jnp.float32), jnp.zeros((N_SECTION, KVH, group, HD), jnp.float32))
    final, unused = lax.scan(fold, start, jnp.arange(N_SECTION, dtype=jnp.int32))
    decode_out = (final[2] / final[1][..., None]).astype(jnp.bfloat16).reshape(N_SECTION, HQ * HD)
    return (decode_out, fresh_keys_all)
```

```python
import functools

import jax
import jax.numpy as jnp
import numpy as np
from jax import lax
from jax.experimental import pallas as pl
from jax.experimental.pallas import tpu as pltpu
from jax.sharding import PartitionSpec as P

HQ = 32
KVH = 4
HD = 128
GROUP = HQ // KVH
SCALE = HD ** (-0.5)
LANES = 128
NEG = -1e30
VMEM = 60 * 1024 * 1024


def iota(shape, dim):
    return lax.broadcasted_iota(jnp.int32, shape, dim)


def call(kernel, outs, *args, cost=None, smem=()):
    return pl.pallas_call(
        kernel,
        out_shape=outs,
        in_specs=[
            pl.BlockSpec(memory_space=pltpu.SMEM if i in smem else pltpu.VMEM)
            for i in range(len(args))
        ],
        out_specs=jax.tree.map(lambda _: pl.BlockSpec(memory_space=pltpu.VMEM), outs),
        compiler_params=pltpu.CompilerParams(vmem_limit_bytes=VMEM),
        cost_estimate=cost,
    )(*args)


def cost(flops, nbytes):
    return pl.CostEstimate(flops=int(flops), bytes_accessed=int(nbytes), transcendentals=0)


def rank_before(hits):
    items = hits.shape[1]
    earlier = (iota((items, items), 0) < iota((items, items), 1)).astype(jnp.bfloat16)
    before = jnp.dot(hits.astype(jnp.bfloat16), earlier, preferred_element_type=jnp.float32)
    return jnp.sum(before * hits, axis=0, keepdims=True).astype(jnp.int32)


def prep_kernel(
    sections, cape, capr, image_ref, place_ref, owner_ref, query_ref, out_slot, out_block, out_message
):
    target, place, owner = image_ref[...], place_ref[...], owner_ref[...]
    hits = ((target == iota((sections, target.shape[1]), 0)) & (target >= 0)).astype(jnp.float32)
    rank = rank_before(hits)
    out_slot[...] = jnp.where(target >= 0, target * cape + rank, -1)
    at_rank = (rank == iota((LANES, target.shape[1]), 0)).astype(jnp.bfloat16)
    numbered = (hits * (place + 1).astype(jnp.float32)).astype(jnp.bfloat16)
    positions = lax.dot_general(
        numbered, at_rank, (((1,), (1,)), ((), ())), preferred_element_type=jnp.float32
    )
    positions = (positions - 1.0).astype(jnp.bfloat16)
    query = query_ref[...]
    heads = query.shape[0]
    out_message[:, :heads, :] = jnp.broadcast_to(query[None], (sections,) + query.shape)
    out_message[:, heads:, :] = jnp.broadcast_to(
        positions[:, None, :], (sections, out_message.shape[1] - heads, LANES)
    )
    owner_hits = ((owner == iota((sections, owner.shape[1]), 0)) & (owner >= 0)).astype(jnp.float32)
    out_block[...] = jnp.where(owner >= 0, owner * capr + rank_before(owner_hits), -1)


def norm_kernel(
    blocks, features, swap_width, slot_ref, text, image, text_far, image_far, gain, gain_far, out_ref
):
    half, width = blocks // 2, out_ref.shape[3]
    swap = slot_ref[blocks]
    for kind, (near_ref, far_ref) in enumerate(((text, text_far), (image, image_far))):
        near = near_ref[...].astype(jnp.float32)
        far = far_ref[...].astype(jnp.float32)
        total = jnp.sum(near * near, axis=1, keepdims=True) + jnp.sum(
            far * far, axis=1, keepdims=True
        )
        factor = lax.rsqrt(total * (1.0 / features) + 1e-06)
        for side, (ref, gains) in enumerate(((near_ref, gain), (far_ref, gain_far))):
            for j in range(half):
                at = pl.ds(j * width, width)
                block = ref[:, at].astype(jnp.float32) * factor * gains[:, at]
                block = block.astype(jnp.bfloat16)
                slot = slot_ref[side * half + j]
                out_ref[slot, kind] = block
                if swap_width:
                    turned = (swap > 0) & (slot > 0)

                    @pl.when(turned)
                    def _():
                        out_ref[slot, kind, :, :swap_width] = block[:, width - swap_width :]
                        out_ref[slot, kind, :, width - swap_width :] = block[:, :swap_width]


def normalize(slots, blocks, swap_width, text, image, text_far, image_far, gain, gain_far):
    rows, near = text.shape
    width = 2 * near // blocks
    tile = 32
    rows_spec = pl.BlockSpec((tile, near), lambda i, s: (i, 0))
    gain_spec = pl.BlockSpec((1, near), lambda i, s: (0, 0))
    return pl.pallas_call(
        functools.partial(norm_kernel, blocks, 2 * near, swap_width),
        out_shape=jax.ShapeDtypeStruct((blocks, 2, rows, width), jnp.bfloat16),
        grid_spec=pltpu.PrefetchScalarGridSpec(
            num_scalar_prefetch=1,
            grid=(rows // tile,),
            in_specs=[rows_spec] * 4 + [gain_spec] * 2,
            out_specs=pl.BlockSpec((blocks, 2, tile, width), lambda i, s: (0, 0, i, 0)),
        ),
        compiler_params=pltpu.CompilerParams(vmem_limit_bytes=VMEM),
        cost_estimate=cost(0, 8 * rows * 2 * near),
    )(slots, text, image, text_far, image_far, gain, gain_far)


def pool_kernel(message_ref, pool_ref, owner_ref, out_ref):
    sections, heads = out_ref.shape[0], out_ref.shape[1]
    keys = owner_ref.shape[1]
    owned = owner_ref[...] == iota((sections * GROUP, keys), 0) // GROUP
    for h in range(heads // GROUP):
        query = message_ref[:, h * GROUP : (h + 1) * GROUP, :].astype(jnp.float32)
        query = query.reshape(sections * GROUP, HD).astype(jnp.bfloat16)
        key = pool_ref[:, 2 * h * HD : (2 * h + 1) * HD]
        value = pool_ref[:, (2 * h + 1) * HD : (2 * h + 2) * HD]
        top, total, acc = attend(query, key, value, owned)
        lane = iota((sections * GROUP, LANES), 1)
        state = jnp.where(lane == 0, top, jnp.where(lane == 1, total, 0.0))
        out_ref[:, h * GROUP : (h + 1) * GROUP, :HD] = acc.reshape(sections, GROUP, HD)
        out_ref[:, h * GROUP : (h + 1) * GROUP, HD:] = state.reshape(sections, GROUP, LANES)


def attend(query, key, value, mask):
    scores = (
        lax.dot_general(query, key, (((1,), (1,)), ((), ())), preferred_element_type=jnp.float32)
        * SCALE
    )
    scores = jnp.where(mask, scores, NEG)
    top = jnp.max(scores, axis=1, keepdims=True)
    expo = jnp.where(mask, jnp.exp(scores - top), 0.0)
    total = jnp.sum(expo, axis=1, keepdims=True)
    acc = jnp.dot(expo.astype(jnp.bfloat16), value, preferred_element_type=jnp.float32)
    return top, total, acc


def finish_kernel(acc_ref, bias_ref, slot_ref, text_ref, send_ref):
    rows = text_ref.shape[0]
    text_ref[...] = (acc_ref[:rows] + bias_ref[...]).astype(jnp.bfloat16)
    image = (acc_ref[rows:] + bias_ref[...]).astype(jnp.bfloat16)
    place = (iota((send_ref.shape[0], rows), 0) == slot_ref[...]).astype(jnp.bfloat16)
    send_ref[...] = jnp.dot(place, image, preferred_element_type=jnp.float32).astype(jnp.bfloat16)


def place_kernel(text_ref, arrived_ref, position_ref, slot_ref, count_ref, rows_ref, blocks_ref):
    rows = text_ref.shape[0]
    row = iota((rows, arrived_ref.shape[0]), 0)
    match = (row == position_ref[...]) & (row < count_ref[0])
    filled = jnp.max(match.astype(jnp.float32), axis=1, keepdims=True) > 0.0
    placed = jnp.dot(
        match.astype(jnp.bfloat16), arrived_ref[...], preferred_element_type=jnp.float32
    )
    whole = jnp.where(filled, placed, text_ref[...].astype(jnp.float32)).astype(jnp.bfloat16)
    rows_ref[...] = whole
    slots = (iota((blocks_ref.shape[0], rows), 0) == slot_ref[...]).astype(jnp.bfloat16)
    blocks_ref[...] = jnp.dot(slots, whole, preferred_element_type=jnp.float32).astype(jnp.bfloat16)


def decode_kernel(rows_ref, query_ref, partial_ref, length_ref, out_ref):
    rows = rows_ref.shape[0]
    mask = iota((GROUP, rows), 1) < length_ref[0]
    for h in range(query_ref.shape[0] // GROUP):
        at = slice(h * GROUP, (h + 1) * GROUP)
        key = rows_ref[:, 2 * h * HD : (2 * h + 1) * HD]
        value = rows_ref[:, (2 * h + 1) * HD : (2 * h + 2) * HD]
        top, total, acc = attend(query_ref[at, :], key, value, mask)
        old_acc = partial_ref[:, at, :HD]
        old_top = partial_ref[:, at, HD : HD + 1]
        old_total = partial_ref[:, at, HD + 1 : HD + 2]
        best = jnp.maximum(top, jnp.max(old_top, axis=0))
        fresh_factor = jnp.exp(top - best)
        old_factor = jnp.exp(old_top - best[None])
        total = total * fresh_factor + jnp.sum(old_total * old_factor, axis=0)
        acc = acc * fresh_factor + jnp.sum(old_acc * old_factor, axis=0)
        out_ref[at, :] = (acc / total).astype(jnp.bfloat16)


def ring_order(sections):
    return list(range(0, sections, 2)) + list(range(1, sections, 2))[::-1]


def feature_slots(sections, tensors, ring):
    if not ring:
        return np.array([[[t, 1 - t] for t in range(tensors)] for _ in range(sections)], np.int32)
    order = ring_order(sections)
    table = np.zeros((sections, tensors, sections), np.int32)
    distances = [0] + [s * d for d in range(1, sections // 2) for s in (1, -1)] + [sections // 2]
    for at, section in enumerate(order):
        for slot, distance in enumerate(distances):
            source = order[(at - distance) % sections]
            for t in range(tensors):
                local = (source - t * (sections // tensors)) % sections
                table[section, t, local] = slot
    return table


def ring_project(normed, weight):
    sections = lax.axis_size("section")
    order = ring_order(sections)
    ahead = [(order[i], order[(i + 1) % sections]) for i in range(sections)]
    back = [(b, a) for a, b in ahead]
    depth = weight.shape[0]
    part = depth // 4
    index = lax.axis_index("groups")

    def up(x):
        return lax.ppermute(x, "section", ahead)

    def down(x):
        return lax.ppermute(x, "section", back)

    def across(x):
        return lax.ppermute(x, "groups", [(0, 1), (1, 0)])

    def product(slot, first, last, block):
        return jnp.dot(normed[slot, :, first:last], block, preferred_element_type=jnp.float32)

    own = lax.dynamic_slice_in_dim(weight, index * (depth - part), part, 0)
    middle = weight[part : depth - part]
    acc = product(0, 0, depth, weight)
    up_own, up_middle, down_own, down_middle = own, middle, own, middle
    slot = 1
    for _ in range(1, sections // 2):
        up_own, down_own = up(up_own), down(down_own)
        up_far, down_far = across(up_own), across(down_own)
        up_middle, down_middle = up(up_middle), down(down_middle)
        for near, mid, far in ((up_own, up_middle, up_far), (down_own, down_middle, down_far)):
            acc = acc + product(slot, 0, depth, jnp.concatenate([near, mid, far], 0))
            slot += 1
    last_own = up(up_own)
    last_far = across(last_own)
    eighth = part // 2
    last_middle = jnp.concatenate([up(up_middle[:eighth]), down(down_middle[eighth:])], 0)
    return acc + product(slot, 0, depth, jnp.concatenate([last_own, last_middle, last_far], 0))


def gather_project(normed, weight):
    whole = lax.all_gather(weight, "section", axis=0, tiled=True)
    width = normed.shape[2]
    acc = jnp.dot(normed[0], whole[:width], preferred_element_type=jnp.float32)
    return acc + jnp.dot(normed[1], whole[width:], preferred_element_type=jnp.float32)


def shards(
    text_embed,
    image_embed,
    image_count,
    prompt_len,
    embed_target,
    kv_weight,
    kv_bias,
    norm_gain,
    queries,
    old_pool,
    pool_owner,
    pool_fill,
    block_owner,
):
    sections, tensors = lax.axis_size("section"), lax.axis_size("tensor")
    rows, near = text_embed.shape
    width = kv_weight.shape[1]
    heads = queries.shape[1] // HD
    cape = rows // sections
    block_rows = old_pool.shape[1]
    capr = (block_owner.shape[0] + sections - 1) // sections * block_rows
    ring = (
        sections <= 16
        and sections % (2 * tensors) == 0
        and lax.axis_size("groups") == 2
        and kv_weight.shape[0] % (8 * LANES) == 0
    )
    section, tensor = lax.axis_index("section"), lax.axis_index("tensor")

    def exchange(x):
        return lax.all_to_all(x, "section", split_axis=0, concat_axis=0, tiled=True)

    def beside(x):
        return lax.ppermute(x, "tensor", [(0, 1), (1, 0)])

    table = feature_slots(sections, tensors, ring)
    blocks = table.shape[2]
    turn = lax.axis_index("groups").astype(jnp.int32).reshape(1)
    slots = lax.dynamic_slice(jnp.asarray(table), (section, tensor, 0), (1, 1, blocks))
    slots = jnp.concatenate([slots.reshape(blocks), turn])
    gains = norm_gain.reshape(tensors, near)
    gain = lax.dynamic_slice(gains, (tensor, 0), (1, near))
    gain_far = lax.dynamic_slice(gains, (1 - tensor, 0), (1, near))
    normed = normalize(
        slots,
        blocks,
        kv_weight.shape[0] // 4 if ring else 0,
        text_embed,
        image_embed,
        beside(text_embed),
        beside(image_embed),
        gain,
        gain_far,
    ).reshape(blocks, 2 * rows, -1)

    target = embed_target.reshape(1, rows)
    owner_rows = jnp.repeat(block_owner, block_rows).reshape(1, -1)
    query = queries.reshape(heads, HD)
    image_slot, block_slot, message = call(
        functools.partial(prep_kernel, sections, cape, capr),
        (
            jax.ShapeDtypeStruct((1, rows), jnp.int32),
            jax.ShapeDtypeStruct((1, owner_rows.shape[1]), jnp.int32),
            jax.ShapeDtypeStruct((sections, 2 * heads, LANES), jnp.bfloat16),
        ),
        jnp.where(target >= 0, target // rows, -1),
        target % rows,
        owner_rows,
        query,
    )
    message = exchange(message)
    position = message[:, heads, :cape].astype(jnp.int32).reshape(1, sections * cape)

    pool_rows = old_pool.reshape(-1, width)
    held = jnp.arange(block_rows, dtype=jnp.int32)[None, :] < pool_fill[:, None]
    held_owner = jnp.where(held, pool_owner[:, None], -1).reshape(1, -1)
    partial = exchange(
        call(
            pool_kernel,
            jax.ShapeDtypeStruct((sections, heads, 2 * HD), jnp.float32),
            message,
            pool_rows,
            held_owner,
        )
    )

    acc = (ring_project if ring else gather_project)(normed, kv_weight)
    text_rows, send = call(
        finish_kernel,
        (
            jax.ShapeDtypeStruct((rows, width), jnp.bfloat16),
            jax.ShapeDtypeStruct((sections * cape, width), jnp.bfloat16),
        ),
        acc,
        kv_bias.reshape(1, width),
        image_slot,
    )
    arrived = exchange(send.reshape(sections, cape, width)).reshape(sections * cape, width)
    whole_rows, block_data = call(
        place_kernel,
        (
            jax.ShapeDtypeStruct((rows, width), jnp.bfloat16),
            jax.ShapeDtypeStruct((sections * capr, width), jnp.bfloat16),
        ),
        text_rows,
        arrived,
        position,
        block_slot,
        image_count,
        smem=(4,),
    )
    fresh = exchange(block_data.reshape(sections, capr, width)).reshape(sections * capr, width)
    decoded = call(
        decode_kernel,
        jax.ShapeDtypeStruct((heads, HD), jnp.bfloat16),
        whole_rows,
        query,
        partial,
        prompt_len,
        smem=(3,),
    )
    return decoded.reshape(1, heads * HD), fresh


def solution(mesh):
    return jax.shard_map(
        shards,
        mesh=mesh,
        in_specs=(
            P(("groups", "section"), "tensor"),
            P(("groups", "section"), "tensor"),
            P(("groups", "section")),
            P(("groups", "section")),
            P(("groups", "section")),
            P("section", "tensor"),
            P("tensor"),
            P(),
            P(("groups", "section"), "tensor"),
            P(("groups", "section"), None, "tensor"),
            P(("groups", "section")),
            P(("groups", "section")),
            P(("groups", "section")),
        ),
        out_specs=(P(("groups", "section"), "tensor"), P(("groups", "section"), "tensor")),
        check_vma=False,
    )
```

```python
import functools

import jax
import jax.numpy as jnp
import numpy as np
from jax import lax
from jax.experimental import pallas as pl
from jax.experimental.pallas import tpu as pltpu
from jax.sharding import PartitionSpec as P

HQ = 32
KVH = 4
HD = 128
GROUP = HQ // KVH
SCALE = HD ** (-0.5)
LANES = 128
NEG = -1e30
VMEM = 24 * 1024 * 1024


def iota(shape, dim):
    return lax.broadcasted_iota(jnp.int32, shape, dim)


def call(kernel, outs, *args, cost=None, smem=(), aliases=None):
    return pl.pallas_call(
        kernel,
        out_shape=outs,
        in_specs=[
            pl.BlockSpec(memory_space=pltpu.SMEM if i in smem else pltpu.VMEM)
            for i in range(len(args))
        ],
        out_specs=jax.tree.map(lambda _: pl.BlockSpec(memory_space=pltpu.VMEM), outs),
        input_output_aliases=aliases or {},
        compiler_params=pltpu.CompilerParams(vmem_limit_bytes=VMEM),
        cost_estimate=cost,
    )(*args)


def cost(flops, nbytes):
    return pl.CostEstimate(flops=int(flops), bytes_accessed=int(nbytes), transcendentals=0)


def rank_before(hits):
    items = hits.shape[1]
    earlier = (iota((items, items), 0) < iota((items, items), 1)).astype(jnp.bfloat16)
    before = jnp.dot(hits.astype(jnp.bfloat16), earlier, preferred_element_type=jnp.float32)
    return jnp.sum(before * hits, axis=0, keepdims=True).astype(jnp.int32)


def spread(values, items):
    groups = values.shape[1]
    share = items // groups
    same = iota((groups, items), 0) * share
    column = iota((groups, items), 1)
    same = ((column >= same) & (column < same + share)).astype(jnp.bfloat16)
    wide = jnp.broadcast_to(values.astype(jnp.float32), (8, groups)).astype(jnp.bfloat16)
    wide = jnp.dot(wide, same, preferred_element_type=jnp.float32)
    return wide[:1].astype(jnp.int32)


def image_slots(target, sections, cape):
    rows = target.shape[1]
    index = jnp.floor((target.astype(jnp.float32) + 0.5) * (1.0 / rows)).astype(jnp.int32)
    place = target - index * rows
    hits = ((index == iota((sections, rows), 0)) & (target >= 0)).astype(jnp.float32)
    rank = rank_before(hits)
    at_rank = (rank == iota((LANES, rows), 0)).astype(jnp.bfloat16)
    numbered = (hits * (place + 1).astype(jnp.float32)).astype(jnp.bfloat16)
    positions = lax.dot_general(
        numbered, at_rank, (((1,), (1,)), ((), ())), preferred_element_type=jnp.float32
    )
    return jnp.where(target >= 0, index * cape + rank, -1), positions - 1.0


def block_slots(owner, sections, capr, block_rows):
    owner = spread(owner, owner.shape[1] * block_rows)
    hits = ((owner == iota((sections, owner.shape[1]), 0)) & (owner >= 0)).astype(jnp.float32)
    return jnp.where(owner >= 0, owner * capr + rank_before(hits), -1)


def query_group(query_ref, h):
    heads = [
        query_ref[:, j * HD : (j + 1) * HD].astype(jnp.float32)
        for j in range(h * GROUP, (h + 1) * GROUP)
    ]
    return jnp.concatenate(heads, axis=0)


def prep_kernel(
    sections, cape, capr, block_rows, target_ref, owner_ref, query_ref, out_slot, out_block, out_message
):
    out_slot[...], positions = image_slots(target_ref[...], sections, cape)
    heads = query_ref.shape[1] // HD
    query = jnp.concatenate([query_group(query_ref, h) for h in range(heads // GROUP)], axis=0)
    query = query.astype(jnp.bfloat16)
    out_message[:, :heads, :] = jnp.broadcast_to(query[None], (sections,) + query.shape)
    out_message[:, heads:, :] = jnp.broadcast_to(
        positions.astype(jnp.bfloat16)[:, None, :], (sections, out_message.shape[1] - heads, LANES)
    )
    out_block[...] = block_slots(owner_ref[...], sections, capr, block_rows)


def open_kernel(
    sections, cape, capr, block_rows, group_ref, weight_ref, target_ref, owner_ref, query_ref,
    out_own, out_middle, out_slot, out_block
):
    part = out_middle.shape[0] // 2
    turned = pl.multiple_of(group_ref[0] * (weight_ref.shape[0] - part), part)
    out_own[:part] = weight_ref[pl.ds(turned, part), :]
    out_middle[...] = weight_ref[part : 3 * part, :]
    out_slot[...], positions = image_slots(target_ref[...], sections, cape)
    groups = query_ref.shape[1] // (GROUP * HD)
    told = [query_group(query_ref, h) for h in range(groups)]
    told.append(jnp.zeros((GROUP, out_own.shape[1] - groups * HD), jnp.float32))
    told = jnp.concatenate(told, axis=1)
    positions = jnp.concatenate(
        [positions, jnp.zeros((sections, out_own.shape[1] - LANES), jnp.float32)], axis=1
    )
    out_own[part:] = jnp.concatenate([told, positions], axis=0).astype(jnp.bfloat16)
    out_block[...] = block_slots(owner_ref[...], sections, capr, block_rows)


def norm_kernel(blocks, features, half_ref, near_ref, far_ref, gain, gain_far, out_ref, done_ref):
    half, width = blocks // 2, out_ref.shape[2]
    near = near_ref[...].astype(jnp.float32)
    far = far_ref[...].astype(jnp.float32)
    total = jnp.sum(near * near, axis=1, keepdims=True) + jnp.sum(far * far, axis=1, keepdims=True)
    factor = lax.rsqrt(total * (1.0 / features) + 1e-06)
    for side, (ref, gains) in enumerate(((near_ref, gain), (far_ref, gain_far))):
        for j in range(half):
            at = pl.ds(j * width, width)
            block = ref[:, at].astype(jnp.float32) * factor * gains[:, at]
            out_ref[side * half + j] = block.astype(jnp.bfloat16)
    done_ref[...] = jnp.zeros_like(done_ref)


def normalize(blocks, half, near, far, gains):
    rows, features = near.shape
    width = 2 * features // blocks
    tile = 64
    rows_spec = pl.BlockSpec((tile, features), lambda i, h: (i, 0))
    return pl.pallas_call(
        functools.partial(norm_kernel, blocks, 2 * features),
        out_shape=(
            jax.ShapeDtypeStruct((blocks, rows, width), jnp.bfloat16),
            jax.ShapeDtypeStruct((8, LANES), jnp.float32),
        ),
        grid_spec=pltpu.PrefetchScalarGridSpec(
            num_scalar_prefetch=1,
            grid=(rows // tile,),
            in_specs=[
                rows_spec,
                rows_spec,
                pl.BlockSpec((1, features), lambda i, h: (0, h[0])),
                pl.BlockSpec((1, features), lambda i, h: (0, 1 - h[0])),
            ],
            out_specs=(
                pl.BlockSpec((blocks, tile, width), lambda i, h: (0, i, 0)),
                pl.BlockSpec((8, LANES), lambda i, h: (0, 0)),
            ),
        ),
        compiler_params=pltpu.CompilerParams(vmem_limit_bytes=VMEM),
        cost_estimate=cost(0, 8 * rows * 2 * features),
    )(half, near, far, gains, gains)


def pool_rows(pool_ref):
    block_rows = pool_ref.shape[1]
    pool = pool_ref[...].astype(jnp.float32)
    return jnp.concatenate([pool[:, i, :] for i in range(block_rows)], axis=0).astype(jnp.bfloat16)


def positions_in_slots(sent, source, cape):
    sources = sent.shape[0]
    slots = sources * cape
    column = iota((sources, slots), 1)
    rank = column - jnp.floor((column.astype(jnp.float32) + 0.5) * (1.0 / cape)).astype(jnp.int32) * cape
    at_source = (column >= source * cape) & (column < source * cape + cape)
    at_rank = (iota((LANES, slots), 0) == rank[:1]).astype(jnp.bfloat16)
    wide = jnp.dot(sent.astype(jnp.bfloat16), at_rank, preferred_element_type=jnp.float32)
    return jnp.sum(jnp.where(at_source, wide, 0.0), axis=0, keepdims=True).astype(jnp.int32)


def pool_kernel(cape, message_ref, pool_ref, owner_ref, fill_ref, out_ref, position_ref):
    sections, heads = out_ref.shape[0], out_ref.shape[1]
    held, block_rows, _ = pool_ref.shape
    request = iota((sections * GROUP, held), 0)
    owner = owner_ref[...]
    owned = (request >= owner * GROUP) & (request < owner * GROUP + GROUP)
    mask = jnp.concatenate(
        [(owned & (fill_ref[...] > i)).astype(jnp.float32) for i in range(block_rows)], axis=1
    )
    pool = pool_rows(pool_ref)
    for h in range(heads // GROUP):
        query = message_ref[:, h * GROUP : (h + 1) * GROUP, :].astype(jnp.float32)
        query = query.reshape(sections * GROUP, HD).astype(jnp.bfloat16)
        key = pool[:, 2 * h * HD : (2 * h + 1) * HD]
        value = pool[:, (2 * h + 1) * HD : (2 * h + 2) * HD]
        top, total, acc = attend(query, key, value, mask > 0.0)
        lane = iota((sections * GROUP, LANES), 1)
        state = jnp.where(lane == 0, top, jnp.where(lane == 1, total, 0.0))
        out_ref[:, h * GROUP : (h + 1) * GROUP, :HD] = acc.reshape(sections, GROUP, HD)
        out_ref[:, h * GROUP : (h + 1) * GROUP, HD:] = state.reshape(sections, GROUP, LANES)
    sent = message_ref[:, heads : heads + 1, :].astype(jnp.float32).reshape(sections, LANES)
    position_ref[...] = positions_in_slots(sent, iota((sections, 1), 0), cape)


def ring_pool_kernel(sections, cape, source_ref, *refs):
    told_refs = refs[:sections]
    pool_ref, owner_ref, fill_ref, out_ref, position_ref = refs[sections:]
    held, block_rows, _ = pool_ref.shape
    heads = out_ref.shape[1] // 2
    groups = heads // GROUP
    part = told_refs[0].shape[0] - GROUP - sections
    told = [ref[part:, :].astype(jnp.float32) for ref in told_refs]
    owner, fill = owner_ref[...], fill_ref[...]
    masks = []
    for j in range(sections):
        owned = owner == source_ref[j]
        mask = [(owned & (fill > i)).astype(jnp.float32) for i in range(block_rows)]
        masks.append(jnp.broadcast_to(jnp.concatenate(mask, axis=1), (GROUP, held * block_rows)))
    mask = jnp.concatenate(masks, axis=0) > 0.0
    pool = pool_rows(pool_ref)
    sums, states = [], []
    lane = iota((sections * GROUP, LANES), 1)
    for h in range(groups):
        query = jnp.concatenate([t[:GROUP, h * HD : (h + 1) * HD] for t in told], axis=0)
        key = pool[:, 2 * h * HD : (2 * h + 1) * HD]
        value = pool[:, (2 * h + 1) * HD : (2 * h + 2) * HD]
        top, total, acc = attend(query.astype(jnp.bfloat16), key, value, mask)
        terms = bf16_terms(top, 3) + bf16_terms(total, 2)
        state = jnp.zeros((sections * GROUP, LANES), jnp.float32)
        for k, term in enumerate(terms):
            state = jnp.where(lane == k, term, state)
        sums.append(acc)
        states.append(state)
    for j in range(sections):
        at = slice(j * GROUP, (j + 1) * GROUP)
        rows = jnp.concatenate([x[at] for x in sums] + [x[at] for x in states], axis=0)
        out_ref[source_ref[j]] = rows.astype(jnp.bfloat16)
    own = iota((sections, LANES), 0) == source_ref[0]
    sent = jnp.concatenate(
        [
            jnp.sum(jnp.where(own, t[GROUP:, :LANES], 0.0), axis=0, keepdims=True) for t in told
        ],
        axis=0,
    )
    source = jnp.zeros((sections, 1), jnp.int32)
    for j in range(sections):
        source = jnp.where(iota((sections, 1), 0) == j, source_ref[j], source)
    position_ref[...] = positions_in_slots(sent, source, cape)


def bf16_terms(value, count):
    terms = []
    for _ in range(count):
        term = value.astype(jnp.bfloat16).astype(jnp.float32)
        terms.append(term)
        value = value - term
    return terms


def attend(query, key, value, mask):
    scores = (
        lax.dot_general(query, key, (((1,), (1,)), ((), ())), preferred_element_type=jnp.float32)
        * SCALE
    )
    scores = jnp.where(mask, scores, NEG)
    top = jnp.max(scores, axis=1, keepdims=True)
    expo = jnp.where(mask, jnp.exp(scores - top), 0.0)
    total = jnp.sum(expo, axis=1, keepdims=True)
    acc = jnp.dot(expo.astype(jnp.bfloat16), value, preferred_element_type=jnp.float32)
    return top, total, acc


def product(rows_ref, block, quarter_ref, weights):
    near, middle, far = weights
    part = middle.shape[0] // 2
    turned = quarter_ref[0] * (2 * part + part)
    near_at = pl.multiple_of(turned, part)
    far_at = pl.multiple_of(3 * part - turned, part)

    def times(at, weight):
        return jnp.dot(rows_ref[block, :, at], weight, preferred_element_type=jnp.float32)

    return (
        times(pl.ds(part, 2 * part), middle)
        + times(pl.ds(near_at, part), near)
        + times(pl.ds(far_at, part), far)
    )


def step_kernel(
    step, index_ref, quarter_ref, text_ref, image_ref, near_up, middle_up, near_down, middle_down, far_ref,
    text_in, image_in, text_out, image_out
):
    part = middle_up.shape[0] // 2
    up = (near_up[:part], middle_up[...], far_ref[:part])
    down = (near_down[:part], middle_down[...], far_ref[part:])
    first, second = index_ref[2 * step - 1], index_ref[2 * step]
    for ref, given, out in ((text_ref, text_in, text_out), (image_ref, image_in, image_out)):
        out[...] = (
            given[...]
            + product(ref, first, quarter_ref, up)
            + product(ref, second, quarter_ref, down)
        )


def first_kernel(index_ref, text_ref, image_ref, weight_ref, text_out, image_out):
    weight = weight_ref[...]
    block = index_ref[0]
    text_out[...] = jnp.dot(text_ref[block], weight, preferred_element_type=jnp.float32)
    image_out[...] = jnp.dot(image_ref[block], weight, preferred_element_type=jnp.float32)


def last_kernel(
    step, index_ref, quarter_ref, text_ref, image_ref, near_ref, middle_ref, far_ref, text_in, image_in, bias_ref,
    slot_ref, partial_ref, text_out, send_out
):
    sections, cape, _ = send_out.shape
    width = image_in.shape[1]
    block = index_ref[step]
    weights = (near_ref[: middle_ref.shape[0] // 2], middle_ref[...], far_ref[...])
    image = image_in[...] + product(image_ref, block, quarter_ref, weights) + bias_ref[...]
    place = (iota((sections * cape, image.shape[0]), 0) == slot_ref[...]).astype(jnp.bfloat16)
    send = jnp.dot(place, image.astype(jnp.bfloat16), preferred_element_type=jnp.float32)
    send_out[:, :, :width] = send.astype(jnp.bfloat16).reshape(sections, cape, width)
    send_out[:, :, width:] = partial_ref[...]
    text = text_in[...] + product(text_ref, block, quarter_ref, weights) + bias_ref[...]
    text_out[...] = text.astype(jnp.bfloat16)


def finish_kernel(text_ref, image_ref, bias_ref, slot_ref, text_out, send_out):
    text_out[...] = (text_ref[...] + bias_ref[...]).astype(jnp.bfloat16)
    image = (image_ref[...] + bias_ref[...]).astype(jnp.bfloat16)
    place = (iota((send_out.shape[0], image.shape[0]), 0) == slot_ref[...]).astype(jnp.bfloat16)
    send_out[...] = jnp.dot(place, image, preferred_element_type=jnp.float32).astype(jnp.bfloat16)


def place_kernel(text_ref, arrived_ref, position_ref, slot_ref, count_ref, rows_ref, blocks_ref):
    rows = text_ref.shape[0]
    sections, cape, _ = arrived_ref.shape
    width = text_ref.shape[1]
    row = iota((rows, sections * cape), 0)
    match = (row == position_ref[...]) & (row < count_ref[0])
    filled = jnp.max(match.astype(jnp.float32), axis=1, keepdims=True) > 0.0
    arrived = arrived_ref[:, :, :width].astype(jnp.float32).reshape(sections * cape, width)
    placed = jnp.dot(
        match.astype(jnp.bfloat16), arrived.astype(jnp.bfloat16), preferred_element_type=jnp.float32
    )
    whole = jnp.where(filled, placed, text_ref[...].astype(jnp.float32)).astype(jnp.bfloat16)
    rows_ref[...] = whole
    slots = (iota((blocks_ref.shape[0], rows), 0) == slot_ref[...]).astype(jnp.bfloat16)
    blocks_ref[...] = jnp.dot(slots, whole, preferred_element_type=jnp.float32).astype(jnp.bfloat16)


def decode_kernel(packed, rows_ref, query_ref, partial_ref, length_ref, out_ref):
    rows = rows_ref.shape[0]
    heads = query_ref.shape[1] // HD
    mask = iota((GROUP, rows), 1) < length_ref[0]
    if packed:
        partial = partial_ref[:, : 2 * heads, rows_ref.shape[1] :].astype(jnp.float32)
    for h in range(heads // GROUP):
        at = slice(h * GROUP, (h + 1) * GROUP)
        key = rows_ref[:, 2 * h * HD : (2 * h + 1) * HD]
        value = rows_ref[:, (2 * h + 1) * HD : (2 * h + 2) * HD]
        query = query_group(query_ref, h).astype(jnp.bfloat16)
        top, total, acc = attend(query, key, value, mask)
        if packed:
            old_acc = partial[:, at, :]
            state = partial[:, heads + h * GROUP : heads + (h + 1) * GROUP, :]
            old_top = state[:, :, 0:1] + state[:, :, 1:2] + state[:, :, 2:3]
            old_total = state[:, :, 3:4] + state[:, :, 4:5]
        else:
            old_acc = partial_ref[:, at, :HD]
            old_top = partial_ref[:, at, HD : HD + 1]
            old_total = partial_ref[:, at, HD + 1 : HD + 2]
        best = jnp.maximum(top, jnp.max(old_top, axis=0))
        fresh_factor = jnp.exp(top - best)
        old_factor = jnp.exp(old_top - best[None])
        total = total * fresh_factor + jnp.sum(old_total * old_factor, axis=0)
        acc = acc * fresh_factor + jnp.sum(old_acc * old_factor, axis=0)
        result = (acc / total).astype(jnp.bfloat16)
        for j in range(GROUP):
            lane = (h * GROUP + j) * HD
            out_ref[:, lane : lane + HD] = result[j : j + 1]


def beside(x):
    return lax.ppermute(x, "tensor", [(0, 1), (1, 0)])


def exchange(x):
    return lax.all_to_all(x, "section", split_axis=0, concat_axis=0, tiled=True)


def ring_order(sections):
    return list(range(0, sections, 2)) + list(range(1, sections, 2))[::-1]


def ring_tables(sections, tensors):
    order = ring_order(sections)
    table = np.zeros((sections, tensors, 2 * sections), np.int32)
    distances = [0] + [s * d for d in range(1, sections // 2) for s in (1, -1)] + [sections // 2]
    for at, section in enumerate(order):
        for step, distance in enumerate(distances):
            source = order[(at - distance) % sections]
            for t in range(tensors):
                table[section, t, step] = (source - t * (sections // tensors)) % sections
            table[section, :, sections + step] = source
    return table


def after(values, *others):
    held = lax.optimization_barrier((tuple(values), others))
    return held[0]


def ring_path(
    text, image, target, weight, bias, gains, queries, pool, owner, fill, block_owner, half, cape, capr
):
    sections = lax.axis_size("section")
    order = ring_order(sections)
    ahead = [(order[i], order[(i + 1) % sections]) for i in range(sections)]
    back = [(b, a) for a, b in ahead]
    depth, width = weight.shape
    part = depth // 4
    rows = text.shape[0]
    heads = queries.shape[1] // HD
    group = lax.axis_index("groups").astype(jnp.int32)

    def up(x):
        return lax.ppermute(x, "section", ahead)

    def down(x):
        return lax.ppermute(x, "section", back)

    def across(x):
        return lax.ppermute(x, "groups", [(0, 1), (1, 0)])

    table = jnp.asarray(ring_tables(sections, lax.axis_size("tensor")))
    index = lax.dynamic_slice(
        table, (lax.axis_index("section"), lax.axis_index("tensor"), 0), (1, 1, 2 * sections)
    ).reshape(2 * sections)
    quarter = group.reshape(1)
    states = (jax.ShapeDtypeStruct((rows, width), jnp.float32),) * 2
    flops = 4 * rows * depth * width

    def step_product(step, state):
        return call(
            functools.partial(step_kernel, step), states, index, quarter, *normed,
            owns[step][0], middles[step][0], owns[step][1], middles[step][1], fars[step], *state,
            smem=(0, 1), aliases={9: 0, 10: 1}, cost=cost(2 * flops, 0),
        )

    own, middle, image_slot, block_slot = call(
        functools.partial(open_kernel, sections, cape, capr, pool.shape[1]),
        (
            jax.ShapeDtypeStruct((part + GROUP + sections, width), jnp.bfloat16),
            jax.ShapeDtypeStruct((2 * part, width), jnp.bfloat16),
            jax.ShapeDtypeStruct((1, rows), jnp.int32),
            jax.ShapeDtypeStruct((1, block_owner.shape[1] * pool.shape[1]), jnp.int32),
        ),
        quarter, weight, target, block_owner, queries,
        smem=(0,),
    )
    near_own = [up(own), down(own)]
    text_far = beside(text)
    near_middle = [up(middle), down(middle)]
    image_far = beside(image)
    last = sections // 2 - 1
    owns, middles, fars = {}, {}, {}
    told = [own]
    waiting, state = [], None
    for step in range(1, last + 1):
        *near_own, text_far = after((*near_own, text_far), *waiting)
        owns[step] = tuple(near_own)
        told += near_own
        fars[step] = across(jnp.concatenate([x[:part] for x in near_own], 0))
        near_own = [up(near_own[0])] + ([down(near_own[1])] if step < last else [])
        waiting = []
        if step == 1:
            normed_text, token = normalize(sections, half, text, text_far, gains)
            waiting = [token]
        elif step == 2:
            normed_image, token = normalize(sections, half, image, image_far, gains)
            normed = (normed_text, normed_image)
            state = call(
                first_kernel, states, index, *normed, weight, smem=(0,), cost=cost(flops, 0)
            )
            waiting = [token]
        else:
            state = step_product(step - 2, state)
            waiting = [*state]
        *near_middle, image_far = after((*near_middle, image_far), *waiting)
        middles[step] = tuple(near_middle)
        near_middle = ([up(near_middle[0])] if step < last else []) + [down(near_middle[1])]
        waiting = [fars[step]]
    state = step_product(last - 1, state)
    (last_own,) = after(near_own, *waiting, *state)
    last_far = across(last_own[:part])
    state = step_product(last, state)
    partial, position = call(
        functools.partial(ring_pool_kernel, sections, cape),
        (
            jax.ShapeDtypeStruct((sections, 2 * heads, HD), jnp.bfloat16),
            jax.ShapeDtypeStruct((1, sections * cape), jnp.int32),
        ),
        index[sections:], *told, last_own, pool, owner, fill,
        smem=(0,),
    )
    text_rows, send = call(
        functools.partial(last_kernel, sections - 1),
        (
            jax.ShapeDtypeStruct((rows, width), jnp.bfloat16),
            jax.ShapeDtypeStruct((sections, cape, width + HD), jnp.bfloat16),
        ),
        index, quarter, *normed, last_own, near_middle[0], last_far, *state, bias, image_slot, partial,
        smem=(0, 1), cost=cost(flops, 0),
    )
    arrived = exchange(send)
    return text_rows, arrived, position, block_slot, arrived


def gather_path(
    text, image, target, weight, bias, gains, queries, pool, owner, fill, block_owner, half, cape, capr
):
    sections = lax.axis_size("section")
    rows, near = text.shape
    width = weight.shape[1]
    heads = queries.shape[1] // HD
    image_slot, block_slot, message = call(
        functools.partial(prep_kernel, sections, cape, capr, pool.shape[1]),
        (
            jax.ShapeDtypeStruct((1, rows), jnp.int32),
            jax.ShapeDtypeStruct((1, block_owner.shape[1] * pool.shape[1]), jnp.int32),
            jax.ShapeDtypeStruct((sections, 2 * heads, LANES), jnp.bfloat16),
        ),
        target, block_owner, queries,
    )
    partial, position = call(
        functools.partial(pool_kernel, cape),
        (
            jax.ShapeDtypeStruct((sections, heads, 2 * HD), jnp.float32),
            jax.ShapeDtypeStruct((1, sections * cape), jnp.int32),
        ),
        exchange(message), pool, owner, fill,
    )
    normed = [normalize(2, half, x, beside(x), gains)[0] for x in (text, image)]
    whole = lax.all_gather(weight, "section", axis=0, tiled=True)
    first = lax.dynamic_slice_in_dim(whole, half[0] * near, near, 0)
    second = lax.dynamic_slice_in_dim(whole, (1 - half[0]) * near, near, 0)
    text_sum, image_sum = (
        jnp.dot(n[0], first, preferred_element_type=jnp.float32)
        + jnp.dot(n[1], second, preferred_element_type=jnp.float32)
        for n in normed
    )
    text_rows, send = call(
        finish_kernel,
        (
            jax.ShapeDtypeStruct((rows, width), jnp.bfloat16),
            jax.ShapeDtypeStruct((sections * cape, width), jnp.bfloat16),
        ),
        text_sum, image_sum, bias, image_slot,
    )
    arrived = exchange(send.reshape(sections, cape, width))
    return text_rows, arrived, position, block_slot, exchange(partial)


def shards(
    text_embed,
    image_embed,
    image_count,
    prompt_len,
    embed_target,
    kv_weight,
    kv_bias,
    norm_gain,
    queries,
    old_pool,
    pool_owner,
    pool_fill,
    block_owner,
):
    sections, tensors = lax.axis_size("section"), lax.axis_size("tensor")
    rows = text_embed.shape[0]
    width = kv_weight.shape[1]
    heads = queries.shape[1] // HD
    cape = rows // sections
    block_rows = old_pool.shape[1]
    capr = (block_owner.shape[0] + sections - 1) // sections * block_rows
    ring = (
        sections == 8
        and tensors == 2
        and lax.axis_size("groups") == 2
        and kv_weight.shape[0] % (8 * LANES) == 0
        and cape == 2 * heads
    )
    text_rows, arrived, position, block_slot, partial = (ring_path if ring else gather_path)(
        text_embed,
        image_embed,
        embed_target.reshape(1, -1),
        kv_weight,
        kv_bias.reshape(1, -1),
        norm_gain.reshape(1, -1),
        queries,
        old_pool,
        pool_owner.reshape(1, -1),
        pool_fill.reshape(1, -1),
        block_owner.reshape(1, -1),
        lax.axis_index("tensor").astype(jnp.int32).reshape(1),
        cape,
        capr,
    )
    whole_rows, block_data = call(
        place_kernel,
        (
            jax.ShapeDtypeStruct((rows, width), jnp.bfloat16),
            jax.ShapeDtypeStruct((sections * capr, width), jnp.bfloat16),
        ),
        text_rows,
        arrived,
        position,
        block_slot,
        image_count,
        smem=(4,),
    )
    fresh = exchange(block_data.reshape(sections, capr, width)).reshape(sections * capr, width)
    decoded = call(
        functools.partial(decode_kernel, ring),
        jax.ShapeDtypeStruct((1, heads * HD), jnp.bfloat16),
        whole_rows,
        queries,
        partial,
        prompt_len,
        smem=(3,),
    )
    return decoded, fresh


def solution(mesh):
    return jax.shard_map(
        shards,
        mesh=mesh,
        in_specs=(
            P(("groups", "section"), "tensor"),
            P(("groups", "section"), "tensor"),
            P(("groups", "section")),
            P(("groups", "section")),
            P(("groups", "section")),
            P("section", "tensor"),
            P("tensor"),
            P(),
            P(("groups", "section"), "tensor"),
            P(("groups", "section"), None, "tensor"),
            P(("groups", "section")),
            P(("groups", "section")),
            P(("groups", "section")),
        ),
        out_specs=(P(("groups", "section"), "tensor"), P(("groups", "section"), "tensor")),
        check_vma=False,
    )
```

```python
import functools

import jax
import jax.numpy as jnp
import numpy as np
from jax import lax
from jax.experimental import pallas as pl
from jax.experimental.pallas import tpu as pltpu
from jax.sharding import PartitionSpec as P

HQ = 32
KVH = 4
HD = 128
GROUP = HQ // KVH
SCALE = HD ** (-0.5)
LANES = 128
NEG = -1e30
VMEM = 14 * 1024 * 1024
VMEM_ALL = 56 * 1024 * 1024


def iota(shape, dim):
    return lax.broadcasted_iota(jnp.int32, shape, dim)


def call(kernel, outs, *args, cost=None, smem=(), aliases=None, scratch=()):
    return pl.pallas_call(
        kernel,
        out_shape=outs,
        in_specs=[
            pl.BlockSpec(memory_space=pltpu.SMEM if i in smem else pltpu.VMEM)
            for i in range(len(args))
        ],
        out_specs=jax.tree.map(lambda _: pl.BlockSpec(memory_space=pltpu.VMEM), outs),
        input_output_aliases=aliases or {},
        scratch_shapes=scratch,
        compiler_params=pltpu.CompilerParams(vmem_limit_bytes=VMEM),
        cost_estimate=cost,
    )(*args)


def cost(flops, nbytes):
    return pl.CostEstimate(flops=int(flops), bytes_accessed=int(nbytes), transcendentals=0)


def rank_before(hits):
    items = hits.shape[1]
    earlier = (iota((items, items), 0) < iota((items, items), 1)).astype(jnp.bfloat16)
    before = jnp.dot(hits.astype(jnp.bfloat16), earlier, preferred_element_type=jnp.float32)
    return jnp.sum(before * hits, axis=0, keepdims=True).astype(jnp.int32)


def spread(values, items):
    groups = values.shape[1]
    share = items // groups
    same = iota((groups, items), 0) * share
    column = iota((groups, items), 1)
    same = ((column >= same) & (column < same + share)).astype(jnp.bfloat16)
    wide = jnp.broadcast_to(values.astype(jnp.float32), (8, groups)).astype(jnp.bfloat16)
    wide = jnp.dot(wide, same, preferred_element_type=jnp.float32)
    return wide[:1].astype(jnp.int32)


def image_slots(target, sections, cape):
    rows = target.shape[1]
    index = jnp.floor((target.astype(jnp.float32) + 0.5) * (1.0 / rows)).astype(jnp.int32)
    place = target - index * rows
    hits = ((index == iota((sections, rows), 0)) & (target >= 0)).astype(jnp.float32)
    rank = rank_before(hits)
    at_rank = (rank == iota((LANES, rows), 0)).astype(jnp.bfloat16)
    numbered = (hits * (place + 1).astype(jnp.float32)).astype(jnp.bfloat16)
    positions = lax.dot_general(
        numbered, at_rank, (((1,), (1,)), ((), ())), preferred_element_type=jnp.float32
    )
    return jnp.where(target >= 0, index * cape + rank, -1), positions - 1.0


def block_slots(owner, sections, capr, block_rows):
    owner = spread(owner, owner.shape[1] * block_rows)
    hits = ((owner == iota((sections, owner.shape[1]), 0)) & (owner >= 0)).astype(jnp.float32)
    return jnp.where(owner >= 0, owner * capr + rank_before(hits), -1)


def query_group(query_ref, h):
    heads = [
        query_ref[:, j * HD : (j + 1) * HD].astype(jnp.float32)
        for j in range(h * GROUP, (h + 1) * GROUP)
    ]
    return jnp.concatenate(heads, axis=0)


def prep_kernel(
    sections, cape, capr, block_rows, target_ref, owner_ref, query_ref, out_slot, out_block, out_message
):
    out_slot[...], positions = image_slots(target_ref[...], sections, cape)
    heads = query_ref.shape[1] // HD
    query = jnp.concatenate([query_group(query_ref, h) for h in range(heads // GROUP)], axis=0)
    query = query.astype(jnp.bfloat16)
    out_message[:, :heads, :] = jnp.broadcast_to(query[None], (sections,) + query.shape)
    out_message[:, heads:, :] = jnp.broadcast_to(
        positions.astype(jnp.bfloat16)[:, None, :], (sections, out_message.shape[1] - heads, LANES)
    )
    out_block[...] = block_slots(owner_ref[...], sections, capr, block_rows)


def open_kernel(
    sections, cape, capr, block_rows, group_ref, base_ref, half_ref, weight_hbm, target_hbm, owner_hbm, query_hbm,
    out_own, out_middle, out_slot, out_block, target_ref, owner_ref, query_ref, sems
):
    depth, middle = weight_hbm.shape[0], out_middle.shape[0]
    part = (depth - middle) // 2
    turned = pl.multiple_of(group_ref[0] * (depth - part), 16)
    copies = [
        pltpu.make_async_copy(source, target, sems.at[k])
        for k, (source, target) in enumerate(
            (
                (target_hbm, target_ref),
                (query_hbm, query_ref),
                (owner_hbm, owner_ref),
                (weight_hbm.at[pl.ds(turned, part)], out_own.at[pl.ds(0, part)]),
                (weight_hbm.at[pl.ds(part, middle)], out_middle),
            )
        )
    ]
    for copy in copies:
        copy.start()
    copies[0].wait()
    out_slot[...], positions = image_slots(target_ref[...], sections, cape)
    copies[1].wait()
    groups = query_ref.shape[1] // (GROUP * HD)
    told = [query_group(query_ref, h) for h in range(groups)]
    told.append(jnp.zeros((GROUP, out_own.shape[1] - groups * HD), jnp.float32))
    told = jnp.concatenate(told, axis=1)
    positions = jnp.concatenate(
        [positions, jnp.zeros((sections, out_own.shape[1] - LANES), jnp.float32)], axis=1
    )
    out_own[part:] = jnp.concatenate([told, positions], axis=0).astype(jnp.bfloat16)
    copies[2].wait()
    out_block[...] = block_slots(owner_ref[...], sections, capr, block_rows)
    copies[3].wait()
    copies[4].wait()


NORM_TILE = 64


def norm_kernel(blocks, half_ref, near_hbm, far_hbm, gains_hbm, out_ref, done_ref, near, far, gain, sems):
    tiles, tile, features = near.shape
    width = out_ref.shape[2]
    half = half_ref[0]
    copies = []
    for side in range(2):
        at = pl.multiple_of((half if side == 0 else 1 - half) * features, features)
        copies.append(
            pltpu.make_async_copy(gains_hbm.at[:, pl.ds(at, features)], gain.at[side], sems.at[side])
        )
    for i in range(tiles):
        at = pl.ds(i * tile, tile)
        for side, (hbm, vmem) in enumerate(((near_hbm, near), (far_hbm, far))):
            copies.append(
                pltpu.make_async_copy(hbm.at[at], vmem.at[i], sems.at[2 + 2 * i + side])
            )
    for copy in copies:
        copy.start()
    done_ref[...] = jnp.zeros_like(done_ref)
    copies[0].wait()
    copies[1].wait()
    for i in range(tiles):
        copies[2 + 2 * i].wait()
        copies[3 + 2 * i].wait()
        total = 0.0
        for ref in (near, far):
            value = ref[i].astype(jnp.float32)
            total = total + jnp.sum(value * value, axis=1, keepdims=True)
        factor = lax.rsqrt(total * (1.0 / (2 * features)) + 1e-06)
        for side, ref in enumerate((near, far)):
            for j in range(blocks // 2):
                at = pl.ds(j * width, width)
                block = ref[i, :, at].astype(jnp.float32) * factor * gain[side, :, at]
                out_ref[side * (blocks // 2) + j, pl.ds(i * tile, tile)] = block.astype(jnp.bfloat16)


def normalize(blocks, half, near, far, gains):
    rows, features = near.shape
    tile = min(NORM_TILE, rows)
    held = pltpu.VMEM((rows // tile, tile, features), jnp.bfloat16)
    return pl.pallas_call(
        functools.partial(norm_kernel, blocks),
        out_shape=(
            jax.ShapeDtypeStruct((blocks, rows, 2 * features // blocks), jnp.bfloat16),
            jax.ShapeDtypeStruct((8, LANES), jnp.float32),
        ),
        in_specs=[pl.BlockSpec(memory_space=pltpu.SMEM)]
        + [pl.BlockSpec(memory_space=pltpu.HBM)] * 3,
        out_specs=[pl.BlockSpec(memory_space=pltpu.VMEM)] * 2,
        scratch_shapes=[
            held,
            held,
            pltpu.VMEM((2, 1, features), jnp.float32),
            pltpu.SemaphoreType.DMA((2 + 2 * (rows // tile),)),
        ],
        compiler_params=pltpu.CompilerParams(vmem_limit_bytes=VMEM),
        cost_estimate=cost(1, 1),
    )(half, near, far, gains)


def pool_rows(pool_ref):
    block_rows = pool_ref.shape[1]
    pool = pool_ref[...].astype(jnp.float32)
    return jnp.concatenate([pool[:, i, :] for i in range(block_rows)], axis=0).astype(jnp.bfloat16)


def positions_in_slots(sent, source, cape):
    sources = sent.shape[0]
    slots = sources * cape
    column = iota((sources, slots), 1)
    rank = column - jnp.floor((column.astype(jnp.float32) + 0.5) * (1.0 / cape)).astype(jnp.int32) * cape
    at_source = (column >= source * cape) & (column < source * cape + cape)
    at_rank = (iota((LANES, slots), 0) == rank[:1]).astype(jnp.bfloat16)
    wide = jnp.dot(sent.astype(jnp.bfloat16), at_rank, preferred_element_type=jnp.float32)
    return jnp.sum(jnp.where(at_source, wide, 0.0), axis=0, keepdims=True).astype(jnp.int32)


def pool_kernel(cape, message_ref, pool_ref, owner_ref, fill_ref, out_ref, position_ref):
    sections, heads = out_ref.shape[0], out_ref.shape[1]
    held, block_rows, _ = pool_ref.shape
    request = iota((sections * GROUP, held), 0)
    owner = owner_ref[...]
    owned = (request >= owner * GROUP) & (request < owner * GROUP + GROUP)
    mask = jnp.concatenate(
        [(owned & (fill_ref[...] > i)).astype(jnp.float32) for i in range(block_rows)], axis=1
    )
    pool = pool_rows(pool_ref)
    for h in range(heads // GROUP):
        query = message_ref[:, h * GROUP : (h + 1) * GROUP, :].astype(jnp.float32)
        query = query.reshape(sections * GROUP, HD).astype(jnp.bfloat16)
        key = pool[:, 2 * h * HD : (2 * h + 1) * HD]
        value = pool[:, (2 * h + 1) * HD : (2 * h + 2) * HD]
        top, total, acc = attend(query, key, value, mask > 0.0)
        lane = iota((sections * GROUP, LANES), 1)
        state = jnp.where(lane == 0, top, jnp.where(lane == 1, total, 0.0))
        out_ref[:, h * GROUP : (h + 1) * GROUP, :HD] = acc.reshape(sections, GROUP, HD)
        out_ref[:, h * GROUP : (h + 1) * GROUP, HD:] = state.reshape(sections, GROUP, LANES)
    sent = message_ref[:, heads : heads + 1, :].astype(jnp.float32).reshape(sections, LANES)
    position_ref[...] = positions_in_slots(sent, iota((sections, 1), 0), cape)


def ring_pool_kernel(sections, cape, index_ref, base_ref, *refs):
    told_refs = refs[:sections]
    pool_ref, owner_ref, fill_ref = refs[sections : sections + 3]
    out_ref, position_ref = refs[-2:]
    sources = [index_ref[base_ref[0] + sections + j] for j in range(sections)]
    held, block_rows, _ = pool_ref.shape
    heads = out_ref.shape[1] // 2
    groups = heads // GROUP
    part = told_refs[0].shape[0] - GROUP - sections
    told = [ref[part:, :].astype(jnp.float32) for ref in told_refs]
    owner, fill = owner_ref[...], fill_ref[...]
    masks = []
    for j in range(sections):
        owned = owner == sources[j]
        mask = [(owned & (fill > i)).astype(jnp.float32) for i in range(block_rows)]
        masks.append(jnp.broadcast_to(jnp.concatenate(mask, axis=1), (GROUP, held * block_rows)))
    mask = jnp.concatenate(masks, axis=0) > 0.0
    pool = pool_rows(pool_ref)
    sums, states = [], []
    lane = iota((sections * GROUP, LANES), 1)
    for h in range(groups):
        query = jnp.concatenate([t[:GROUP, h * HD : (h + 1) * HD] for t in told], axis=0)
        key = pool[:, 2 * h * HD : (2 * h + 1) * HD]
        value = pool[:, (2 * h + 1) * HD : (2 * h + 2) * HD]
        top, total, acc = attend(query.astype(jnp.bfloat16), key, value, mask)
        terms = bf16_terms(top, 3) + bf16_terms(total, 2)
        state = jnp.zeros((sections * GROUP, LANES), jnp.float32)
        for k, term in enumerate(terms):
            state = jnp.where(lane == k, term, state)
        sums.append(acc)
        states.append(state)
    for j in range(sections):
        at = slice(j * GROUP, (j + 1) * GROUP)
        rows = jnp.concatenate([x[at] for x in sums] + [x[at] for x in states], axis=0)
        out_ref[sources[j]] = rows.astype(jnp.bfloat16)
    own = iota((sections, LANES), 0) == sources[0]
    sent = jnp.concatenate(
        [
            jnp.sum(jnp.where(own, t[GROUP:, :LANES], 0.0), axis=0, keepdims=True) for t in told
        ],
        axis=0,
    )
    source = jnp.zeros((sections, 1), jnp.int32)
    for j in range(sections):
        source = jnp.where(iota((sections, 1), 0) == j, sources[j], source)
    position_ref[...] = positions_in_slots(sent, source, cape)


def bf16_terms(value, count):
    terms = []
    for _ in range(count):
        term = value.astype(jnp.bfloat16).astype(jnp.float32)
        terms.append(term)
        value = value - term
    return terms


def attend(query, key, value, mask):
    scores = (
        lax.dot_general(query, key, (((1,), (1,)), ((), ())), preferred_element_type=jnp.float32)
        * SCALE
    )
    scores = jnp.where(mask, scores, NEG)
    top = jnp.max(scores, axis=1, keepdims=True)
    expo = jnp.where(mask, jnp.exp(scores - top), 0.0)
    total = jnp.sum(expo, axis=1, keepdims=True)
    acc = jnp.dot(expo.astype(jnp.bfloat16), value, preferred_element_type=jnp.float32)
    return top, total, acc


def fill_slice(whole_ref, group, near, middles, far):
    part, depth = far.shape[0], whole_ref.shape[0]
    own_at = pl.multiple_of(group * (depth - part), 16)
    far_at = pl.multiple_of((1 - group) * (depth - part), 16)
    whole_ref[pl.ds(own_at, part)] = near[:part]
    whole_ref[pl.ds(far_at, part)] = far
    at = part
    for middle in middles:
        whole_ref[at : at + middle.shape[0]] = middle
        at += middle.shape[0]


def times(rows_ref, block, weight_ref):
    return jnp.dot(rows_ref[block], weight_ref[...], preferred_element_type=jnp.float32)


def step_kernel(
    step, index_ref, base_ref, group_ref, text_ref, image_ref, near_up, middle_up, near_down, middle_down, far_ref,
    text_in, image_in, text_out, image_out, first_ref, second_ref
):
    part = far_ref.shape[0] // 2
    fill_slice(first_ref, group_ref[0], near_up[...], [middle_up[...]], far_ref[:part])
    fill_slice(second_ref, group_ref[0], near_down[...], [middle_down[...]], far_ref[part:])
    first, second = (index_ref[base_ref[0] + k] for k in (2 * step - 1, 2 * step))
    for ref, given, out in ((text_ref, text_in, text_out), (image_ref, image_in, image_out)):
        out[...] = given[...] + times(ref, first, first_ref) + times(ref, second, second_ref)


def first_kernel(index_ref, base_ref, text_ref, image_ref, weight_ref, text_out, image_out):
    block = index_ref[base_ref[0]]
    text_out[...] = times(text_ref, block, weight_ref)
    image_out[...] = times(image_ref, block, weight_ref)


def last_image_kernel(
    step, index_ref, base_ref, group_ref, image_ref, near_ref, middle_ref, far_ref, image_in, bias_ref,
    slot_ref, partial_ref, send_out, whole_ref
):
    sections, cape, _ = send_out.shape
    width = image_in.shape[1]
    fill_slice(whole_ref, group_ref[0], near_ref[...], [middle_ref[...]], far_ref[...])
    image = times(image_ref, index_ref[base_ref[0] + step], whole_ref)
    image = image_in[...] + image + bias_ref[...]
    place = (iota((sections * cape, image.shape[0]), 0) == slot_ref[...]).astype(jnp.bfloat16)
    send = jnp.dot(place, image.astype(jnp.bfloat16), preferred_element_type=jnp.float32)
    send_out[:, :, :width] = send.astype(jnp.bfloat16).reshape(sections, cape, width)
    send_out[:, :, width:] = partial_ref[...]


def last_text_kernel(
    step, index_ref, base_ref, text_ref, whole_ref, text_in, bias_ref, text_out
):
    text = times(text_ref, index_ref[base_ref[0] + step], whole_ref)
    text_out[...] = (text_in[...] + text + bias_ref[...]).astype(jnp.bfloat16)


def finish_kernel(text_ref, image_ref, bias_ref, slot_ref, text_out, send_out):
    text_out[...] = (text_ref[...] + bias_ref[...]).astype(jnp.bfloat16)
    image = (image_ref[...] + bias_ref[...]).astype(jnp.bfloat16)
    place = (iota((send_out.shape[0], image.shape[0]), 0) == slot_ref[...]).astype(jnp.bfloat16)
    send_out[...] = jnp.dot(place, image, preferred_element_type=jnp.float32).astype(jnp.bfloat16)


def place_kernel(text_ref, arrived_ref, position_ref, slot_ref, count_ref, rows_ref, blocks_ref):
    rows, width = text_ref.shape
    sections, cape, _ = arrived_ref.shape
    row = iota((rows, sections * cape), 0)
    match = (row == position_ref[...]) & (row < count_ref[0])
    filled = jnp.max(match.astype(jnp.float32), axis=1, keepdims=True) > 0.0
    arrived = arrived_ref[:, :, :width].reshape(sections * cape, width)
    placed = jnp.dot(match.astype(jnp.bfloat16), arrived, preferred_element_type=jnp.float32)
    whole = jnp.where(filled, placed, text_ref[...].astype(jnp.float32)).astype(jnp.bfloat16)
    slots = (iota((blocks_ref.shape[0], rows), 0) == slot_ref[...]).astype(jnp.bfloat16)
    blocks_ref[...] = jnp.dot(slots, whole, preferred_element_type=jnp.float32).astype(jnp.bfloat16)
    rows_ref[...] = whole


def decode_kernel(packed, rows_ref, query_ref, partial_ref, length_ref, out_ref):
    rows = rows_ref.shape[0]
    heads = query_ref.shape[1] // HD
    mask = iota((GROUP, rows), 1) < length_ref[0]
    if packed:
        partial = partial_ref[:, : 2 * heads, rows_ref.shape[1] :].astype(jnp.float32)
    for h in range(heads // GROUP):
        at = slice(h * GROUP, (h + 1) * GROUP)
        key = rows_ref[:, 2 * h * HD : (2 * h + 1) * HD]
        value = rows_ref[:, (2 * h + 1) * HD : (2 * h + 2) * HD]
        query = query_group(query_ref, h).astype(jnp.bfloat16)
        top, total, acc = attend(query, key, value, mask)
        if packed:
            old_acc = partial[:, at, :]
            state = partial[:, heads + h * GROUP : heads + (h + 1) * GROUP, :]
            old_top = state[:, :, 0:1] + state[:, :, 1:2] + state[:, :, 2:3]
            old_total = state[:, :, 3:4] + state[:, :, 4:5]
        else:
            old_acc = partial_ref[:, at, :HD]
            old_top = partial_ref[:, at, HD : HD + 1]
            old_total = partial_ref[:, at, HD + 1 : HD + 2]
        best = jnp.maximum(top, jnp.max(old_top, axis=0))
        fresh_factor = jnp.exp(top - best)
        old_factor = jnp.exp(old_top - best[None])
        total = total * fresh_factor + jnp.sum(old_total * old_factor, axis=0)
        acc = acc * fresh_factor + jnp.sum(old_acc * old_factor, axis=0)
        result = (acc / total).astype(jnp.bfloat16)
        for j in range(GROUP):
            lane = (h * GROUP + j) * HD
            out_ref[:, lane : lane + HD] = result[j : j + 1]


def beside(x):
    return lax.ppermute(x, "tensor", [(0, 1), (1, 0)])


def exchange(x):
    return lax.all_to_all(x, "section", split_axis=0, concat_axis=0, tiled=True)


def ring_order(sections):
    return list(range(0, sections, 2)) + list(range(1, sections, 2))[::-1]


def ring_tables(sections, tensors):
    order = ring_order(sections)
    table = np.zeros((sections, tensors, 2 * sections), np.int32)
    distances = [0] + [s * d for d in range(1, sections // 2) for s in (1, -1)] + [sections // 2]
    for at, section in enumerate(order):
        for step, distance in enumerate(distances):
            source = order[(at - distance) % sections]
            for t in range(tensors):
                table[section, t, step] = (source - t * (sections // tensors)) % sections
            table[section, :, sections + step] = source
    return table


def after(values, others):
    return lax.optimization_barrier((tuple(values), tuple(others)))


def ring_path(
    text, image, target, weight, bias, gains, queries, pool, owner, fill, block_owner, half, cape, capr
):
    sections = lax.axis_size("section")
    order = ring_order(sections)
    ahead = [(order[i], order[(i + 1) % sections]) for i in range(sections)]
    back = [(b, a) for a, b in ahead]
    depth, width = weight.shape
    part = depth // 4
    rows = text.shape[0]
    heads = queries.shape[1] // HD
    group = lax.axis_index("groups").astype(jnp.int32)
    whole_slice = pltpu.VMEM((depth, width), jnp.bfloat16)

    def up(x):
        return lax.ppermute(x, "section", ahead)

    def down(x):
        return lax.ppermute(x, "section", back)

    def across(x):
        return lax.ppermute(x, "groups", [(0, 1), (1, 0)])

    tensors = lax.axis_size("tensor")
    index = jnp.asarray(ring_tables(sections, tensors).reshape(-1))
    base = (lax.axis_index("section") * tensors + lax.axis_index("tensor")) * (2 * sections)
    group, base = group.reshape(1), base.astype(jnp.int32).reshape(1)
    states = (jax.ShapeDtypeStruct((rows, width), jnp.float32),) * 2
    flops = 4 * rows * depth * width

    def step_product(step, state):
        return call(
            functools.partial(step_kernel, step), states, index, base, group, *normed,
            owns[step][0], middles[step][0], owns[step][1], middles[step][1], fars[step], *state,
            smem=(0, 1, 2), aliases={10: 0, 11: 1}, cost=cost(1, 1),
            scratch=[whole_slice] * 2,
        )

    spaces = [pltpu.SMEM] * 3 + [pltpu.HBM] * 4
    own, middle, image_slot, block_slot = pl.pallas_call(
        functools.partial(open_kernel, sections, cape, capr, pool.shape[1]),
        out_shape=(
            jax.ShapeDtypeStruct((part + GROUP + sections, width), jnp.bfloat16),
            jax.ShapeDtypeStruct((depth - 2 * part, width), jnp.bfloat16),
            jax.ShapeDtypeStruct((1, rows), jnp.int32),
            jax.ShapeDtypeStruct((1, block_owner.shape[1] * pool.shape[1]), jnp.int32),
        ),
        in_specs=[pl.BlockSpec(memory_space=space) for space in spaces],
        out_specs=[pl.BlockSpec(memory_space=pltpu.VMEM)] * 4,
        scratch_shapes=[
            pltpu.VMEM(target.shape, jnp.int32),
            pltpu.VMEM(block_owner.shape, jnp.int32),
            pltpu.VMEM(queries.shape, jnp.bfloat16),
            pltpu.SemaphoreType.DMA((5,)),
        ],
        compiler_params=pltpu.CompilerParams(vmem_limit_bytes=VMEM_ALL),
    )(group, base, half, weight, target, block_owner, queries)
    near_own = [up(own), down(own)]
    text_far, image_far = beside(text), beside(image)
    (middle,), (text_far, image_far) = after((middle,), (text_far, image_far))
    near_middle = [up(middle), down(middle)]
    last = sections // 2 - 1
    owns, middles, fars = {}, {}, {}
    told = [own]
    normed_text, token = normalize(sections, half, text, text_far, gains)
    waiting = [token]
    for step in range(1, last + 1):
        near_own, waiting = after(near_own, waiting)
        owns[step] = near_own
        told += near_own
        if step > 1:
            fars[step - 1] = waiting[0]
            waiting = waiting[1:]
        fars[step] = across(jnp.concatenate([x[:part] for x in near_own], 0))
        near_own = [up(near_own[0])] + ([down(near_own[1])] if step < last else [])
        near_middle, waiting = after(near_middle, [*waiting, image_far])
        *waiting, image_far = waiting
        middles[step] = near_middle
        near_middle = ([up(near_middle[0])] if step < last else []) + [down(near_middle[1])]
        if step == 1:
            normed_image, token = normalize(sections, half, image, image_far, gains)
            normed = (normed_text, normed_image)
            state = call(
                first_kernel, states, index, base, *normed, weight, smem=(0, 1), cost=cost(1, 1)
            )
            waiting = [*waiting, token, *state]
        else:
            waiting = [*waiting[:-2], *step_product(step - 1, waiting[-2:])]
        waiting = [fars[step], *waiting]
    (last_own,), waiting = after(near_own, waiting)
    fars[last] = waiting[0]
    last_far = across(last_own[:part])
    state = step_product(last, waiting[-2:])
    partial, position = call(
        functools.partial(ring_pool_kernel, sections, cape),
        (
            jax.ShapeDtypeStruct((sections, 2 * heads, HD), jnp.bfloat16),
            jax.ShapeDtypeStruct((1, sections * cape), jnp.int32),
        ),
        index, base, *told, last_own, pool, owner, fill, *waiting[1:-2],
        smem=(0, 1),
    )
    send, whole = call(
        functools.partial(last_image_kernel, sections - 1),
        (
            jax.ShapeDtypeStruct((sections, cape, width + HD), jnp.bfloat16),
            jax.ShapeDtypeStruct((depth, width), jnp.bfloat16),
        ),
        index, base, group, normed[1], last_own, *near_middle, last_far, state[1], bias, image_slot, partial,
        smem=(0, 1, 2), cost=cost(1, 1),
    )
    arrived = exchange(send)
    text_rows = call(
        functools.partial(last_text_kernel, sections - 1),
        jax.ShapeDtypeStruct((rows, width), jnp.bfloat16),
        index, base, normed[0], whole, state[0], bias,
        smem=(0, 1), cost=cost(1, 1),
    )
    return text_rows, arrived, position, block_slot, arrived


def gather_path(
    text, image, target, weight, bias, gains, queries, pool, owner, fill, block_owner, half, cape, capr
):
    sections = lax.axis_size("section")
    rows, near = text.shape
    width = weight.shape[1]
    heads = queries.shape[1] // HD
    image_slot, block_slot, message = call(
        functools.partial(prep_kernel, sections, cape, capr, pool.shape[1]),
        (
            jax.ShapeDtypeStruct((1, rows), jnp.int32),
            jax.ShapeDtypeStruct((1, block_owner.shape[1] * pool.shape[1]), jnp.int32),
            jax.ShapeDtypeStruct((sections, 2 * heads, LANES), jnp.bfloat16),
        ),
        target, block_owner, queries,
    )
    partial, position = call(
        functools.partial(pool_kernel, cape),
        (
            jax.ShapeDtypeStruct((sections, heads, 2 * HD), jnp.float32),
            jax.ShapeDtypeStruct((1, sections * cape), jnp.int32),
        ),
        exchange(message), pool, owner, fill,
    )
    normed = [normalize(2, half, x, beside(x), gains)[0] for x in (text, image)]
    whole = lax.all_gather(weight, "section", axis=0, tiled=True)
    first = lax.dynamic_slice_in_dim(whole, half[0] * near, near, 0)
    second = lax.dynamic_slice_in_dim(whole, (1 - half[0]) * near, near, 0)
    text_sum, image_sum = (
        jnp.dot(n[0], first, preferred_element_type=jnp.float32)
        + jnp.dot(n[1], second, preferred_element_type=jnp.float32)
        for n in normed
    )
    text_rows, send = call(
        finish_kernel,
        (
            jax.ShapeDtypeStruct((rows, width), jnp.bfloat16),
            jax.ShapeDtypeStruct((sections * cape, width), jnp.bfloat16),
        ),
        text_sum, image_sum, bias, image_slot,
    )
    arrived = exchange(send.reshape(sections, cape, width))
    return text_rows, arrived, position, block_slot, exchange(partial)


def shards(
    text_embed,
    image_embed,
    image_count,
    prompt_len,
    embed_target,
    kv_weight,
    kv_bias,
    norm_gain,
    queries,
    old_pool,
    pool_owner,
    pool_fill,
    block_owner,
):
    sections, tensors = lax.axis_size("section"), lax.axis_size("tensor")
    rows = text_embed.shape[0]
    width = kv_weight.shape[1]
    heads = queries.shape[1] // HD
    cape = rows // sections
    block_rows = old_pool.shape[1]
    capr = (block_owner.shape[0] + sections - 1) // sections * block_rows
    ring = (
        sections == 8
        and tensors == 2
        and lax.axis_size("groups") == 2
        and kv_weight.shape[0] % 1024 == 0
        and cape == 2 * heads
    )
    text_rows, arrived, position, block_slot, partial = (ring_path if ring else gather_path)(
        text_embed,
        image_embed,
        embed_target.reshape(1, -1),
        kv_weight,
        kv_bias.reshape(1, -1),
        norm_gain.reshape(1, -1),
        queries,
        old_pool,
        pool_owner.reshape(1, -1),
        pool_fill.reshape(1, -1),
        block_owner.reshape(1, -1),
        lax.axis_index("tensor").astype(jnp.int32).reshape(1),
        cape,
        capr,
    )
    whole_rows, block_data = call(
        place_kernel,
        (
            jax.ShapeDtypeStruct((rows, width), jnp.bfloat16),
            jax.ShapeDtypeStruct((sections * capr, width), jnp.bfloat16),
        ),
        text_rows,
        arrived,
        position,
        block_slot,
        image_count,
        smem=(4,),
    )
    fresh = exchange(block_data.reshape(sections, capr, width)).reshape(sections * capr, width)
    decoded = call(
        functools.partial(decode_kernel, ring),
        jax.ShapeDtypeStruct((1, heads * HD), jnp.bfloat16),
        whole_rows,
        queries,
        partial,
        prompt_len,
        smem=(3,),
    )
    return decoded, fresh


def solution(mesh):
    return jax.shard_map(
        shards,
        mesh=mesh,
        in_specs=(
            P(("groups", "section"), "tensor"),
            P(("groups", "section"), "tensor"),
            P(("groups", "section")),
            P(("groups", "section")),
            P(("groups", "section")),
            P("section", "tensor"),
            P("tensor"),
            P(),
            P(("groups", "section"), "tensor"),
            P(("groups", "section"), None, "tensor"),
            P(("groups", "section")),
            P(("groups", "section")),
            P(("groups", "section")),
        ),
        out_specs=(P(("groups", "section"), "tensor"), P(("groups", "section"), "tensor")),
        check_vma=False,
    )
```

```python
import functools

import jax
import jax.numpy as jnp
import numpy as np
from jax import lax
from jax.experimental import pallas as pl
from jax.experimental.pallas import tpu as pltpu
from jax.sharding import PartitionSpec as P

HQ = 32
KVH = 4
HD = 128
GROUP = HQ // KVH
SCALE = HD ** (-0.5)
LANES = 128
NEG = -1e30
LEAST_IMAGE = 4
VMEM = 14 * 1024 * 1024
VMEM_ALL = 56 * 1024 * 1024


def iota(shape, dim):
    return lax.broadcasted_iota(jnp.int32, shape, dim)


def call(kernel, outs, *args, cost=None, smem=(), aliases=None, scratch=()):
    return pl.pallas_call(
        kernel,
        out_shape=outs,
        in_specs=[
            pl.BlockSpec(memory_space=pltpu.SMEM if i in smem else pltpu.VMEM)
            for i in range(len(args))
        ],
        out_specs=jax.tree.map(lambda _: pl.BlockSpec(memory_space=pltpu.VMEM), outs),
        input_output_aliases=aliases or {},
        scratch_shapes=scratch,
        compiler_params=pltpu.CompilerParams(vmem_limit_bytes=VMEM),
        cost_estimate=cost,
    )(*args)


def cost(flops, nbytes):
    return pl.CostEstimate(flops=int(flops), bytes_accessed=int(nbytes), transcendentals=0)


def rank_before(hits):
    items = hits.shape[1]
    earlier = (iota((items, items), 0) < iota((items, items), 1)).astype(jnp.bfloat16)
    before = jnp.dot(hits.astype(jnp.bfloat16), earlier, preferred_element_type=jnp.float32)
    return jnp.sum(before * hits, axis=0, keepdims=True).astype(jnp.int32)


def spread(values, items):
    groups = values.shape[1]
    share = items // groups
    same = iota((groups, items), 0) * share
    column = iota((groups, items), 1)
    same = ((column >= same) & (column < same + share)).astype(jnp.bfloat16)
    wide = jnp.broadcast_to(values.astype(jnp.float32), (8, groups)).astype(jnp.bfloat16)
    wide = jnp.dot(wide, same, preferred_element_type=jnp.float32)
    return wide[:1].astype(jnp.int32)


def image_slots(target, sections, cape):
    rows = target.shape[1]
    index = jnp.floor((target.astype(jnp.float32) + 0.5) * (1.0 / rows)).astype(jnp.int32)
    place = target - index * rows
    hits = ((index == iota((sections, rows), 0)) & (target >= 0)).astype(jnp.float32)
    rank = rank_before(hits)
    at_rank = (rank == iota((LANES, rows), 0)).astype(jnp.bfloat16)
    numbered = (hits * (place + 1).astype(jnp.float32)).astype(jnp.bfloat16)
    positions = lax.dot_general(
        numbered, at_rank, (((1,), (1,)), ((), ())), preferred_element_type=jnp.float32
    )
    return jnp.where(target >= 0, index * cape + rank, -1), positions - 1.0


def block_slots(owner, sections, capr, block_rows):
    owner = spread(owner, owner.shape[1] * block_rows)
    hits = ((owner == iota((sections, owner.shape[1]), 0)) & (owner >= 0)).astype(jnp.float32)
    return jnp.where(owner >= 0, owner * capr + rank_before(hits), -1)


def query_group(query_ref, h):
    heads = [
        query_ref[:, j * HD : (j + 1) * HD].astype(jnp.float32)
        for j in range(h * GROUP, (h + 1) * GROUP)
    ]
    return jnp.concatenate(heads, axis=0)


def prep_kernel(
    sections, cape, capr, block_rows, target_ref, owner_ref, query_ref, out_slot, out_block, out_message
):
    out_slot[...], positions = image_slots(target_ref[...], sections, cape)
    heads = query_ref.shape[1] // HD
    query = jnp.concatenate([query_group(query_ref, h) for h in range(heads // GROUP)], axis=0)
    query = query.astype(jnp.bfloat16)
    out_message[:, :heads, :] = jnp.broadcast_to(query[None], (sections,) + query.shape)
    out_message[:, heads:, :] = jnp.broadcast_to(
        positions.astype(jnp.bfloat16)[:, None, :], (sections, out_message.shape[1] - heads, LANES)
    )
    out_block[...] = block_slots(owner_ref[...], sections, capr, block_rows)


def open_kernel(
    sections, cape, capr, block_rows, group_ref, base_ref, half_ref, weight_hbm, target_hbm, owner_hbm, query_hbm,
    image_hbm, text_hbm, out_a, out_b, out_slot, out_block, out_pick, target_ref, owner_ref, query_ref, sems
):
    piece_b = out_b.shape[0]
    piece = out_a.shape[0] - GROUP - sections
    at = pl.multiple_of(group_ref[0] * (piece + piece_b), LANES)
    moves = [
        (target_hbm, target_ref),
        (query_hbm, query_ref),
        (owner_hbm, owner_ref),
        (weight_hbm.at[pl.ds(at, piece)], out_a.at[pl.ds(0, piece)]),
        (weight_hbm.at[pl.ds(at + piece, piece_b)], out_b),
    ]
    width = piece + piece_b
    row = 0
    for kind, source in enumerate((image_hbm, text_hbm)):
        rows = source.shape[0] if kind == 0 else out_pick.shape[0] - row
        first = source.shape[0] - rows
        for j in range(out_pick.shape[1] // width):
            lane = pl.multiple_of((2 * j + 1 - group_ref[0]) * width, LANES)
            moves.append(
                (
                    source.at[pl.ds(first, rows), pl.ds(lane, width)],
                    out_pick.at[pl.ds(row, rows), pl.ds(j * width, width)],
                )
            )
        row += rows
    copies = [
        pltpu.make_async_copy(source, target, sems.at[k])
        for k, (source, target) in enumerate(moves)
    ]
    for copy in copies:
        copy.start()
    copies[0].wait()
    out_slot[...], positions = image_slots(target_ref[...], sections, cape)
    copies[1].wait()
    groups = query_ref.shape[1] // (GROUP * HD)
    told = [query_group(query_ref, h) for h in range(groups)]
    told.append(jnp.zeros((GROUP, out_a.shape[1] - groups * HD), jnp.float32))
    told = jnp.concatenate(told, axis=1)
    positions = jnp.concatenate(
        [positions, jnp.zeros((sections, out_a.shape[1] - LANES), jnp.float32)], axis=1
    )
    out_a[piece:] = jnp.concatenate([told, positions], axis=0).astype(jnp.bfloat16)
    copies[2].wait()
    out_block[...] = block_slots(owner_ref[...], sections, capr, block_rows)
    for copy in copies[3:]:
        copy.wait()


FACTOR_ROWS = 16


def factor_kernel(image_ref, text_ref, out_ref):
    terms = [term for ref in (image_ref, text_ref) for term in bf16_terms(ref[...], 3)]
    terms.append(jnp.zeros((out_ref.shape[0] - len(terms), out_ref.shape[1]), jnp.float32))
    out_ref[...] = jnp.concatenate(terms, axis=0).astype(jnp.bfloat16)


def diagonal(size):
    return iota((size, size), 0) == iota((size, size), 1)


def own_norm_kernel(
    slices, group_ref, half_ref, near_hbm, far_hbm, gains_hbm, out_ref, factor_ref, near, far, gain, sems
):
    tiles, tile, features = near.shape
    width = out_ref.shape[2]
    first = near_hbm.shape[0] - tiles * tile
    half, group = half_ref[0], group_ref[0]
    copies = []
    for side in range(2):
        at = pl.multiple_of((half if side == 0 else 1 - half) * features, features)
        copies.append(
            pltpu.make_async_copy(gains_hbm.at[:, pl.ds(at, features)], gain.at[side], sems.at[side])
        )
    for i in range(tiles):
        at = pl.ds(first + i * tile, tile)
        for side, (hbm, vmem) in enumerate(((near_hbm, near), (far_hbm, far))):
            copies.append(
                pltpu.make_async_copy(hbm.at[at], vmem.at[i], sems.at[2 + 2 * i + side])
            )
    for copy in copies:
        copy.start()
    copies[0].wait()
    copies[1].wait()
    factors = []
    for i in range(tiles):
        copies[2 + 2 * i].wait()
        copies[3 + 2 * i].wait()
        total = 0.0
        for ref in (near, far):
            value = ref[i].astype(jnp.float32)
            total = total + jnp.sum(value * value, axis=1, keepdims=True)
        factor = lax.rsqrt(total * (1.0 / (2 * features)) + 1e-06)
        factors.append(jnp.sum(jnp.where(diagonal(tile), factor, 0.0), axis=0, keepdims=True))
        for side, ref in enumerate((near, far)):
            for j in range(slices // 2):
                at = pl.ds(pl.multiple_of((2 * j + group) * width, LANES), width)
                block = ref[i, :, at].astype(jnp.float32) * factor * gain[side, :, at]
                out_ref[side * (slices // 2) + j, pl.ds(i * tile, tile)] = block.astype(jnp.bfloat16)
    missing = factor_ref.shape[1] - tiles * tile
    if missing:
        factors.append(jnp.zeros((1, missing), jnp.float32))
    factor_ref[...] = jnp.concatenate(factors, axis=1)


def own_norm(slices, group, half, near, far, gains, rows):
    features = near.shape[1]
    tile = NORM_TILE
    held = pltpu.VMEM((rows // tile, tile, features), jnp.bfloat16)
    return pl.pallas_call(
        functools.partial(own_norm_kernel, slices),
        out_shape=(
            jax.ShapeDtypeStruct((slices, rows, features // slices), jnp.bfloat16),
            jax.ShapeDtypeStruct((1, near.shape[0]), jnp.float32),
        ),
        in_specs=[pl.BlockSpec(memory_space=pltpu.SMEM)] * 2
        + [pl.BlockSpec(memory_space=pltpu.HBM)] * 3,
        out_specs=[pl.BlockSpec(memory_space=pltpu.VMEM)] * 2,
        scratch_shapes=[
            held,
            held,
            pltpu.VMEM((2, 1, features), jnp.float32),
            pltpu.SemaphoreType.DMA((2 + 2 * (rows // tile),)),
        ],
        compiler_params=pltpu.CompilerParams(vmem_limit_bytes=VMEM),
        cost_estimate=cost(1, 1),
    )(group, half, near, far, gains)


def other_kernel(
    first_term, first, group_ref, half_ref, index_ref, base_ref, near_hbm, far_hbm, factor_ref, gains_ref, *refs
):
    *weights, out_ref, held, sems = refs
    slices, rows, width = held.shape
    half = slices // 2
    copies = [
        pltpu.make_async_copy(
            hbm.at[pl.ds(first, rows), pl.ds(j * width, width)],
            held.at[side * half + j],
            sems.at[side * half + j],
        )
        for side, hbm in enumerate((near_hbm, far_hbm))
        for j in range(half)
    ]
    for copy in copies:
        copy.start()
    terms = factor_ref[...].astype(jnp.float32)
    factor = terms[first_term : first_term + 1]
    for k in range(1, 3):
        factor = factor + terms[first_term + k : first_term + k + 1]
    factor = jnp.sum(jnp.where(diagonal(rows), factor[:, :rows], 0.0), axis=1, keepdims=True)
    for copy in copies:
        copy.wait()
    total = 0.0
    for k in range(slices):
        block = index_ref[base_ref[0] + k]
        far = (block >= half).astype(jnp.int32)
        side = half_ref[0] + far - 2 * far * half_ref[0]
        lane = (2 * (side * half + block - far * half) + group_ref[0]) * width
        value = held[block].astype(jnp.float32) * factor
        value = value * gains_ref[:, pl.ds(pl.multiple_of(lane, LANES), width)]
        value = value.astype(jnp.bfloat16)
        at = 0
        for weight in weights[2 * k : 2 * k + 2]:
            depth = weight.shape[0] // LANES * LANES
            total = total + jnp.dot(
                value[:, at : at + depth], weight[:depth], preferred_element_type=jnp.float32
            )
            at += depth
    out_ref[...] = total.astype(jnp.bfloat16)


NORM_TILE = 64


def norm_kernel(blocks, half_ref, near_hbm, far_hbm, gains_hbm, out_ref, done_ref, near, far, gain, sems):
    tiles, tile, features = near.shape
    width = out_ref.shape[2]
    half = half_ref[0]
    copies = []
    for side in range(2):
        at = pl.multiple_of((half if side == 0 else 1 - half) * features, features)
        copies.append(
            pltpu.make_async_copy(gains_hbm.at[:, pl.ds(at, features)], gain.at[side], sems.at[side])
        )
    for i in range(tiles):
        at = pl.ds(i * tile, tile)
        for side, (hbm, vmem) in enumerate(((near_hbm, near), (far_hbm, far))):
            copies.append(
                pltpu.make_async_copy(hbm.at[at], vmem.at[i], sems.at[2 + 2 * i + side])
            )
    for copy in copies:
        copy.start()
    done_ref[...] = jnp.zeros_like(done_ref)
    copies[0].wait()
    copies[1].wait()
    for i in range(tiles):
        copies[2 + 2 * i].wait()
        copies[3 + 2 * i].wait()
        total = 0.0
        for ref in (near, far):
            value = ref[i].astype(jnp.float32)
            total = total + jnp.sum(value * value, axis=1, keepdims=True)
        factor = lax.rsqrt(total * (1.0 / (2 * features)) + 1e-06)
        for side, ref in enumerate((near, far)):
            for j in range(blocks // 2):
                at = pl.ds(j * width, width)
                block = ref[i, :, at].astype(jnp.float32) * factor * gain[side, :, at]
                out_ref[side * (blocks // 2) + j, pl.ds(i * tile, tile)] = block.astype(jnp.bfloat16)


def normalize(blocks, half, near, far, gains):
    rows, features = near.shape
    tile = min(NORM_TILE, rows)
    held = pltpu.VMEM((rows // tile, tile, features), jnp.bfloat16)
    return pl.pallas_call(
        functools.partial(norm_kernel, blocks),
        out_shape=(
            jax.ShapeDtypeStruct((blocks, rows, 2 * features // blocks), jnp.bfloat16),
            jax.ShapeDtypeStruct((8, LANES), jnp.float32),
        ),
        in_specs=[pl.BlockSpec(memory_space=pltpu.SMEM)]
        + [pl.BlockSpec(memory_space=pltpu.HBM)] * 3,
        out_specs=[pl.BlockSpec(memory_space=pltpu.VMEM)] * 2,
        scratch_shapes=[
            held,
            held,
            pltpu.VMEM((2, 1, features), jnp.float32),
            pltpu.SemaphoreType.DMA((2 + 2 * (rows // tile),)),
        ],
        compiler_params=pltpu.CompilerParams(vmem_limit_bytes=VMEM),
        cost_estimate=cost(1, 1),
    )(half, near, far, gains)


def pool_rows(pool_ref):
    block_rows = pool_ref.shape[1]
    pool = pool_ref[...].astype(jnp.float32)
    return jnp.concatenate([pool[:, i, :] for i in range(block_rows)], axis=0).astype(jnp.bfloat16)


def positions_in_slots(sent, source, cape):
    sources = sent.shape[0]
    slots = sources * cape
    column = iota((sources, slots), 1)
    rank = column - jnp.floor((column.astype(jnp.float32) + 0.5) * (1.0 / cape)).astype(jnp.int32) * cape
    at_source = (column >= source * cape) & (column < source * cape + cape)
    at_rank = (iota((LANES, slots), 0) == rank[:1]).astype(jnp.bfloat16)
    wide = jnp.dot(sent.astype(jnp.bfloat16), at_rank, preferred_element_type=jnp.float32)
    return jnp.sum(jnp.where(at_source, wide, 0.0), axis=0, keepdims=True).astype(jnp.int32)


def pool_kernel(cape, message_ref, pool_ref, owner_ref, fill_ref, out_ref, position_ref):
    sections, heads = out_ref.shape[0], out_ref.shape[1]
    held, block_rows, _ = pool_ref.shape
    request = iota((sections * GROUP, held), 0)
    owner = owner_ref[...]
    owned = (request >= owner * GROUP) & (request < owner * GROUP + GROUP)
    mask = jnp.concatenate(
        [(owned & (fill_ref[...] > i)).astype(jnp.float32) for i in range(block_rows)], axis=1
    )
    pool = pool_rows(pool_ref)
    for h in range(heads // GROUP):
        query = message_ref[:, h * GROUP : (h + 1) * GROUP, :].astype(jnp.float32)
        query = query.reshape(sections * GROUP, HD).astype(jnp.bfloat16)
        key = pool[:, 2 * h * HD : (2 * h + 1) * HD]
        value = pool[:, (2 * h + 1) * HD : (2 * h + 2) * HD]
        top, total, acc = attend(query, key, value, mask > 0.0)
        lane = iota((sections * GROUP, LANES), 1)
        state = jnp.where(lane == 0, top, jnp.where(lane == 1, total, 0.0))
        out_ref[:, h * GROUP : (h + 1) * GROUP, :HD] = acc.reshape(sections, GROUP, HD)
        out_ref[:, h * GROUP : (h + 1) * GROUP, HD:] = state.reshape(sections, GROUP, LANES)
    sent = message_ref[:, heads : heads + 1, :].astype(jnp.float32).reshape(sections, LANES)
    position_ref[...] = positions_in_slots(sent, iota((sections, 1), 0), cape)


def ring_pool_kernel(sections, cape, index_ref, base_ref, *refs):
    told_refs = refs[:sections]
    pool_ref, owner_ref, fill_ref, slot_ref, out_ref, position_ref, place_ref = refs[sections:]
    place_ref[...] = (iota(place_ref.shape, 0) == slot_ref[...]).astype(jnp.bfloat16)
    sources = [index_ref[base_ref[0] + sections + j] for j in range(sections)]
    held, block_rows, _ = pool_ref.shape
    heads = out_ref.shape[1] // 2
    groups = heads // GROUP
    part = told_refs[0].shape[0] - GROUP - sections
    told = [ref[part:, :].astype(jnp.float32) for ref in told_refs]
    owner, fill = owner_ref[...], fill_ref[...]
    masks = []
    for j in range(sections):
        owned = owner == sources[j]
        mask = [(owned & (fill > i)).astype(jnp.float32) for i in range(block_rows)]
        masks.append(jnp.broadcast_to(jnp.concatenate(mask, axis=1), (GROUP, held * block_rows)))
    mask = jnp.concatenate(masks, axis=0) > 0.0
    pool = pool_rows(pool_ref)
    sums, states = [], []
    lane = iota((sections * GROUP, LANES), 1)
    for h in range(groups):
        query = jnp.concatenate([t[:GROUP, h * HD : (h + 1) * HD] for t in told], axis=0)
        key = pool[:, 2 * h * HD : (2 * h + 1) * HD]
        value = pool[:, (2 * h + 1) * HD : (2 * h + 2) * HD]
        top, total, acc = attend(query.astype(jnp.bfloat16), key, value, mask)
        terms = bf16_terms(top, 3) + bf16_terms(total, 2)
        state = jnp.zeros((sections * GROUP, LANES), jnp.float32)
        for k, term in enumerate(terms):
            state = jnp.where(lane == k, term, state)
        sums.append(acc)
        states.append(state)
    for j in range(sections):
        at = slice(j * GROUP, (j + 1) * GROUP)
        rows = jnp.concatenate([x[at] for x in sums] + [x[at] for x in states], axis=0)
        out_ref[sources[j]] = rows.astype(jnp.bfloat16)
    own = iota((sections, LANES), 0) == sources[0]
    sent = jnp.concatenate(
        [
            jnp.sum(jnp.where(own, t[GROUP:, :LANES], 0.0), axis=0, keepdims=True) for t in told
        ],
        axis=0,
    )
    source = jnp.zeros((sections, 1), jnp.int32)
    for j in range(sections):
        source = jnp.where(iota((sections, 1), 0) == j, sources[j], source)
    position_ref[...] = positions_in_slots(sent, source, cape)


def bf16_terms(value, count):
    terms = []
    for _ in range(count):
        term = value.astype(jnp.bfloat16).astype(jnp.float32)
        terms.append(term)
        value = value - term
    return terms


def attend(query, key, value, mask):
    scores = (
        lax.dot_general(query, key, (((1,), (1,)), ((), ())), preferred_element_type=jnp.float32)
        * SCALE
    )
    scores = jnp.where(mask, scores, NEG)
    top = jnp.max(scores, axis=1, keepdims=True)
    expo = jnp.where(mask, jnp.exp(scores - top), 0.0)
    total = jnp.sum(expo, axis=1, keepdims=True)
    acc = jnp.dot(expo.astype(jnp.bfloat16), value, preferred_element_type=jnp.float32)
    return top, total, acc


def dots_kernel(first, count, biased, index_ref, base_ref, *refs):
    bias = 0.0
    if biased:
        bias, refs = refs[0][...], refs[1:]
    weights, refs = refs[: 2 * count], refs[2 * count :]
    kinds = len(refs) // 3 if len(refs) % 3 == 0 else len(refs) // 2
    rows_refs, given, outs = refs[:kinds], refs[kinds:-kinds], refs[-kinds:]
    pieces = (rows_refs[0].shape[2] - weights[1].shape[0], weights[1].shape[0])
    for kind, (rows_ref, out) in enumerate(zip(rows_refs, outs)):
        total = given[kind][...] + bias if given else 0.0
        for k in range(count):
            block = index_ref[base_ref[0] + first + k]
            for p, at in enumerate((slice(0, pieces[0]), slice(pieces[0], sum(pieces)))):
                total = total + jnp.dot(
                    rows_ref[block, :, at],
                    weights[2 * k + p][: pieces[p]],
                    preferred_element_type=jnp.float32,
                )
        out[...] = total.astype(out.dtype)


def last_image_kernel(image_ref, other_ref, place_ref, partial_ref, send_out):
    sections, cape, _ = send_out.shape
    width = image_ref.shape[1]
    image = image_ref[...] + other_ref[...].astype(jnp.float32)
    send = jnp.dot(place_ref[...], image.astype(jnp.bfloat16), preferred_element_type=jnp.float32)
    send_out[:, :, :width] = send.astype(jnp.bfloat16).reshape(sections, cape, width)
    send_out[:, :, width:] = partial_ref[...]


def finish_kernel(text_ref, image_ref, bias_ref, slot_ref, text_out, send_out):
    text_out[...] = (text_ref[...] + bias_ref[...]).astype(jnp.bfloat16)
    image = (image_ref[...] + bias_ref[...]).astype(jnp.bfloat16)
    place = (iota((send_out.shape[0], image.shape[0]), 0) == slot_ref[...]).astype(jnp.bfloat16)
    send_out[...] = jnp.dot(place, image, preferred_element_type=jnp.float32).astype(jnp.bfloat16)


def place_kernel(
    split, text_ref, *refs
):
    arrived_ref, position_ref, slot_ref, count_ref, rows_ref, blocks_ref = refs[-6:]
    rows, width = rows_ref.shape
    text = text_ref[...].astype(jnp.float32)
    if split:
        text = (text + refs[0][...].astype(jnp.float32)).astype(jnp.bfloat16)
        lead = jnp.zeros((rows - text.shape[0], width), jnp.float32)
        text = jnp.concatenate([lead, text.astype(jnp.float32)], axis=0)
    sections, cape, _ = arrived_ref.shape
    row = iota((rows, sections * cape), 0)
    match = (row == position_ref[...]) & (row < count_ref[0])
    filled = jnp.max(match.astype(jnp.float32), axis=1, keepdims=True) > 0.0
    arrived = arrived_ref[:, :, :width].reshape(sections * cape, width)
    placed = jnp.dot(match.astype(jnp.bfloat16), arrived, preferred_element_type=jnp.float32)
    whole = jnp.where(filled, placed, text).astype(jnp.bfloat16)
    slots = (iota((blocks_ref.shape[0], rows), 0) == slot_ref[...]).astype(jnp.bfloat16)
    blocks_ref[...] = jnp.dot(slots, whole, preferred_element_type=jnp.float32).astype(jnp.bfloat16)
    rows_ref[...] = whole


def decode_kernel(packed, rows_ref, query_ref, partial_ref, length_ref, out_ref):
    rows = rows_ref.shape[0]
    heads = query_ref.shape[1] // HD
    mask = iota((GROUP, rows), 1) < length_ref[0]
    if packed:
        partial = partial_ref[:, : 2 * heads, rows_ref.shape[1] :].astype(jnp.float32)
    for h in range(heads // GROUP):
        at = slice(h * GROUP, (h + 1) * GROUP)
        key = rows_ref[:, 2 * h * HD : (2 * h + 1) * HD]
        value = rows_ref[:, (2 * h + 1) * HD : (2 * h + 2) * HD]
        query = query_group(query_ref, h).astype(jnp.bfloat16)
        top, total, acc = attend(query, key, value, mask)
        if packed:
            old_acc = partial[:, at, :]
            state = partial[:, heads + h * GROUP : heads + (h + 1) * GROUP, :]
            old_top = state[:, :, 0:1] + state[:, :, 1:2] + state[:, :, 2:3]
            old_total = state[:, :, 3:4] + state[:, :, 4:5]
        else:
            old_acc = partial_ref[:, at, :HD]
            old_top = partial_ref[:, at, HD : HD + 1]
            old_total = partial_ref[:, at, HD + 1 : HD + 2]
        best = jnp.maximum(top, jnp.max(old_top, axis=0))
        fresh_factor = jnp.exp(top - best)
        old_factor = jnp.exp(old_top - best[None])
        total = total * fresh_factor + jnp.sum(old_total * old_factor, axis=0)
        acc = acc * fresh_factor + jnp.sum(old_acc * old_factor, axis=0)
        result = (acc / total).astype(jnp.bfloat16)
        for j in range(GROUP):
            lane = (h * GROUP + j) * HD
            out_ref[:, lane : lane + HD] = result[j : j + 1]


def beside(x):
    return lax.ppermute(x, "tensor", [(0, 1), (1, 0)])


def exchange(x):
    return lax.all_to_all(x, "section", split_axis=0, concat_axis=0, tiled=True)


def ring_order(sections):
    return list(range(0, sections, 2)) + list(range(1, sections, 2))[::-1]


def ring_tables(sections, tensors):
    order = ring_order(sections)
    table = np.zeros((sections, tensors, 2 * sections), np.int32)
    distances = [0] + [s * d for d in range(1, sections // 2) for s in (1, -1)] + [sections // 2]
    for at, section in enumerate(order):
        for step, distance in enumerate(distances):
            source = order[(at - distance) % sections]
            for t in range(tensors):
                table[section, t, step] = (source - t * (sections // tensors)) % sections
            table[section, :, sections + step] = source
    return table


def after(values, others):
    return lax.optimization_barrier((tuple(values), tuple(others)))


def ring_path(
    text, image, target, weight, bias, gains, queries, pool, owner, fill, block_owner, half, cape, capr
):
    sections = lax.axis_size("section")
    tensors = lax.axis_size("tensor")
    order = ring_order(sections)
    ahead = [(order[i], order[(i + 1) % sections]) for i in range(sections)]
    back = [(b, a) for a, b in ahead]
    depth, width = weight.shape
    piece = depth // 4
    rows = text.shape[0]
    text_rows = rows - rows // LEAST_IMAGE
    heads = queries.shape[1] // HD
    group = lax.axis_index("groups").astype(jnp.int32).reshape(1)

    def up(x):
        return lax.ppermute(x, "section", ahead)

    def down(x):
        return lax.ppermute(x, "section", back)

    def across(x):
        return lax.ppermute(x, "groups", [(0, 1), (1, 0)])

    index = jnp.asarray(ring_tables(sections, tensors).reshape(-1))
    base = (lax.axis_index("section") * tensors + lax.axis_index("tensor")) * (2 * sections)
    base = base.astype(jnp.int32).reshape(1)

    def dots(first, count, inputs, states, dtype, *added):
        parts = [*added, *(p for pair in slices[first : first + count] for p in pair)]
        shapes = tuple(jax.ShapeDtypeStruct((x.shape[1], width), dtype) for x in inputs)
        return call(
            functools.partial(dots_kernel, first, count, len(added)),
            shapes, index, base, *parts, *inputs, *states,
            smem=(0, 1), cost=cost(1, 1),
            aliases={2 + len(parts) + len(inputs) + k: k for k in range(len(states))},
        )

    def other_rows(first_term, first, rows):
        parts = [p for pair in slices for p in pair]
        return pl.pallas_call(
            functools.partial(other_kernel, first_term, first),
            out_shape=jax.ShapeDtypeStruct((rows, width), jnp.bfloat16),
            in_specs=[pl.BlockSpec(memory_space=pltpu.SMEM)] * 4
            + [pl.BlockSpec(memory_space=pltpu.HBM)] * 2
            + [pl.BlockSpec(memory_space=pltpu.VMEM)] * (2 + len(parts)),
            out_specs=pl.BlockSpec(memory_space=pltpu.VMEM),
            scratch_shapes=[
                pltpu.VMEM((sections, rows, depth // 2), jnp.bfloat16),
                pltpu.SemaphoreType.DMA((sections,)),
            ],
            compiler_params=pltpu.CompilerParams(vmem_limit_bytes=VMEM),
            cost_estimate=cost(1, 1),
        )(group, half, index, base, others, others_far, factors, gains, *parts)

    spaces = [pltpu.SMEM] * 3 + [pltpu.HBM] * 6
    own_a, own_b, image_slot, block_slot, picked = pl.pallas_call(
        functools.partial(open_kernel, sections, cape, capr, pool.shape[1]),
        out_shape=(
            jax.ShapeDtypeStruct((piece + GROUP + sections, width), jnp.bfloat16),
            jax.ShapeDtypeStruct((depth // 2 - piece, width), jnp.bfloat16),
            jax.ShapeDtypeStruct((1, rows), jnp.int32),
            jax.ShapeDtypeStruct((1, block_owner.shape[1] * pool.shape[1]), jnp.int32),
            jax.ShapeDtypeStruct((rows + text_rows, text.shape[1] // 2), jnp.bfloat16),
        ),
        in_specs=[pl.BlockSpec(memory_space=space) for space in spaces],
        out_specs=[pl.BlockSpec(memory_space=pltpu.VMEM)] * 5,
        scratch_shapes=[
            pltpu.VMEM(target.shape, jnp.int32),
            pltpu.VMEM(block_owner.shape, jnp.int32),
            pltpu.VMEM(queries.shape, jnp.bfloat16),
            pltpu.SemaphoreType.DMA((5 + sections,)),
        ],
        compiler_params=pltpu.CompilerParams(vmem_limit_bytes=VMEM_ALL),
    )(group, base, half, weight, target, block_owner, queries, image, text)
    near_a = [up(own_a), down(own_a)]
    others = across(picked)
    text_far, image_far = beside(text), beside(image)
    (own_b,), (text_far, image_far) = after((own_b,), (text_far, image_far))
    near_b = [up(own_b), down(own_b)]
    last = sections // 2 - 1
    slices = [(own_a, own_b)]
    normed_image, image_factor = own_norm(sections, group, half, image, image_far, gains, rows)
    waiting, late = [image_factor], text_far
    for step in range(1, last + 1):
        near_a, waiting = after(near_a, waiting)
        held_a = near_a
        near_a = [up(near_a[0])] + ([down(near_a[1])] if step < last else [])
        near_b, waiting = after(near_b, [*waiting, late])
        *waiting, late = waiting
        slices += list(zip(held_a, near_b))
        near_b = ([up(near_b[0])] if step < last else []) + [down(near_b[1])]
        if step == 1:
            image_factor = waiting[0]
            normed_text, text_factor = own_norm(
                sections, group, half, text, late, gains, text_rows
            )
            waiting, late = [image_factor, text_factor], image_factor
        elif step == 2:
            factors = call(
                factor_kernel,
                jax.ShapeDtypeStruct((FACTOR_ROWS, rows), jnp.bfloat16),
                *waiting,
            )
            state = dots(0, 2 * step + 1, (normed_text, normed_image), (), jnp.float32)
            waiting, late = [*state], factors
    state = waiting
    (others, factors), last_slice = after((others, late), (*near_a, *near_b))
    slices.append(last_slice)
    others_far, factors = beside(others), across(factors)
    told = [a for a, _ in slices]
    partial, position, place = call(
        functools.partial(ring_pool_kernel, sections, cape),
        (
            jax.ShapeDtypeStruct((sections, 2 * heads, HD), jnp.bfloat16),
            jax.ShapeDtypeStruct((1, sections * cape), jnp.int32),
            jax.ShapeDtypeStruct((sections * cape, rows), jnp.bfloat16),
        ),
        index, base, *told, pool, owner, fill, image_slot,
        smem=(0, 1),
    )
    done = 2 * last - 1
    sums = dots(done, sections - done, (normed_text, normed_image), state, jnp.float32, bias)
    (others_far, factors), (*sums, partial, place) = after(
        (others_far, factors), (*sums, partial, place)
    )
    image_back = across(other_rows(0, 0, rows))
    text_back = other_rows(3, rows, text_rows)
    (image_back,), (text_back,) = after((image_back,), (text_back,))
    text_back = across(text_back)
    send = call(
        last_image_kernel,
        jax.ShapeDtypeStruct((sections, cape, width + HD), jnp.bfloat16),
        sums[1], image_back, place, partial,
    )
    arrived = exchange(send)
    return (sums[0], text_back), arrived, position, block_slot, arrived


def gather_path(
    text, image, target, weight, bias, gains, queries, pool, owner, fill, block_owner, half, cape, capr
):
    sections = lax.axis_size("section")
    rows, near = text.shape
    width = weight.shape[1]
    heads = queries.shape[1] // HD
    image_slot, block_slot, message = call(
        functools.partial(prep_kernel, sections, cape, capr, pool.shape[1]),
        (
            jax.ShapeDtypeStruct((1, rows), jnp.int32),
            jax.ShapeDtypeStruct((1, block_owner.shape[1] * pool.shape[1]), jnp.int32),
            jax.ShapeDtypeStruct((sections, 2 * heads, LANES), jnp.bfloat16),
        ),
        target, block_owner, queries,
    )
    partial, position = call(
        functools.partial(pool_kernel, cape),
        (
            jax.ShapeDtypeStruct((sections, heads, 2 * HD), jnp.float32),
            jax.ShapeDtypeStruct((1, sections * cape), jnp.int32),
        ),
        exchange(message), pool, owner, fill,
    )
    normed = [normalize(2, half, x, beside(x), gains)[0] for x in (text, image)]
    whole = lax.all_gather(weight, "section", axis=0, tiled=True)
    first = lax.dynamic_slice_in_dim(whole, half[0] * near, near, 0)
    second = lax.dynamic_slice_in_dim(whole, (1 - half[0]) * near, near, 0)
    text_sum, image_sum = (
        jnp.dot(n[0], first, preferred_element_type=jnp.float32)
        + jnp.dot(n[1], second, preferred_element_type=jnp.float32)
        for n in normed
    )
    text_rows, send = call(
        finish_kernel,
        (
            jax.ShapeDtypeStruct((rows, width), jnp.bfloat16),
            jax.ShapeDtypeStruct((sections * cape, width), jnp.bfloat16),
        ),
        text_sum, image_sum, bias, image_slot,
    )
    arrived = exchange(send.reshape(sections, cape, width))
    return (text_rows,), arrived, position, block_slot, exchange(partial)


def shards(
    text_embed,
    image_embed,
    image_count,
    prompt_len,
    embed_target,
    kv_weight,
    kv_bias,
    norm_gain,
    queries,
    old_pool,
    pool_owner,
    pool_fill,
    block_owner,
):
    sections, tensors = lax.axis_size("section"), lax.axis_size("tensor")
    rows = text_embed.shape[0]
    width = kv_weight.shape[1]
    heads = queries.shape[1] // HD
    cape = rows // sections
    block_rows = old_pool.shape[1]
    capr = (block_owner.shape[0] + sections - 1) // sections * block_rows
    ring = (
        sections == 8
        and tensors == 2
        and lax.axis_size("groups") == 2
        and kv_weight.shape[0] == 1024
        and rows == 2 * LANES
        and cape == 2 * heads
    )
    text_rows, arrived, position, block_slot, partial = (ring_path if ring else gather_path)(
        text_embed,
        image_embed,
        embed_target.reshape(1, -1),
        kv_weight,
        kv_bias.reshape(1, -1),
        norm_gain.reshape(1, -1),
        queries,
        old_pool,
        pool_owner.reshape(1, -1),
        pool_fill.reshape(1, -1),
        block_owner.reshape(1, -1),
        lax.axis_index("tensor").astype(jnp.int32).reshape(1),
        cape,
        capr,
    )
    whole_rows, block_data = call(
        functools.partial(place_kernel, ring),
        (
            jax.ShapeDtypeStruct((rows, width), jnp.bfloat16),
            jax.ShapeDtypeStruct((sections * capr, width), jnp.bfloat16),
        ),
        *text_rows,
        arrived,
        position,
        block_slot,
        image_count,
        smem=(len(text_rows) + 3,),
    )
    fresh = exchange(block_data.reshape(sections, capr, width)).reshape(sections * capr, width)
    decoded = call(
        functools.partial(decode_kernel, ring),
        jax.ShapeDtypeStruct((1, heads * HD), jnp.bfloat16),
        whole_rows,
        queries,
        partial,
        prompt_len,
        smem=(3,),
    )
    return decoded, fresh


def solution(mesh):
    return jax.shard_map(
        shards,
        mesh=mesh,
        in_specs=(
            P(("groups", "section"), "tensor"),
            P(("groups", "section"), "tensor"),
            P(("groups", "section")),
            P(("groups", "section")),
            P(("groups", "section")),
            P("section", "tensor"),
            P("tensor"),
            P(),
            P(("groups", "section"), "tensor"),
            P(("groups", "section"), None, "tensor"),
            P(("groups", "section")),
            P(("groups", "section")),
            P(("groups", "section")),
        ),
        out_specs=(P(("groups", "section"), "tensor"), P(("groups", "section"), "tensor")),
        check_vma=False,
    )
```

```python
import functools

import jax
import jax.numpy as jnp
import numpy as np
from jax import lax
from jax.experimental import pallas as pl
from jax.experimental.pallas import tpu as pltpu
from jax.sharding import PartitionSpec as P

HQ = 32
KVH = 4
HD = 128
GROUP = HQ // KVH
SCALE = HD ** (-0.5)
LANES = 128
NEG = -1e30
LEAST_IMAGE = 4
VMEM = 14 * 1024 * 1024
VMEM_ALL = 56 * 1024 * 1024


def iota(shape, dim):
    return lax.broadcasted_iota(jnp.int32, shape, dim)


def call(kernel, outs, *args, cost=None, smem=(), aliases=None, scratch=()):
    return pl.pallas_call(
        kernel,
        out_shape=outs,
        in_specs=[
            pl.BlockSpec(memory_space=pltpu.SMEM if i in smem else pltpu.VMEM)
            for i in range(len(args))
        ],
        out_specs=jax.tree.map(lambda _: pl.BlockSpec(memory_space=pltpu.VMEM), outs),
        input_output_aliases=aliases or {},
        scratch_shapes=scratch,
        compiler_params=pltpu.CompilerParams(vmem_limit_bytes=VMEM),
        cost_estimate=cost,
    )(*args)


def cost(flops, nbytes):
    return pl.CostEstimate(flops=int(flops), bytes_accessed=int(nbytes), transcendentals=0)


def rank_before(hits):
    items = hits.shape[1]
    earlier = (iota((items, items), 0) < iota((items, items), 1)).astype(jnp.bfloat16)
    before = jnp.dot(hits.astype(jnp.bfloat16), earlier, preferred_element_type=jnp.float32)
    return jnp.sum(before * hits, axis=0, keepdims=True).astype(jnp.int32)


def spread(values, items):
    groups = values.shape[1]
    share = items // groups
    same = iota((groups, items), 0) * share
    column = iota((groups, items), 1)
    same = ((column >= same) & (column < same + share)).astype(jnp.bfloat16)
    wide = jnp.broadcast_to(values.astype(jnp.float32), (8, groups)).astype(jnp.bfloat16)
    wide = jnp.dot(wide, same, preferred_element_type=jnp.float32)
    return wide[:1].astype(jnp.int32)


def image_slots(target, sections, cape):
    rows = target.shape[1]
    index = jnp.floor((target.astype(jnp.float32) + 0.5) * (1.0 / rows)).astype(jnp.int32)
    place = target - index * rows
    hits = ((index == iota((sections, rows), 0)) & (target >= 0)).astype(jnp.float32)
    rank = rank_before(hits)
    at_rank = (rank == iota((LANES, rows), 0)).astype(jnp.bfloat16)
    numbered = (hits * (place + 1).astype(jnp.float32)).astype(jnp.bfloat16)
    positions = lax.dot_general(
        numbered, at_rank, (((1,), (1,)), ((), ())), preferred_element_type=jnp.float32
    )
    return jnp.where(target >= 0, index * cape + rank, -1), positions - 1.0


def block_slots(owner, sections, capr, block_rows):
    owner = spread(owner, owner.shape[1] * block_rows)
    hits = ((owner == iota((sections, owner.shape[1]), 0)) & (owner >= 0)).astype(jnp.float32)
    return jnp.where(owner >= 0, owner * capr + rank_before(hits), -1)


def query_group(query_ref, h):
    heads = [
        query_ref[:, j * HD : (j + 1) * HD].astype(jnp.float32)
        for j in range(h * GROUP, (h + 1) * GROUP)
    ]
    return jnp.concatenate(heads, axis=0)


def prep_kernel(
    sections, cape, capr, block_rows, target_ref, owner_ref, query_ref, out_slot, out_block, out_message
):
    out_slot[...], positions = image_slots(target_ref[...], sections, cape)
    heads = query_ref.shape[1] // HD
    query = jnp.concatenate([query_group(query_ref, h) for h in range(heads // GROUP)], axis=0)
    query = query.astype(jnp.bfloat16)
    out_message[:, :heads, :] = jnp.broadcast_to(query[None], (sections,) + query.shape)
    out_message[:, heads:, :] = jnp.broadcast_to(
        positions.astype(jnp.bfloat16)[:, None, :], (sections, out_message.shape[1] - heads, LANES)
    )
    out_block[...] = block_slots(owner_ref[...], sections, capr, block_rows)


def open_kernel(
    sections, cape, capr, block_rows, group_ref, base_ref, half_ref, weight_hbm, target_hbm, owner_hbm, query_hbm,
    image_hbm, text_hbm, out_a, out_b, out_slot, out_block, out_pick, target_ref, owner_ref, query_ref, sems
):
    piece_b = out_b.shape[0]
    piece = out_a.shape[0] - GROUP - sections
    at = pl.multiple_of(group_ref[0] * (piece + piece_b), LANES)
    moves = [
        (target_hbm, target_ref),
        (query_hbm, query_ref),
        (owner_hbm, owner_ref),
        (weight_hbm.at[pl.ds(at, piece)], out_a.at[pl.ds(0, piece)]),
        (weight_hbm.at[pl.ds(at + piece, piece_b)], out_b),
    ]
    width = piece + piece_b
    row = 0
    for kind, source in enumerate((image_hbm, text_hbm)):
        rows = source.shape[0] if kind == 0 else out_pick.shape[0] - row
        first = source.shape[0] - rows
        for j in range(out_pick.shape[1] // width):
            lane = pl.multiple_of((2 * j + 1 - group_ref[0]) * width, LANES)
            moves.append(
                (
                    source.at[pl.ds(first, rows), pl.ds(lane, width)],
                    out_pick.at[pl.ds(row, rows), pl.ds(j * width, width)],
                )
            )
        row += rows
    copies = [
        pltpu.make_async_copy(source, target, sems.at[k])
        for k, (source, target) in enumerate(moves)
    ]
    for copy in copies:
        copy.start()
    copies[0].wait()
    out_slot[...], positions = image_slots(target_ref[...], sections, cape)
    copies[1].wait()
    groups = query_ref.shape[1] // (GROUP * HD)
    told = [query_group(query_ref, h) for h in range(groups)]
    told.append(jnp.zeros((GROUP, out_a.shape[1] - groups * HD), jnp.float32))
    told = jnp.concatenate(told, axis=1)
    positions = jnp.concatenate(
        [positions, jnp.zeros((sections, out_a.shape[1] - LANES), jnp.float32)], axis=1
    )
    out_a[piece:] = jnp.concatenate([told, positions], axis=0).astype(jnp.bfloat16)
    copies[2].wait()
    out_block[...] = block_slots(owner_ref[...], sections, capr, block_rows)
    for copy in copies[3:]:
        copy.wait()


FACTOR_ROWS = 16


def factor_kernel(image_ref, text_ref, out_ref):
    terms = [term for ref in (image_ref, text_ref) for term in bf16_terms(ref[...], 3)]
    terms.append(jnp.zeros((out_ref.shape[0] - len(terms), out_ref.shape[1]), jnp.float32))
    out_ref[...] = jnp.concatenate(terms, axis=0).astype(jnp.bfloat16)


def diagonal(size):
    return iota((size, size), 0) == iota((size, size), 1)


def own_norm_kernel(
    slices, group_ref, half_ref, near_hbm, far_hbm, gains_hbm, out_ref, factor_ref, near, far, gain, sems
):
    tiles, tile, features = near.shape
    width = out_ref.shape[2]
    first = near_hbm.shape[0] - tiles * tile
    half, group = half_ref[0], group_ref[0]
    copies = []
    for side in range(2):
        at = pl.multiple_of((half if side == 0 else 1 - half) * features, features)
        copies.append(
            pltpu.make_async_copy(gains_hbm.at[:, pl.ds(at, features)], gain.at[side], sems.at[side])
        )
    for i in range(tiles):
        at = pl.ds(first + i * tile, tile)
        for side, (hbm, vmem) in enumerate(((near_hbm, near), (far_hbm, far))):
            copies.append(
                pltpu.make_async_copy(hbm.at[at], vmem.at[i], sems.at[2 + 2 * i + side])
            )
    for copy in copies:
        copy.start()
    copies[0].wait()
    copies[1].wait()
    factors = []
    for i in range(tiles):
        copies[2 + 2 * i].wait()
        copies[3 + 2 * i].wait()
        total = 0.0
        for ref in (near, far):
            value = ref[i].astype(jnp.float32)
            total = total + jnp.sum(value * value, axis=1, keepdims=True)
        factor = lax.rsqrt(total * (1.0 / (2 * features)) + 1e-06)
        factors.append(jnp.sum(jnp.where(diagonal(tile), factor, 0.0), axis=0, keepdims=True))
        for side, ref in enumerate((near, far)):
            for j in range(slices // 2):
                at = pl.ds(pl.multiple_of((2 * j + group) * width, LANES), width)
                block = ref[i, :, at].astype(jnp.float32) * factor * gain[side, :, at]
                out_ref[side * (slices // 2) + j, pl.ds(i * tile, tile)] = block.astype(jnp.bfloat16)
    missing = factor_ref.shape[1] - tiles * tile
    if missing:
        factors.append(jnp.zeros((1, missing), jnp.float32))
    factor_ref[...] = jnp.concatenate(factors, axis=1)


def own_norm(slices, group, half, near, far, gains, rows):
    features = near.shape[1]
    tile = NORM_TILE
    held = pltpu.VMEM((rows // tile, tile, features), jnp.bfloat16)
    return pl.pallas_call(
        functools.partial(own_norm_kernel, slices),
        out_shape=(
            jax.ShapeDtypeStruct((slices, rows, features // slices), jnp.bfloat16),
            jax.ShapeDtypeStruct((1, near.shape[0]), jnp.float32),
        ),
        in_specs=[pl.BlockSpec(memory_space=pltpu.SMEM)] * 2
        + [pl.BlockSpec(memory_space=pltpu.HBM)] * 3,
        out_specs=[pl.BlockSpec(memory_space=pltpu.VMEM)] * 2,
        scratch_shapes=[
            held,
            held,
            pltpu.VMEM((2, 1, features), jnp.float32),
            pltpu.SemaphoreType.DMA((2 + 2 * (rows // tile),)),
        ],
        compiler_params=pltpu.CompilerParams(vmem_limit_bytes=VMEM),
        cost_estimate=cost(1, 1),
    )(group, half, near, far, gains)


def other_kernel(
    first_term, group_ref, half_ref, index_ref, base_ref, near_ref, far_ref, factor_ref, gains_ref, *refs
):
    *weights, out_ref = refs
    slices, rows = len(weights) // 2, out_ref.shape[0]
    half, width = slices // 2, near_ref.shape[1] // (slices // 2)
    terms = factor_ref[...].astype(jnp.float32)
    factor = terms[first_term : first_term + 1]
    for k in range(1, 3):
        factor = factor + terms[first_term + k : first_term + k + 1]
    factor = jnp.sum(jnp.where(diagonal(rows), factor[:, :rows], 0.0), axis=1, keepdims=True)
    total = 0.0
    for k in range(slices):
        block = index_ref[base_ref[0] + k]
        far = (block >= half).astype(jnp.int32)
        side = half_ref[0] + far - 2 * far * half_ref[0]
        lane = (2 * (side * half + block - far * half) + group_ref[0]) * width
        at = pl.ds(pl.multiple_of((block - far * half) * width, LANES), width)
        value = jnp.where(far > 0, far_ref[:, at], near_ref[:, at]).astype(jnp.float32) * factor
        value = value * gains_ref[:, pl.ds(pl.multiple_of(lane, LANES), width)]
        value = value.astype(jnp.bfloat16)
        at = 0
        for weight in weights[2 * k : 2 * k + 2]:
            depth = weight.shape[0] // LANES * LANES
            total = total + jnp.dot(
                value[:, at : at + depth], weight[:depth], preferred_element_type=jnp.float32
            )
            at += depth
    out_ref[...] = total.astype(jnp.bfloat16)


NORM_TILE = 64


def norm_kernel(blocks, half_ref, near_hbm, far_hbm, gains_hbm, out_ref, done_ref, near, far, gain, sems):
    tiles, tile, features = near.shape
    width = out_ref.shape[2]
    half = half_ref[0]
    copies = []
    for side in range(2):
        at = pl.multiple_of((half if side == 0 else 1 - half) * features, features)
        copies.append(
            pltpu.make_async_copy(gains_hbm.at[:, pl.ds(at, features)], gain.at[side], sems.at[side])
        )
    for i in range(tiles):
        at = pl.ds(i * tile, tile)
        for side, (hbm, vmem) in enumerate(((near_hbm, near), (far_hbm, far))):
            copies.append(
                pltpu.make_async_copy(hbm.at[at], vmem.at[i], sems.at[2 + 2 * i + side])
            )
    for copy in copies:
        copy.start()
    done_ref[...] = jnp.zeros_like(done_ref)
    copies[0].wait()
    copies[1].wait()
    for i in range(tiles):
        copies[2 + 2 * i].wait()
        copies[3 + 2 * i].wait()
        total = 0.0
        for ref in (near, far):
            value = ref[i].astype(jnp.float32)
            total = total + jnp.sum(value * value, axis=1, keepdims=True)
        factor = lax.rsqrt(total * (1.0 / (2 * features)) + 1e-06)
        for side, ref in enumerate((near, far)):
            for j in range(blocks // 2):
                at = pl.ds(j * width, width)
                block = ref[i, :, at].astype(jnp.float32) * factor * gain[side, :, at]
                out_ref[side * (blocks // 2) + j, pl.ds(i * tile, tile)] = block.astype(jnp.bfloat16)


def normalize(blocks, half, near, far, gains):
    rows, features = near.shape
    tile = min(NORM_TILE, rows)
    held = pltpu.VMEM((rows // tile, tile, features), jnp.bfloat16)
    return pl.pallas_call(
        functools.partial(norm_kernel, blocks),
        out_shape=(
            jax.ShapeDtypeStruct((blocks, rows, 2 * features // blocks), jnp.bfloat16),
            jax.ShapeDtypeStruct((8, LANES), jnp.float32),
        ),
        in_specs=[pl.BlockSpec(memory_space=pltpu.SMEM)]
        + [pl.BlockSpec(memory_space=pltpu.HBM)] * 3,
        out_specs=[pl.BlockSpec(memory_space=pltpu.VMEM)] * 2,
        scratch_shapes=[
            held,
            held,
            pltpu.VMEM((2, 1, features), jnp.float32),
            pltpu.SemaphoreType.DMA((2 + 2 * (rows // tile),)),
        ],
        compiler_params=pltpu.CompilerParams(vmem_limit_bytes=VMEM),
        cost_estimate=cost(1, 1),
    )(half, near, far, gains)


def pool_rows(pool_ref):
    block_rows = pool_ref.shape[1]
    pool = pool_ref[...].astype(jnp.float32)
    return jnp.concatenate([pool[:, i, :] for i in range(block_rows)], axis=0).astype(jnp.bfloat16)


def positions_in_slots(sent, source, cape):
    sources = sent.shape[0]
    slots = sources * cape
    column = iota((sources, slots), 1)
    rank = column - jnp.floor((column.astype(jnp.float32) + 0.5) * (1.0 / cape)).astype(jnp.int32) * cape
    at_source = (column >= source * cape) & (column < source * cape + cape)
    at_rank = (iota((LANES, slots), 0) == rank[:1]).astype(jnp.bfloat16)
    wide = jnp.dot(sent.astype(jnp.bfloat16), at_rank, preferred_element_type=jnp.float32)
    return jnp.sum(jnp.where(at_source, wide, 0.0), axis=0, keepdims=True).astype(jnp.int32)


def pool_kernel(cape, message_ref, pool_ref, owner_ref, fill_ref, out_ref, position_ref):
    sections, heads = out_ref.shape[0], out_ref.shape[1]
    held, block_rows, _ = pool_ref.shape
    request = iota((sections * GROUP, held), 0)
    owner = owner_ref[...]
    owned = (request >= owner * GROUP) & (request < owner * GROUP + GROUP)
    mask = jnp.concatenate(
        [(owned & (fill_ref[...] > i)).astype(jnp.float32) for i in range(block_rows)], axis=1
    )
    pool = pool_rows(pool_ref)
    for h in range(heads // GROUP):
        query = message_ref[:, h * GROUP : (h + 1) * GROUP, :].astype(jnp.float32)
        query = query.reshape(sections * GROUP, HD).astype(jnp.bfloat16)
        key = pool[:, 2 * h * HD : (2 * h + 1) * HD]
        value = pool[:, (2 * h + 1) * HD : (2 * h + 2) * HD]
        top, total, acc = attend(query, key, value, mask > 0.0)
        lane = iota((sections * GROUP, LANES), 1)
        state = jnp.where(lane == 0, top, jnp.where(lane == 1, total, 0.0))
        out_ref[:, h * GROUP : (h + 1) * GROUP, :HD] = acc.reshape(sections, GROUP, HD)
        out_ref[:, h * GROUP : (h + 1) * GROUP, HD:] = state.reshape(sections, GROUP, LANES)
    sent = message_ref[:, heads : heads + 1, :].astype(jnp.float32).reshape(sections, LANES)
    position_ref[...] = positions_in_slots(sent, iota((sections, 1), 0), cape)


def ring_pool_kernel(sections, cape, index_ref, base_ref, *refs):
    told_refs = refs[:sections]
    pool_ref, owner_ref, fill_ref, slot_ref, out_ref, position_ref, place_ref = refs[sections:]
    place_ref[...] = (iota(place_ref.shape, 0) == slot_ref[...]).astype(jnp.bfloat16)
    sources = [index_ref[base_ref[0] + sections + j] for j in range(sections)]
    held, block_rows, _ = pool_ref.shape
    heads = out_ref.shape[1] // 2
    groups = heads // GROUP
    part = told_refs[0].shape[0] - GROUP - sections
    told = [ref[part:, :].astype(jnp.float32) for ref in told_refs]
    owner, fill = owner_ref[...], fill_ref[...]
    masks = []
    for j in range(sections):
        owned = owner == sources[j]
        mask = [(owned & (fill > i)).astype(jnp.float32) for i in range(block_rows)]
        masks.append(jnp.broadcast_to(jnp.concatenate(mask, axis=1), (GROUP, held * block_rows)))
    mask = jnp.concatenate(masks, axis=0) > 0.0
    pool = pool_rows(pool_ref)
    sums, states = [], []
    lane = iota((sections * GROUP, LANES), 1)
    for h in range(groups):
        query = jnp.concatenate([t[:GROUP, h * HD : (h + 1) * HD] for t in told], axis=0)
        key = pool[:, 2 * h * HD : (2 * h + 1) * HD]
        value = pool[:, (2 * h + 1) * HD : (2 * h + 2) * HD]
        top, total, acc = attend(query.astype(jnp.bfloat16), key, value, mask)
        terms = bf16_terms(top, 3) + bf16_terms(total, 2)
        state = jnp.zeros((sections * GROUP, LANES), jnp.float32)
        for k, term in enumerate(terms):
            state = jnp.where(lane == k, term, state)
        sums.append(acc)
        states.append(state)
    for j in range(sections):
        at = slice(j * GROUP, (j + 1) * GROUP)
        rows = jnp.concatenate([x[at] for x in sums] + [x[at] for x in states], axis=0)
        out_ref[sources[j]] = rows.astype(jnp.bfloat16)
    own = iota((sections, LANES), 0) == sources[0]
    sent = jnp.concatenate(
        [
            jnp.sum(jnp.where(own, t[GROUP:, :LANES], 0.0), axis=0, keepdims=True) for t in told
        ],
        axis=0,
    )
    source = jnp.zeros((sections, 1), jnp.int32)
    for j in range(sections):
        source = jnp.where(iota((sections, 1), 0) == j, sources[j], source)
    position_ref[...] = positions_in_slots(sent, source, cape)


def bf16_terms(value, count):
    terms = []
    for _ in range(count):
        term = value.astype(jnp.bfloat16).astype(jnp.float32)
        terms.append(term)
        value = value - term
    return terms


def attend(query, key, value, mask):
    scores = (
        lax.dot_general(query, key, (((1,), (1,)), ((), ())), preferred_element_type=jnp.float32)
        * SCALE
    )
    scores = jnp.where(mask, scores, NEG)
    top = jnp.max(scores, axis=1, keepdims=True)
    expo = jnp.where(mask, jnp.exp(scores - top), 0.0)
    total = jnp.sum(expo, axis=1, keepdims=True)
    acc = jnp.dot(expo.astype(jnp.bfloat16), value, preferred_element_type=jnp.float32)
    return top, total, acc


def dots_kernel(first, count, biased, index_ref, base_ref, *refs):
    bias = 0.0
    if biased:
        bias, refs = refs[0][...], refs[1:]
    weights, refs = refs[: 2 * count], refs[2 * count :]
    kinds = len(refs) // 3 if len(refs) % 3 == 0 else len(refs) // 2
    rows_refs, given, outs = refs[:kinds], refs[kinds:-kinds], refs[-kinds:]
    pieces = (rows_refs[0].shape[2] - weights[1].shape[0], weights[1].shape[0])
    for kind, (rows_ref, out) in enumerate(zip(rows_refs, outs)):
        total = given[kind][...] + bias if given else 0.0
        for k in range(count):
            block = index_ref[base_ref[0] + first + k]
            for p, at in enumerate((slice(0, pieces[0]), slice(pieces[0], sum(pieces)))):
                total = total + jnp.dot(
                    rows_ref[block, :, at],
                    weights[2 * k + p][: pieces[p]],
                    preferred_element_type=jnp.float32,
                )
        out[...] = total.astype(out.dtype)


def last_image_kernel(image_ref, other_ref, place_ref, partial_ref, send_out):
    sections, cape, _ = send_out.shape
    width = image_ref.shape[1]
    image = image_ref[...] + other_ref[...].astype(jnp.float32)
    send = jnp.dot(place_ref[...], image.astype(jnp.bfloat16), preferred_element_type=jnp.float32)
    send_out[:, :, :width] = send.astype(jnp.bfloat16).reshape(sections, cape, width)
    send_out[:, :, width:] = partial_ref[...]


def finish_kernel(text_ref, image_ref, bias_ref, slot_ref, text_out, send_out):
    text_out[...] = (text_ref[...] + bias_ref[...]).astype(jnp.bfloat16)
    image = (image_ref[...] + bias_ref[...]).astype(jnp.bfloat16)
    place = (iota((send_out.shape[0], image.shape[0]), 0) == slot_ref[...]).astype(jnp.bfloat16)
    send_out[...] = jnp.dot(place, image, preferred_element_type=jnp.float32).astype(jnp.bfloat16)


def place_kernel(
    split, text_ref, *refs
):
    arrived_ref, position_ref, slot_ref, count_ref, rows_ref, blocks_ref = refs[-6:]
    rows, width = rows_ref.shape
    text = text_ref[...].astype(jnp.float32)
    if split:
        text = (text + refs[0][...].astype(jnp.float32)).astype(jnp.bfloat16)
        lead = jnp.zeros((rows - text.shape[0], width), jnp.float32)
        text = jnp.concatenate([lead, text.astype(jnp.float32)], axis=0)
    sections, cape, _ = arrived_ref.shape
    row = iota((rows, sections * cape), 0)
    match = (row == position_ref[...]) & (row < count_ref[0])
    filled = jnp.max(match.astype(jnp.float32), axis=1, keepdims=True) > 0.0
    arrived = arrived_ref[:, :, :width].reshape(sections * cape, width)
    placed = jnp.dot(match.astype(jnp.bfloat16), arrived, preferred_element_type=jnp.float32)
    whole = jnp.where(filled, placed, text).astype(jnp.bfloat16)
    slots = (iota((blocks_ref.shape[0], rows), 0) == slot_ref[...]).astype(jnp.bfloat16)
    blocks_ref[...] = jnp.dot(slots, whole, preferred_element_type=jnp.float32).astype(jnp.bfloat16)
    rows_ref[...] = whole


def decode_kernel(packed, rows_ref, query_ref, partial_ref, length_ref, out_ref):
    rows = rows_ref.shape[0]
    heads = query_ref.shape[1] // HD
    mask = iota((GROUP, rows), 1) < length_ref[0]
    if packed:
        partial = partial_ref[:, : 2 * heads, rows_ref.shape[1] :].astype(jnp.float32)
    for h in range(heads // GROUP):
        at = slice(h * GROUP, (h + 1) * GROUP)
        key = rows_ref[:, 2 * h * HD : (2 * h + 1) * HD]
        value = rows_ref[:, (2 * h + 1) * HD : (2 * h + 2) * HD]
        query = query_group(query_ref, h).astype(jnp.bfloat16)
        top, total, acc = attend(query, key, value, mask)
        if packed:
            old_acc = partial[:, at, :]
            state = partial[:, heads + h * GROUP : heads + (h + 1) * GROUP, :]
            old_top = state[:, :, 0:1] + state[:, :, 1:2] + state[:, :, 2:3]
            old_total = state[:, :, 3:4] + state[:, :, 4:5]
        else:
            old_acc = partial_ref[:, at, :HD]
            old_top = partial_ref[:, at, HD : HD + 1]
            old_total = partial_ref[:, at, HD + 1 : HD + 2]
        best = jnp.maximum(top, jnp.max(old_top, axis=0))
        fresh_factor = jnp.exp(top - best)
        old_factor = jnp.exp(old_top - best[None])
        total = total * fresh_factor + jnp.sum(old_total * old_factor, axis=0)
        acc = acc * fresh_factor + jnp.sum(old_acc * old_factor, axis=0)
        result = (acc / total).astype(jnp.bfloat16)
        for j in range(GROUP):
            lane = (h * GROUP + j) * HD
            out_ref[:, lane : lane + HD] = result[j : j + 1]


def beside(x):
    return lax.ppermute(x, "tensor", [(0, 1), (1, 0)])


def exchange(x):
    return lax.all_to_all(x, "section", split_axis=0, concat_axis=0, tiled=True)


def ring_order(sections):
    return list(range(0, sections, 2)) + list(range(1, sections, 2))[::-1]


def ring_tables(sections, tensors):
    order = ring_order(sections)
    table = np.zeros((sections, tensors, 2 * sections), np.int32)
    distances = [0] + [s * d for d in range(1, sections // 2) for s in (1, -1)] + [sections // 2]
    for at, section in enumerate(order):
        for step, distance in enumerate(distances):
            source = order[(at - distance) % sections]
            for t in range(tensors):
                table[section, t, step] = (source - t * (sections // tensors)) % sections
            table[section, :, sections + step] = source
    return table


def after(values, others):
    return lax.optimization_barrier((tuple(values), tuple(others)))


def ring_path(
    text, image, target, weight, bias, gains, queries, pool, owner, fill, block_owner, half, cape, capr
):
    sections = lax.axis_size("section")
    tensors = lax.axis_size("tensor")
    order = ring_order(sections)
    ahead = [(order[i], order[(i + 1) % sections]) for i in range(sections)]
    back = [(b, a) for a, b in ahead]
    depth, width = weight.shape
    piece = depth // 4
    rows = text.shape[0]
    text_rows = rows - rows // LEAST_IMAGE
    heads = queries.shape[1] // HD
    group = lax.axis_index("groups").astype(jnp.int32).reshape(1)

    def up(x):
        return lax.ppermute(x, "section", ahead)

    def down(x):
        return lax.ppermute(x, "section", back)

    def across(x):
        return lax.ppermute(x, "groups", [(0, 1), (1, 0)])

    index = jnp.asarray(ring_tables(sections, tensors).reshape(-1))
    base = (lax.axis_index("section") * tensors + lax.axis_index("tensor")) * (2 * sections)
    base = base.astype(jnp.int32).reshape(1)

    def dots(first, count, inputs, states, dtype, *added):
        parts = [*added, *(p for pair in slices[first : first + count] for p in pair)]
        shapes = tuple(jax.ShapeDtypeStruct((x.shape[1], width), dtype) for x in inputs)
        return call(
            functools.partial(dots_kernel, first, count, len(added)),
            shapes, index, base, *parts, *inputs, *states,
            smem=(0, 1), cost=cost(1, 1),
            aliases={2 + len(parts) + len(inputs) + k: k for k in range(len(states))},
        )

    def other_rows(first_term, near, far):
        rows = near.shape[0]
        parts = [p for pair in slices for p in pair]
        return pl.pallas_call(
            functools.partial(other_kernel, first_term),
            out_shape=jax.ShapeDtypeStruct((rows, width), jnp.bfloat16),
            in_specs=[pl.BlockSpec(memory_space=pltpu.SMEM)] * 4
            + [pl.BlockSpec(memory_space=pltpu.VMEM)] * (4 + len(parts)),
            out_specs=pl.BlockSpec(memory_space=pltpu.VMEM),
            compiler_params=pltpu.CompilerParams(vmem_limit_bytes=VMEM),
            cost_estimate=cost(1, 1),
        )(group, half, index, base, near, far, factors, gains, *parts)

    spaces = [pltpu.SMEM] * 3 + [pltpu.HBM] * 6
    own_a, own_b, image_slot, block_slot, picked = pl.pallas_call(
        functools.partial(open_kernel, sections, cape, capr, pool.shape[1]),
        out_shape=(
            jax.ShapeDtypeStruct((piece + GROUP + sections, width), jnp.bfloat16),
            jax.ShapeDtypeStruct((depth // 2 - piece, width), jnp.bfloat16),
            jax.ShapeDtypeStruct((1, rows), jnp.int32),
            jax.ShapeDtypeStruct((1, block_owner.shape[1] * pool.shape[1]), jnp.int32),
            jax.ShapeDtypeStruct((rows + text_rows, text.shape[1] // 2), jnp.bfloat16),
        ),
        in_specs=[pl.BlockSpec(memory_space=space) for space in spaces],
        out_specs=[pl.BlockSpec(memory_space=pltpu.VMEM)] * 5,
        scratch_shapes=[
            pltpu.VMEM(target.shape, jnp.int32),
            pltpu.VMEM(block_owner.shape, jnp.int32),
            pltpu.VMEM(queries.shape, jnp.bfloat16),
            pltpu.SemaphoreType.DMA((5 + sections,)),
        ],
        compiler_params=pltpu.CompilerParams(vmem_limit_bytes=VMEM_ALL),
    )(group, base, half, weight, target, block_owner, queries, image, text)
    near_a = [up(own_a), down(own_a)]
    others = across(picked)
    text_far, image_far = beside(text), beside(image)
    (own_b,), (text_far, image_far) = after((own_b,), (text_far, image_far))
    near_b = [up(own_b), down(own_b)]
    last = sections // 2 - 1
    slices = [(own_a, own_b)]
    normed_image, image_factor = own_norm(sections, group, half, image, image_far, gains, rows)
    waiting, late = [image_factor], text_far
    for step in range(1, last + 1):
        near_a, waiting = after(near_a, waiting)
        held_a = near_a
        near_a = [up(near_a[0])] + ([down(near_a[1])] if step < last else [])
        near_b, waiting = after(near_b, [*waiting, late])
        *waiting, late = waiting
        slices += list(zip(held_a, near_b))
        near_b = ([up(near_b[0])] if step < last else []) + [down(near_b[1])]
        if step == 1:
            image_factor = waiting[0]
            normed_text, text_factor = own_norm(
                sections, group, half, text, late, gains, text_rows
            )
            waiting, late = [image_factor, text_factor], image_factor
        elif step == 2:
            factors = call(
                factor_kernel,
                jax.ShapeDtypeStruct((FACTOR_ROWS, rows), jnp.bfloat16),
                *waiting,
            )
            state = dots(0, 2 * step + 1, (normed_text, normed_image), (), jnp.float32)
            waiting, late = [*state], factors
    state = waiting
    (other_image, other_text, factors), last_slice = after(
        (others[:rows], others[rows:], late), (*near_a, *near_b)
    )
    slices.append(last_slice)
    image_far, factors = beside(other_image), across(factors)
    told = [a for a, _ in slices]
    partial, position, place = call(
        functools.partial(ring_pool_kernel, sections, cape),
        (
            jax.ShapeDtypeStruct((sections, 2 * heads, HD), jnp.bfloat16),
            jax.ShapeDtypeStruct((1, sections * cape), jnp.int32),
            jax.ShapeDtypeStruct((sections * cape, rows), jnp.bfloat16),
        ),
        index, base, *told, pool, owner, fill, image_slot,
        smem=(0, 1),
    )
    done = 2 * last - 1
    sums = dots(done, sections - done, (normed_text, normed_image), state, jnp.float32, bias)
    (image_far, factors), sums = after((image_far, factors), sums)
    image_back = across(other_rows(0, other_image, image_far))
    text_back = other_rows(3, other_text, beside(other_text))
    (image_back,), (text_back, partial, place) = after(
        (image_back,), (text_back, partial, place)
    )
    text_back = across(text_back)
    send = call(
        last_image_kernel,
        jax.ShapeDtypeStruct((sections, cape, width + HD), jnp.bfloat16),
        sums[1], image_back, place, partial,
    )
    arrived = exchange(send)
    return (sums[0], text_back), arrived, position, block_slot, arrived


def gather_path(
    text, image, target, weight, bias, gains, queries, pool, owner, fill, block_owner, half, cape, capr
):
    sections = lax.axis_size("section")
    rows, near = text.shape
    width = weight.shape[1]
    heads = queries.shape[1] // HD
    image_slot, block_slot, message = call(
        functools.partial(prep_kernel, sections, cape, capr, pool.shape[1]),
        (
            jax.ShapeDtypeStruct((1, rows), jnp.int32),
            jax.ShapeDtypeStruct((1, block_owner.shape[1] * pool.shape[1]), jnp.int32),
            jax.ShapeDtypeStruct((sections, 2 * heads, LANES), jnp.bfloat16),
        ),
        target, block_owner, queries,
    )
    partial, position = call(
        functools.partial(pool_kernel, cape),
        (
            jax.ShapeDtypeStruct((sections, heads, 2 * HD), jnp.float32),
            jax.ShapeDtypeStruct((1, sections * cape), jnp.int32),
        ),
        exchange(message), pool, owner, fill,
    )
    normed = [normalize(2, half, x, beside(x), gains)[0] for x in (text, image)]
    whole = lax.all_gather(weight, "section", axis=0, tiled=True)
    first = lax.dynamic_slice_in_dim(whole, half[0] * near, near, 0)
    second = lax.dynamic_slice_in_dim(whole, (1 - half[0]) * near, near, 0)
    text_sum, image_sum = (
        jnp.dot(n[0], first, preferred_element_type=jnp.float32)
        + jnp.dot(n[1], second, preferred_element_type=jnp.float32)
        for n in normed
    )
    text_rows, send = call(
        finish_kernel,
        (
            jax.ShapeDtypeStruct((rows, width), jnp.bfloat16),
            jax.ShapeDtypeStruct((sections * cape, width), jnp.bfloat16),
        ),
        text_sum, image_sum, bias, image_slot,
    )
    arrived = exchange(send.reshape(sections, cape, width))
    return (text_rows,), arrived, position, block_slot, exchange(partial)


def shards(
    text_embed,
    image_embed,
    image_count,
    prompt_len,
    embed_target,
    kv_weight,
    kv_bias,
    norm_gain,
    queries,
    old_pool,
    pool_owner,
    pool_fill,
    block_owner,
):
    sections, tensors = lax.axis_size("section"), lax.axis_size("tensor")
    rows = text_embed.shape[0]
    width = kv_weight.shape[1]
    heads = queries.shape[1] // HD
    cape = rows // sections
    block_rows = old_pool.shape[1]
    capr = (block_owner.shape[0] + sections - 1) // sections * block_rows
    ring = (
        sections == 8
        and tensors == 2
        and lax.axis_size("groups") == 2
        and kv_weight.shape[0] == 1024
        and rows == 2 * LANES
        and cape == 2 * heads
    )
    text_rows, arrived, position, block_slot, partial = (ring_path if ring else gather_path)(
        text_embed,
        image_embed,
        embed_target.reshape(1, -1),
        kv_weight,
        kv_bias.reshape(1, -1),
        norm_gain.reshape(1, -1),
        queries,
        old_pool,
        pool_owner.reshape(1, -1),
        pool_fill.reshape(1, -1),
        block_owner.reshape(1, -1),
        lax.axis_index("tensor").astype(jnp.int32).reshape(1),
        cape,
        capr,
    )
    whole_rows, block_data = call(
        functools.partial(place_kernel, ring),
        (
            jax.ShapeDtypeStruct((rows, width), jnp.bfloat16),
            jax.ShapeDtypeStruct((sections * capr, width), jnp.bfloat16),
        ),
        *text_rows,
        arrived,
        position,
        block_slot,
        image_count,
        smem=(len(text_rows) + 3,),
    )
    fresh = exchange(block_data.reshape(sections, capr, width)).reshape(sections * capr, width)
    decoded = call(
        functools.partial(decode_kernel, ring),
        jax.ShapeDtypeStruct((1, heads * HD), jnp.bfloat16),
        whole_rows,
        queries,
        partial,
        prompt_len,
        smem=(3,),
    )
    return decoded, fresh


def solution(mesh):
    return jax.shard_map(
        shards,
        mesh=mesh,
        in_specs=(
            P(("groups", "section"), "tensor"),
            P(("groups", "section"), "tensor"),
            P(("groups", "section")),
            P(("groups", "section")),
            P(("groups", "section")),
            P("section", "tensor"),
            P("tensor"),
            P(),
            P(("groups", "section"), "tensor"),
            P(("groups", "section"), None, "tensor"),
            P(("groups", "section")),
            P(("groups", "section")),
            P(("groups", "section")),
        ),
        out_specs=(P(("groups", "section"), "tensor"), P(("groups", "section"), "tensor")),
        check_vma=False,
    )
```

```python
import functools

import jax
import jax.numpy as jnp
import numpy as np
from jax import lax
from jax.experimental import pallas as pl
from jax.experimental.pallas import tpu as pltpu
from jax.sharding import PartitionSpec as P

HQ = 32
KVH = 4
HD = 128
GROUP = HQ // KVH
SCALE = HD ** (-0.5)
LANES = 128
NEG = -1e30
LEAST_IMAGE = 4
VMEM = 14 * 1024 * 1024
VMEM_ALL = 56 * 1024 * 1024


def iota(shape, dim):
    return lax.broadcasted_iota(jnp.int32, shape, dim)


def call(kernel, outs, *args, cost=None, smem=(), aliases=None, scratch=()):
    return pl.pallas_call(
        kernel,
        out_shape=outs,
        in_specs=[
            pl.BlockSpec(memory_space=pltpu.SMEM if i in smem else pltpu.VMEM)
            for i in range(len(args))
        ],
        out_specs=jax.tree.map(lambda _: pl.BlockSpec(memory_space=pltpu.VMEM), outs),
        input_output_aliases=aliases or {},
        scratch_shapes=scratch,
        compiler_params=pltpu.CompilerParams(vmem_limit_bytes=VMEM),
        cost_estimate=cost,
    )(*args)


def cost(flops, nbytes):
    return pl.CostEstimate(flops=int(flops), bytes_accessed=int(nbytes), transcendentals=0)


def rank_before(hits):
    items = hits.shape[1]
    earlier = (iota((items, items), 0) < iota((items, items), 1)).astype(jnp.bfloat16)
    before = jnp.dot(hits.astype(jnp.bfloat16), earlier, preferred_element_type=jnp.float32)
    return jnp.sum(before * hits, axis=0, keepdims=True).astype(jnp.int32)


def spread(values, items):
    groups = values.shape[1]
    share = items // groups
    same = iota((groups, items), 0) * share
    column = iota((groups, items), 1)
    same = ((column >= same) & (column < same + share)).astype(jnp.bfloat16)
    wide = jnp.broadcast_to(values.astype(jnp.float32), (8, groups)).astype(jnp.bfloat16)
    wide = jnp.dot(wide, same, preferred_element_type=jnp.float32)
    return wide[:1].astype(jnp.int32)


def image_slots(target, sections, cape):
    rows = target.shape[1]
    index = jnp.floor((target.astype(jnp.float32) + 0.5) * (1.0 / rows)).astype(jnp.int32)
    place = target - index * rows
    hits = ((index == iota((sections, rows), 0)) & (target >= 0)).astype(jnp.float32)
    rank = rank_before(hits)
    at_rank = (rank == iota((LANES, rows), 0)).astype(jnp.bfloat16)
    numbered = (hits * (place + 1).astype(jnp.float32)).astype(jnp.bfloat16)
    positions = lax.dot_general(
        numbered, at_rank, (((1,), (1,)), ((), ())), preferred_element_type=jnp.float32
    )
    return jnp.where(target >= 0, index * cape + rank, -1), positions - 1.0


def block_slots(owner, sections, capr, block_rows):
    owner = spread(owner, owner.shape[1] * block_rows)
    hits = ((owner == iota((sections, owner.shape[1]), 0)) & (owner >= 0)).astype(jnp.float32)
    return jnp.where(owner >= 0, owner * capr + rank_before(hits), -1)


def query_group(query_ref, h):
    heads = [
        query_ref[:, j * HD : (j + 1) * HD].astype(jnp.float32)
        for j in range(h * GROUP, (h + 1) * GROUP)
    ]
    return jnp.concatenate(heads, axis=0)


def prep_kernel(
    sections, cape, capr, block_rows, target_ref, owner_ref, query_ref, out_slot, out_block, out_message
):
    out_slot[...], positions = image_slots(target_ref[...], sections, cape)
    heads = query_ref.shape[1] // HD
    query = jnp.concatenate([query_group(query_ref, h) for h in range(heads // GROUP)], axis=0)
    query = query.astype(jnp.bfloat16)
    out_message[:, :heads, :] = jnp.broadcast_to(query[None], (sections,) + query.shape)
    out_message[:, heads:, :] = jnp.broadcast_to(
        positions.astype(jnp.bfloat16)[:, None, :], (sections, out_message.shape[1] - heads, LANES)
    )
    out_block[...] = block_slots(owner_ref[...], sections, capr, block_rows)


def open_kernel(
    sections, cape, capr, block_rows, group_ref, base_ref, half_ref, weight_hbm, target_hbm, owner_hbm, query_hbm,
    image_hbm, text_hbm, out_a, out_b, out_slot, out_block, out_pick, target_ref, owner_ref, query_ref, sems
):
    piece_b = out_b.shape[0]
    piece = out_a.shape[0] - GROUP
    at = pl.multiple_of(group_ref[0] * (piece + piece_b), LANES)
    moves = [
        (target_hbm, target_ref),
        (query_hbm, query_ref),
        (owner_hbm, owner_ref),
        (weight_hbm.at[pl.ds(at, piece)], out_a.at[pl.ds(0, piece)]),
        (weight_hbm.at[pl.ds(at + piece, piece_b)], out_b),
    ]
    width = piece + piece_b
    row = 0
    for kind, source in enumerate((image_hbm, text_hbm)):
        rows = source.shape[0] if kind == 0 else out_pick.shape[0] - row
        first = source.shape[0] - rows
        for j in range(out_pick.shape[1] // width):
            lane = pl.multiple_of((2 * j + 1 - group_ref[0]) * width, LANES)
            moves.append(
                (
                    source.at[pl.ds(first, rows), pl.ds(lane, width)],
                    out_pick.at[pl.ds(row, rows), pl.ds(j * width, width)],
                )
            )
        row += rows
    copies = [
        pltpu.make_async_copy(source, target, sems.at[k])
        for k, (source, target) in enumerate(moves)
    ]
    for copy in copies:
        copy.start()
    copies[0].wait()
    out_slot[...], positions = image_slots(target_ref[...], sections, cape)
    copies[1].wait()
    groups = query_ref.shape[1] // (GROUP * HD)
    told = [query_group(query_ref, h) for h in range(groups)]
    told += [positions, jnp.zeros((GROUP, out_a.shape[1] - groups * HD - LANES), jnp.float32)]
    out_a[piece:] = jnp.concatenate(told, axis=1).astype(jnp.bfloat16)
    copies[2].wait()
    out_block[...] = block_slots(owner_ref[...], sections, capr, block_rows)
    for copy in copies[3:]:
        copy.wait()


FACTOR_ROWS = 16


def factor_kernel(image_ref, text_ref, out_ref):
    terms = [term for ref in (image_ref, text_ref) for term in bf16_terms(ref[...], 3)]
    terms.append(jnp.zeros((out_ref.shape[0] - len(terms), out_ref.shape[1]), jnp.float32))
    out_ref[...] = jnp.concatenate(terms, axis=0).astype(jnp.bfloat16)


def diagonal(size):
    return iota((size, size), 0) == iota((size, size), 1)


def own_norm_kernel(
    slices, group_ref, half_ref, near_hbm, far_hbm, gains_hbm, out_ref, factor_ref, near, far, gain, sems
):
    tiles, tile, features = near.shape
    width = out_ref.shape[2]
    first = near_hbm.shape[0] - tiles * tile
    half, group = half_ref[0], group_ref[0]
    copies = []
    for side in range(2):
        at = pl.multiple_of((half if side == 0 else 1 - half) * features, features)
        copies.append(
            pltpu.make_async_copy(gains_hbm.at[:, pl.ds(at, features)], gain.at[side], sems.at[side])
        )
    for i in range(tiles):
        at = pl.ds(first + i * tile, tile)
        for side, (hbm, vmem) in enumerate(((near_hbm, near), (far_hbm, far))):
            copies.append(
                pltpu.make_async_copy(hbm.at[at], vmem.at[i], sems.at[2 + 2 * i + side])
            )
    for copy in copies:
        copy.start()
    copies[0].wait()
    copies[1].wait()
    factors = []
    for i in range(tiles):
        copies[2 + 2 * i].wait()
        copies[3 + 2 * i].wait()
        total = 0.0
        for ref in (near, far):
            value = ref[i].astype(jnp.float32)
            total = total + jnp.sum(value * value, axis=1, keepdims=True)
        factor = lax.rsqrt(total * (1.0 / (2 * features)) + 1e-06)
        factors.append(jnp.sum(jnp.where(diagonal(tile), factor, 0.0), axis=0, keepdims=True))
        for side, ref in enumerate((near, far)):
            for j in range(slices // 2):
                at = pl.ds(pl.multiple_of((2 * j + group) * width, LANES), width)
                block = ref[i, :, at].astype(jnp.float32) * factor * gain[side, :, at]
                out_ref[side * (slices // 2) + j, pl.ds(i * tile, tile)] = block.astype(jnp.bfloat16)
    missing = factor_ref.shape[1] - tiles * tile
    if missing:
        factors.append(jnp.zeros((1, missing), jnp.float32))
    factor_ref[...] = jnp.concatenate(factors, axis=1)


def own_norm(slices, group, half, near, far, gains, rows):
    features = near.shape[1]
    tile = NORM_TILE
    held = pltpu.VMEM((rows // tile, tile, features), jnp.bfloat16)
    return pl.pallas_call(
        functools.partial(own_norm_kernel, slices),
        out_shape=(
            jax.ShapeDtypeStruct((slices, rows, features // slices), jnp.bfloat16),
            jax.ShapeDtypeStruct((1, near.shape[0]), jnp.float32),
        ),
        in_specs=[pl.BlockSpec(memory_space=pltpu.SMEM)] * 2
        + [pl.BlockSpec(memory_space=pltpu.HBM)] * 3,
        out_specs=[pl.BlockSpec(memory_space=pltpu.VMEM)] * 2,
        scratch_shapes=[
            held,
            held,
            pltpu.VMEM((2, 1, features), jnp.float32),
            pltpu.SemaphoreType.DMA((2 + 2 * (rows // tile),)),
        ],
        compiler_params=pltpu.CompilerParams(vmem_limit_bytes=VMEM),
        cost_estimate=cost(1.2e10, 1),
    )(group, half, near, far, gains)


def other_kernel(
    first_term, group_ref, half_ref, index_ref, base_ref, near_ref, far_ref, factor_ref, gains_ref, *refs
):
    *weights, out_ref = refs
    slices, rows = len(weights) // 2, out_ref.shape[0]
    half, width = slices // 2, near_ref.shape[1] // (slices // 2)
    terms = factor_ref[...].astype(jnp.float32)
    factor = terms[first_term : first_term + 1]
    for k in range(1, 3):
        factor = factor + terms[first_term + k : first_term + k + 1]
    factor = jnp.sum(jnp.where(diagonal(rows), factor[:, :rows], 0.0), axis=1, keepdims=True)
    total = 0.0
    for k in range(slices):
        block = index_ref[base_ref[0] + k]
        far = (block >= half).astype(jnp.int32)
        side = half_ref[0] + far - 2 * far * half_ref[0]
        lane = (2 * (side * half + block - far * half) + group_ref[0]) * width
        at = pl.ds(pl.multiple_of((block - far * half) * width, LANES), width)
        value = jnp.where(far > 0, far_ref[:, at], near_ref[:, at]).astype(jnp.float32) * factor
        value = value * gains_ref[:, pl.ds(pl.multiple_of(lane, LANES), width)]
        value = value.astype(jnp.bfloat16)
        at = 0
        for weight in weights[2 * k : 2 * k + 2]:
            depth = weight.shape[0] // LANES * LANES
            total = total + jnp.dot(
                value[:, at : at + depth], weight[:depth], preferred_element_type=jnp.float32
            )
            at += depth
    out_ref[...] = total.astype(jnp.bfloat16)


NORM_TILE = 64


def norm_kernel(blocks, half_ref, near_hbm, far_hbm, gains_hbm, out_ref, done_ref, near, far, gain, sems):
    tiles, tile, features = near.shape
    width = out_ref.shape[2]
    half = half_ref[0]
    copies = []
    for side in range(2):
        at = pl.multiple_of((half if side == 0 else 1 - half) * features, features)
        copies.append(
            pltpu.make_async_copy(gains_hbm.at[:, pl.ds(at, features)], gain.at[side], sems.at[side])
        )
    for i in range(tiles):
        at = pl.ds(i * tile, tile)
        for side, (hbm, vmem) in enumerate(((near_hbm, near), (far_hbm, far))):
            copies.append(
                pltpu.make_async_copy(hbm.at[at], vmem.at[i], sems.at[2 + 2 * i + side])
            )
    for copy in copies:
        copy.start()
    done_ref[...] = jnp.zeros_like(done_ref)
    copies[0].wait()
    copies[1].wait()
    for i in range(tiles):
        copies[2 + 2 * i].wait()
        copies[3 + 2 * i].wait()
        total = 0.0
        for ref in (near, far):
            value = ref[i].astype(jnp.float32)
            total = total + jnp.sum(value * value, axis=1, keepdims=True)
        factor = lax.rsqrt(total * (1.0 / (2 * features)) + 1e-06)
        for side, ref in enumerate((near, far)):
            for j in range(blocks // 2):
                at = pl.ds(j * width, width)
                block = ref[i, :, at].astype(jnp.float32) * factor * gain[side, :, at]
                out_ref[side * (blocks // 2) + j, pl.ds(i * tile, tile)] = block.astype(jnp.bfloat16)


def normalize(blocks, half, near, far, gains):
    rows, features = near.shape
    tile = min(NORM_TILE, rows)
    held = pltpu.VMEM((rows // tile, tile, features), jnp.bfloat16)
    return pl.pallas_call(
        functools.partial(norm_kernel, blocks),
        out_shape=(
            jax.ShapeDtypeStruct((blocks, rows, 2 * features // blocks), jnp.bfloat16),
            jax.ShapeDtypeStruct((8, LANES), jnp.float32),
        ),
        in_specs=[pl.BlockSpec(memory_space=pltpu.SMEM)]
        + [pl.BlockSpec(memory_space=pltpu.HBM)] * 3,
        out_specs=[pl.BlockSpec(memory_space=pltpu.VMEM)] * 2,
        scratch_shapes=[
            held,
            held,
            pltpu.VMEM((2, 1, features), jnp.float32),
            pltpu.SemaphoreType.DMA((2 + 2 * (rows // tile),)),
        ],
        compiler_params=pltpu.CompilerParams(vmem_limit_bytes=VMEM),
        cost_estimate=cost(1, 1),
    )(half, near, far, gains)


def pool_rows(pool_ref):
    block_rows = pool_ref.shape[1]
    pool = pool_ref[...].astype(jnp.float32)
    return jnp.concatenate([pool[:, i, :] for i in range(block_rows)], axis=0).astype(jnp.bfloat16)


def positions_in_slots(sent, source, cape):
    sources = sent.shape[0]
    slots = sources * cape
    column = iota((sources, slots), 1)
    rank = column - jnp.floor((column.astype(jnp.float32) + 0.5) * (1.0 / cape)).astype(jnp.int32) * cape
    at_source = (column >= source * cape) & (column < source * cape + cape)
    at_rank = (iota((LANES, slots), 0) == rank[:1]).astype(jnp.bfloat16)
    wide = jnp.dot(sent.astype(jnp.bfloat16), at_rank, preferred_element_type=jnp.float32)
    return jnp.sum(jnp.where(at_source, wide, 0.0), axis=0, keepdims=True).astype(jnp.int32)


def pool_kernel(cape, message_ref, pool_ref, owner_ref, fill_ref, out_ref, position_ref):
    sections, heads = out_ref.shape[0], out_ref.shape[1]
    held, block_rows, _ = pool_ref.shape
    request = iota((sections * GROUP, held), 0)
    owner = owner_ref[...]
    owned = (request >= owner * GROUP) & (request < owner * GROUP + GROUP)
    mask = jnp.concatenate(
        [(owned & (fill_ref[...] > i)).astype(jnp.float32) for i in range(block_rows)], axis=1
    )
    pool = pool_rows(pool_ref)
    for h in range(heads // GROUP):
        query = message_ref[:, h * GROUP : (h + 1) * GROUP, :].astype(jnp.float32)
        query = query.reshape(sections * GROUP, HD).astype(jnp.bfloat16)
        key = pool[:, 2 * h * HD : (2 * h + 1) * HD]
        value = pool[:, (2 * h + 1) * HD : (2 * h + 2) * HD]
        top, total, acc = attend(query, key, value, mask > 0.0)
        lane = iota((sections * GROUP, LANES), 1)
        state = jnp.where(lane == 0, top, jnp.where(lane == 1, total, 0.0))
        out_ref[:, h * GROUP : (h + 1) * GROUP, :HD] = acc.reshape(sections, GROUP, HD)
        out_ref[:, h * GROUP : (h + 1) * GROUP, HD:] = state.reshape(sections, GROUP, LANES)
    sent = message_ref[:, heads : heads + 1, :].astype(jnp.float32).reshape(sections, LANES)
    position_ref[...] = positions_in_slots(sent, iota((sections, 1), 0), cape)


def ring_pool_kernel(sections, cape, index_ref, base_ref, *refs):
    told_refs = refs[:sections]
    pool_ref, owner_ref, fill_ref, slot_ref, out_ref, position_ref, place_ref = refs[sections:]
    place_ref[...] = (iota(place_ref.shape, 0) == slot_ref[...]).astype(jnp.bfloat16)
    sources = [index_ref[base_ref[0] + sections + j] for j in range(sections)]
    held, block_rows, _ = pool_ref.shape
    heads = out_ref.shape[1] // 2
    groups = heads // GROUP
    told = [ref[ref.shape[0] - GROUP :, :].astype(jnp.float32) for ref in told_refs]
    owner, fill = owner_ref[...], fill_ref[...]
    masks = []
    for j in range(sections):
        owned = owner == sources[j]
        mask = [(owned & (fill > i)).astype(jnp.float32) for i in range(block_rows)]
        masks.append(jnp.broadcast_to(jnp.concatenate(mask, axis=1), (GROUP, held * block_rows)))
    mask = jnp.concatenate(masks, axis=0) > 0.0
    pool = pool_rows(pool_ref)
    sums, states = [], []
    lane = iota((sections * GROUP, LANES), 1)
    for h in range(groups):
        query = jnp.concatenate([t[:GROUP, h * HD : (h + 1) * HD] for t in told], axis=0)
        key = pool[:, 2 * h * HD : (2 * h + 1) * HD]
        value = pool[:, (2 * h + 1) * HD : (2 * h + 2) * HD]
        top, total, acc = attend(query.astype(jnp.bfloat16), key, value, mask)
        terms = bf16_terms(top, 3) + bf16_terms(total, 2)
        state = jnp.zeros((sections * GROUP, LANES), jnp.float32)
        for k, term in enumerate(terms):
            state = jnp.where(lane == k, term, state)
        sums.append(acc)
        states.append(state)
    for j in range(sections):
        at = slice(j * GROUP, (j + 1) * GROUP)
        rows = jnp.concatenate([x[at] for x in sums] + [x[at] for x in states], axis=0)
        out_ref[sources[j]] = rows.astype(jnp.bfloat16)
    own = iota((sections, LANES), 0) == sources[0]
    sent = jnp.concatenate(
        [
            jnp.sum(jnp.where(own, t[:, groups * HD : groups * HD + LANES], 0.0), axis=0, keepdims=True)
            for t in told
        ],
        axis=0,
    )
    source = jnp.zeros((sections, 1), jnp.int32)
    for j in range(sections):
        source = jnp.where(iota((sections, 1), 0) == j, sources[j], source)
    position_ref[...] = positions_in_slots(sent, source, cape)


def bf16_terms(value, count):
    terms = []
    for _ in range(count):
        term = value.astype(jnp.bfloat16).astype(jnp.float32)
        terms.append(term)
        value = value - term
    return terms


def attend(query, key, value, mask):
    scores = (
        lax.dot_general(query, key, (((1,), (1,)), ((), ())), preferred_element_type=jnp.float32)
        * SCALE
    )
    scores = jnp.where(mask, scores, NEG)
    top = jnp.max(scores, axis=1, keepdims=True)
    expo = jnp.where(mask, jnp.exp(scores - top), 0.0)
    total = jnp.sum(expo, axis=1, keepdims=True)
    acc = jnp.dot(expo.astype(jnp.bfloat16), value, preferred_element_type=jnp.float32)
    return top, total, acc


def dots_kernel(first, count, biased, index_ref, base_ref, *refs):
    bias = 0.0
    if biased:
        bias, refs = refs[0][...], refs[1:]
    weights, refs = refs[: 2 * count], refs[2 * count :]
    kinds = len(refs) // 3 if len(refs) % 3 == 0 else len(refs) // 2
    rows_refs, given, outs = refs[:kinds], refs[kinds:-kinds], refs[-kinds:]
    pieces = (rows_refs[0].shape[2] - weights[1].shape[0], weights[1].shape[0])
    for kind, (rows_ref, out) in enumerate(zip(rows_refs, outs)):
        total = given[kind][...] + bias if given else 0.0
        for k in range(count):
            block = index_ref[base_ref[0] + first + k]
            for p, at in enumerate((slice(0, pieces[0]), slice(pieces[0], sum(pieces)))):
                total = total + jnp.dot(
                    rows_ref[block, :, at],
                    weights[2 * k + p][: pieces[p]],
                    preferred_element_type=jnp.float32,
                )
        out[...] = total.astype(out.dtype)


def last_image_kernel(image_ref, other_ref, place_ref, partial_ref, send_out):
    sections, cape, _ = send_out.shape
    width = image_ref.shape[1]
    image = image_ref[...] + other_ref[...].astype(jnp.float32)
    send = jnp.dot(place_ref[...], image.astype(jnp.bfloat16), preferred_element_type=jnp.float32)
    send_out[:, :, :width] = send.astype(jnp.bfloat16).reshape(sections, cape, width)
    send_out[:, :, width:] = partial_ref[...]


def finish_kernel(text_ref, image_ref, bias_ref, slot_ref, text_out, send_out):
    text_out[...] = (text_ref[...] + bias_ref[...]).astype(jnp.bfloat16)
    image = (image_ref[...] + bias_ref[...]).astype(jnp.bfloat16)
    place = (iota((send_out.shape[0], image.shape[0]), 0) == slot_ref[...]).astype(jnp.bfloat16)
    send_out[...] = jnp.dot(place, image, preferred_element_type=jnp.float32).astype(jnp.bfloat16)


def place_kernel(
    split, text_ref, *refs
):
    arrived_ref, position_ref, slot_ref, count_ref, rows_ref, blocks_ref = refs[-6:]
    rows, width = rows_ref.shape
    text = text_ref[...].astype(jnp.float32)
    if split:
        text = (text + refs[0][...].astype(jnp.float32)).astype(jnp.bfloat16)
        lead = jnp.zeros((rows - text.shape[0], width), jnp.float32)
        text = jnp.concatenate([lead, text.astype(jnp.float32)], axis=0)
    sections, cape, _ = arrived_ref.shape
    row = iota((rows, sections * cape), 0)
    match = (row == position_ref[...]) & (row < count_ref[0])
    filled = jnp.max(match.astype(jnp.float32), axis=1, keepdims=True) > 0.0
    arrived = arrived_ref[:, :, :width].reshape(sections * cape, width)
    placed = jnp.dot(match.astype(jnp.bfloat16), arrived, preferred_element_type=jnp.float32)
    whole = jnp.where(filled, placed, text).astype(jnp.bfloat16)
    slots = (iota((blocks_ref.shape[0], rows), 0) == slot_ref[...]).astype(jnp.bfloat16)
    blocks_ref[...] = jnp.dot(slots, whole, preferred_element_type=jnp.float32).astype(jnp.bfloat16)
    rows_ref[...] = whole


def decode_kernel(packed, rows_ref, query_ref, partial_ref, length_ref, out_ref):
    rows = rows_ref.shape[0]
    heads = query_ref.shape[1] // HD
    mask = iota((GROUP, rows), 1) < length_ref[0]
    if packed:
        partial = partial_ref[:, : 2 * heads, rows_ref.shape[1] :].astype(jnp.float32)
    for h in range(heads // GROUP):
        at = slice(h * GROUP, (h + 1) * GROUP)
        key = rows_ref[:, 2 * h * HD : (2 * h + 1) * HD]
        value = rows_ref[:, (2 * h + 1) * HD : (2 * h + 2) * HD]
        query = query_group(query_ref, h).astype(jnp.bfloat16)
        top, total, acc = attend(query, key, value, mask)
        if packed:
            old_acc = partial[:, at, :]
            state = partial[:, heads + h * GROUP : heads + (h + 1) * GROUP, :]
            old_top = state[:, :, 0:1] + state[:, :, 1:2] + state[:, :, 2:3]
            old_total = state[:, :, 3:4] + state[:, :, 4:5]
        else:
            old_acc = partial_ref[:, at, :HD]
            old_top = partial_ref[:, at, HD : HD + 1]
            old_total = partial_ref[:, at, HD + 1 : HD + 2]
        best = jnp.maximum(top, jnp.max(old_top, axis=0))
        fresh_factor = jnp.exp(top - best)
        old_factor = jnp.exp(old_top - best[None])
        total = total * fresh_factor + jnp.sum(old_total * old_factor, axis=0)
        acc = acc * fresh_factor + jnp.sum(old_acc * old_factor, axis=0)
        result = (acc / total).astype(jnp.bfloat16)
        for j in range(GROUP):
            lane = (h * GROUP + j) * HD
            out_ref[:, lane : lane + HD] = result[j : j + 1]


def beside(x):
    return lax.ppermute(x, "tensor", [(0, 1), (1, 0)])


def exchange(x):
    return lax.all_to_all(x, "section", split_axis=0, concat_axis=0, tiled=True)


def ring_order(sections):
    return list(range(0, sections, 2)) + list(range(1, sections, 2))[::-1]


def ring_tables(sections, tensors):
    order = ring_order(sections)
    table = np.zeros((sections, tensors, 2 * sections), np.int32)
    distances = [0] + [s * d for d in range(1, sections // 2) for s in (1, -1)] + [sections // 2]
    for at, section in enumerate(order):
        for step, distance in enumerate(distances):
            source = order[(at - distance) % sections]
            for t in range(tensors):
                table[section, t, step] = (source - t * (sections // tensors)) % sections
            table[section, :, sections + step] = source
    return table


def after(values, others):
    return lax.optimization_barrier((tuple(values), tuple(others)))


def ring_path(
    text, image, target, weight, bias, gains, queries, pool, owner, fill, block_owner, half, cape, capr
):
    sections = lax.axis_size("section")
    tensors = lax.axis_size("tensor")
    order = ring_order(sections)
    ahead = [(order[i], order[(i + 1) % sections]) for i in range(sections)]
    back = [(b, a) for a, b in ahead]
    depth, width = weight.shape
    piece = depth // 4
    rows = text.shape[0]
    text_rows = rows - rows // LEAST_IMAGE
    heads = queries.shape[1] // HD
    group = lax.axis_index("groups").astype(jnp.int32).reshape(1)

    def up(x):
        return lax.ppermute(x, "section", ahead)

    def down(x):
        return lax.ppermute(x, "section", back)

    def across(x):
        return lax.ppermute(x, "groups", [(0, 1), (1, 0)])

    index = jnp.asarray(ring_tables(sections, tensors).reshape(-1))
    base = (lax.axis_index("section") * tensors + lax.axis_index("tensor")) * (2 * sections)
    base = base.astype(jnp.int32).reshape(1)

    def dots(first, count, inputs, states, dtype, *added):
        parts = [*added, *(p for pair in slices[first : first + count] for p in pair)]
        shapes = tuple(jax.ShapeDtypeStruct((x.shape[1], width), dtype) for x in inputs)
        return call(
            functools.partial(dots_kernel, first, count, len(added)),
            shapes, index, base, *parts, *inputs, *states,
            smem=(0, 1), cost=cost(1.2e10 if count == 5 else 1, 1),
            aliases={2 + len(parts) + len(inputs) + k: k for k in range(len(states))},
        )

    def other_rows(first_term, near, far):
        rows = near.shape[0]
        parts = [p for pair in slices for p in pair]
        return pl.pallas_call(
            functools.partial(other_kernel, first_term),
            out_shape=jax.ShapeDtypeStruct((rows, width), jnp.bfloat16),
            in_specs=[pl.BlockSpec(memory_space=pltpu.SMEM)] * 4
            + [pl.BlockSpec(memory_space=pltpu.VMEM)] * (4 + len(parts)),
            out_specs=pl.BlockSpec(memory_space=pltpu.VMEM),
            compiler_params=pltpu.CompilerParams(vmem_limit_bytes=VMEM),
            cost_estimate=cost(1, 1),
        )(group, half, index, base, near, far, factors, gains, *parts)

    spaces = [pltpu.SMEM] * 3 + [pltpu.HBM] * 6
    own_a, own_b, image_slot, block_slot, picked = pl.pallas_call(
        functools.partial(open_kernel, sections, cape, capr, pool.shape[1]),
        out_shape=(
            jax.ShapeDtypeStruct((piece + GROUP, width), jnp.bfloat16),
            jax.ShapeDtypeStruct((depth // 2 - piece, width), jnp.bfloat16),
            jax.ShapeDtypeStruct((1, rows), jnp.int32),
            jax.ShapeDtypeStruct((1, block_owner.shape[1] * pool.shape[1]), jnp.int32),
            jax.ShapeDtypeStruct((rows + text_rows, text.shape[1] // 2), jnp.bfloat16),
        ),
        in_specs=[pl.BlockSpec(memory_space=space) for space in spaces],
        out_specs=[pl.BlockSpec(memory_space=pltpu.VMEM)] * 5,
        scratch_shapes=[
            pltpu.VMEM(target.shape, jnp.int32),
            pltpu.VMEM(block_owner.shape, jnp.int32),
            pltpu.VMEM(queries.shape, jnp.bfloat16),
            pltpu.SemaphoreType.DMA((5 + sections,)),
        ],
        compiler_params=pltpu.CompilerParams(vmem_limit_bytes=VMEM_ALL),
    )(group, base, half, weight, target, block_owner, queries, image, text)
    near_a = [up(own_a), down(own_a)]
    others = across(picked)
    text_far, image_far = beside(text), beside(image)
    (own_b,), (text_far, image_far) = after((own_b,), (text_far, image_far))
    near_b = [up(own_b), down(own_b)]
    last = sections // 2 - 1
    slices = [(own_a, own_b)]
    normed_image, image_factor = own_norm(sections, group, half, image, image_far, gains, rows)
    waiting, late = [image_factor], text_far
    for step in range(1, last + 1):
        near_a, waiting = after(near_a, waiting)
        held_a = near_a
        near_a = [up(near_a[0])] + ([down(near_a[1])] if step < last else [])
        near_b, waiting = after(near_b, [*waiting, late])
        *waiting, late = waiting
        slices += list(zip(held_a, near_b))
        near_b = ([up(near_b[0])] if step < last else []) + [down(near_b[1])]
        if step == 1:
            image_factor = waiting[0]
            normed_text, text_factor = own_norm(
                sections, group, half, text, late, gains, text_rows
            )
            waiting, late = [image_factor, text_factor], image_factor
        elif step == 2:
            factors = call(
                factor_kernel,
                jax.ShapeDtypeStruct((FACTOR_ROWS, rows), jnp.bfloat16),
                *waiting,
            )
            state = dots(0, 2 * step + 1, (normed_text, normed_image), (), jnp.float32)
            waiting, late = [*state], factors
    state = waiting
    (other_image, other_text, factors), last_slice = after(
        (others[:rows], others[rows:], late), (*near_a, *near_b)
    )
    slices.append(last_slice)
    image_far, factors = beside(other_image), across(factors)
    told = [a for a, _ in slices]
    partial, position, place = call(
        functools.partial(ring_pool_kernel, sections, cape),
        (
            jax.ShapeDtypeStruct((sections, 2 * heads, HD), jnp.bfloat16),
            jax.ShapeDtypeStruct((1, sections * cape), jnp.int32),
            jax.ShapeDtypeStruct((sections * cape, rows), jnp.bfloat16),
        ),
        index, base, *told, pool, owner, fill, image_slot,
        smem=(0, 1),
    )
    done = 2 * last - 1
    sums = dots(done, sections - done, (normed_text, normed_image), state, jnp.float32, bias)
    (image_far, factors), sums = after((image_far, factors), sums)
    image_back = across(other_rows(0, other_image, image_far))
    text_back = other_rows(3, other_text, beside(other_text))
    (image_back,), (text_back, partial, place) = after(
        (image_back,), (text_back, partial, place)
    )
    text_back = across(text_back)
    send = call(
        last_image_kernel,
        jax.ShapeDtypeStruct((sections, cape, width + HD), jnp.bfloat16),
        sums[1], image_back, place, partial,
    )
    arrived = exchange(send)
    return (sums[0], text_back), arrived, position, block_slot, arrived


def gather_path(
    text, image, target, weight, bias, gains, queries, pool, owner, fill, block_owner, half, cape, capr
):
    sections = lax.axis_size("section")
    rows, near = text.shape
    width = weight.shape[1]
    heads = queries.shape[1] // HD
    image_slot, block_slot, message = call(
        functools.partial(prep_kernel, sections, cape, capr, pool.shape[1]),
        (
            jax.ShapeDtypeStruct((1, rows), jnp.int32),
            jax.ShapeDtypeStruct((1, block_owner.shape[1] * pool.shape[1]), jnp.int32),
            jax.ShapeDtypeStruct((sections, 2 * heads, LANES), jnp.bfloat16),
        ),
        target, block_owner, queries,
    )
    partial, position = call(
        functools.partial(pool_kernel, cape),
        (
            jax.ShapeDtypeStruct((sections, heads, 2 * HD), jnp.float32),
            jax.ShapeDtypeStruct((1, sections * cape), jnp.int32),
        ),
        exchange(message), pool, owner, fill,
    )
    normed = [normalize(2, half, x, beside(x), gains)[0] for x in (text, image)]
    whole = lax.all_gather(weight, "section", axis=0, tiled=True)
    first = lax.dynamic_slice_in_dim(whole, half[0] * near, near, 0)
    second = lax.dynamic_slice_in_dim(whole, (1 - half[0]) * near, near, 0)
    text_sum, image_sum = (
        jnp.dot(n[0], first, preferred_element_type=jnp.float32)
        + jnp.dot(n[1], second, preferred_element_type=jnp.float32)
        for n in normed
    )
    text_rows, send = call(
        finish_kernel,
        (
            jax.ShapeDtypeStruct((rows, width), jnp.bfloat16),
            jax.ShapeDtypeStruct((sections * cape, width), jnp.bfloat16),
        ),
        text_sum, image_sum, bias, image_slot,
    )
    arrived = exchange(send.reshape(sections, cape, width))
    return (text_rows,), arrived, position, block_slot, exchange(partial)


def shards(
    text_embed,
    image_embed,
    image_count,
    prompt_len,
    embed_target,
    kv_weight,
    kv_bias,
    norm_gain,
    queries,
    old_pool,
    pool_owner,
    pool_fill,
    block_owner,
):
    sections, tensors = lax.axis_size("section"), lax.axis_size("tensor")
    rows = text_embed.shape[0]
    width = kv_weight.shape[1]
    heads = queries.shape[1] // HD
    cape = rows // sections
    block_rows = old_pool.shape[1]
    capr = (block_owner.shape[0] + sections - 1) // sections * block_rows
    ring = (
        sections == GROUP
        and tensors == 2
        and lax.axis_size("groups") == 2
        and kv_weight.shape[0] == 1024
        and rows == 2 * LANES
        and cape == 2 * heads
    )
    text_rows, arrived, position, block_slot, partial = (ring_path if ring else gather_path)(
        text_embed,
        image_embed,
        embed_target.reshape(1, -1),
        kv_weight,
        kv_bias.reshape(1, -1),
        norm_gain.reshape(1, -1),
        queries,
        old_pool,
        pool_owner.reshape(1, -1),
        pool_fill.reshape(1, -1),
        block_owner.reshape(1, -1),
        lax.axis_index("tensor").astype(jnp.int32).reshape(1),
        cape,
        capr,
    )
    whole_rows, block_data = call(
        functools.partial(place_kernel, ring),
        (
            jax.ShapeDtypeStruct((rows, width), jnp.bfloat16),
            jax.ShapeDtypeStruct((sections * capr, width), jnp.bfloat16),
        ),
        *text_rows,
        arrived,
        position,
        block_slot,
        image_count,
        smem=(len(text_rows) + 3,),
    )
    fresh = exchange(block_data.reshape(sections, capr, width)).reshape(sections * capr, width)
    decoded = call(
        functools.partial(decode_kernel, ring),
        jax.ShapeDtypeStruct((1, heads * HD), jnp.bfloat16),
        whole_rows,
        queries,
        partial,
        prompt_len,
        smem=(3,),
    )
    return decoded, fresh


def solution(mesh):
    return jax.shard_map(
        shards,
        mesh=mesh,
        in_specs=(
            P(("groups", "section"), "tensor"),
            P(("groups", "section"), "tensor"),
            P(("groups", "section")),
            P(("groups", "section")),
            P(("groups", "section")),
            P("section", "tensor"),
            P("tensor"),
            P(),
            P(("groups", "section"), "tensor"),
            P(("groups", "section"), None, "tensor"),
            P(("groups", "section")),
            P(("groups", "section")),
            P(("groups", "section")),
        ),
        out_specs=(P(("groups", "section"), "tensor"), P(("groups", "section"), "tensor")),
        check_vma=False,
    )
```

```python
import functools

import jax
import jax.numpy as jnp
import numpy as np
from jax import lax
from jax.experimental import pallas as pl
from jax.experimental.pallas import tpu as pltpu
from jax.sharding import PartitionSpec as P

HQ = 32
KVH = 4
HD = 128
GROUP = HQ // KVH
SCALE = HD ** (-0.5)
LANES = 128
NEG = -1e30
LEAST_IMAGE = 4
VMEM = 14 * 1024 * 1024
VMEM_ALL = 56 * 1024 * 1024


def iota(shape, dim):
    return lax.broadcasted_iota(jnp.int32, shape, dim)


def call(kernel, outs, *args, cost=None, smem=(), aliases=None, scratch=()):
    return pl.pallas_call(
        kernel,
        out_shape=outs,
        in_specs=[
            pl.BlockSpec(memory_space=pltpu.SMEM if i in smem else pltpu.VMEM)
            for i in range(len(args))
        ],
        out_specs=jax.tree.map(lambda _: pl.BlockSpec(memory_space=pltpu.VMEM), outs),
        input_output_aliases=aliases or {},
        scratch_shapes=scratch,
        compiler_params=pltpu.CompilerParams(vmem_limit_bytes=VMEM),
        cost_estimate=cost,
    )(*args)


def cost(flops, nbytes):
    return pl.CostEstimate(flops=int(flops), bytes_accessed=int(nbytes), transcendentals=0)


def rank_before(hits):
    items = hits.shape[1]
    earlier = (iota((items, items), 0) < iota((items, items), 1)).astype(jnp.bfloat16)
    before = jnp.dot(hits.astype(jnp.bfloat16), earlier, preferred_element_type=jnp.float32)
    return jnp.sum(before * hits, axis=0, keepdims=True).astype(jnp.int32)


def spread(values, items):
    groups = values.shape[1]
    share = items // groups
    same = iota((groups, items), 0) * share
    column = iota((groups, items), 1)
    same = ((column >= same) & (column < same + share)).astype(jnp.bfloat16)
    wide = jnp.broadcast_to(values.astype(jnp.float32), (8, groups)).astype(jnp.bfloat16)
    wide = jnp.dot(wide, same, preferred_element_type=jnp.float32)
    return wide[:1].astype(jnp.int32)


def image_slots(target, sections, cape):
    rows = target.shape[1]
    index = jnp.floor((target.astype(jnp.float32) + 0.5) * (1.0 / rows)).astype(jnp.int32)
    place = target - index * rows
    hits = ((index == iota((sections, rows), 0)) & (target >= 0)).astype(jnp.float32)
    rank = rank_before(hits)
    at_rank = (rank == iota((LANES, rows), 0)).astype(jnp.bfloat16)
    numbered = (hits * (place + 1).astype(jnp.float32)).astype(jnp.bfloat16)
    positions = lax.dot_general(
        numbered, at_rank, (((1,), (1,)), ((), ())), preferred_element_type=jnp.float32
    )
    return jnp.where(target >= 0, index * cape + rank, -1), positions - 1.0


def block_slots(owner, sections, capr, block_rows):
    owner = spread(owner, owner.shape[1] * block_rows)
    hits = ((owner == iota((sections, owner.shape[1]), 0)) & (owner >= 0)).astype(jnp.float32)
    return jnp.where(owner >= 0, owner * capr + rank_before(hits), -1)


def query_group(query_ref, h):
    heads = [
        query_ref[:, j * HD : (j + 1) * HD].astype(jnp.float32)
        for j in range(h * GROUP, (h + 1) * GROUP)
    ]
    return jnp.concatenate(heads, axis=0)


def prep_kernel(
    sections, cape, capr, block_rows, target_ref, owner_ref, query_ref, out_slot, out_block, out_message
):
    out_slot[...], positions = image_slots(target_ref[...], sections, cape)
    heads = query_ref.shape[1] // HD
    query = jnp.concatenate([query_group(query_ref, h) for h in range(heads // GROUP)], axis=0)
    query = query.astype(jnp.bfloat16)
    out_message[:, :heads, :] = jnp.broadcast_to(query[None], (sections,) + query.shape)
    out_message[:, heads:, :] = jnp.broadcast_to(
        positions.astype(jnp.bfloat16)[:, None, :], (sections, out_message.shape[1] - heads, LANES)
    )
    out_block[...] = block_slots(owner_ref[...], sections, capr, block_rows)


def open_kernel(
    sections, cape, capr, block_rows, group_ref, base_ref, half_ref, weight_hbm, target_hbm, owner_hbm, query_hbm,
    image_hbm, text_hbm, out_a, out_b, out_slot, out_block, out_pick, target_ref, owner_ref, query_ref, sems
):
    piece_b = out_b.shape[0]
    piece = out_a.shape[0] - GROUP - sections
    at = pl.multiple_of(group_ref[0] * (piece + piece_b), LANES)
    moves = [
        (target_hbm, target_ref),
        (query_hbm, query_ref),
        (owner_hbm, owner_ref),
        (weight_hbm.at[pl.ds(at, piece)], out_a.at[pl.ds(0, piece)]),
        (weight_hbm.at[pl.ds(at + piece, piece_b)], out_b),
    ]
    width = piece + piece_b
    row = 0
    for kind, source in enumerate((image_hbm, text_hbm)):
        rows = source.shape[0] if kind == 0 else out_pick.shape[0] - row
        first = source.shape[0] - rows
        for j in range(out_pick.shape[1] // width):
            lane = pl.multiple_of((2 * j + 1 - group_ref[0]) * width, LANES)
            moves.append(
                (
                    source.at[pl.ds(first, rows), pl.ds(lane, width)],
                    out_pick.at[pl.ds(row, rows), pl.ds(j * width, width)],
                )
            )
        row += rows
    copies = [
        pltpu.make_async_copy(source, target, sems.at[k])
        for k, (source, target) in enumerate(moves)
    ]
    for copy in copies:
        copy.start()
    copies[0].wait()
    out_slot[...], positions = image_slots(target_ref[...], sections, cape)
    copies[1].wait()
    groups = query_ref.shape[1] // (GROUP * HD)
    told = [query_group(query_ref, h) for h in range(groups)]
    told.append(jnp.zeros((GROUP, out_a.shape[1] - groups * HD), jnp.float32))
    told = jnp.concatenate(told, axis=1)
    positions = jnp.concatenate(
        [positions, jnp.zeros((sections, out_a.shape[1] - LANES), jnp.float32)], axis=1
    )
    out_a[piece:] = jnp.concatenate([told, positions], axis=0).astype(jnp.bfloat16)
    copies[2].wait()
    out_block[...] = block_slots(owner_ref[...], sections, capr, block_rows)
    for copy in copies[3:]:
        copy.wait()


FACTOR_ROWS = 16


def factor_kernel(image_ref, text_ref, out_ref):
    terms = [term for ref in (image_ref, text_ref) for term in bf16_terms(ref[...], 3)]
    terms.append(jnp.zeros((out_ref.shape[0] - len(terms), out_ref.shape[1]), jnp.float32))
    out_ref[...] = jnp.concatenate(terms, axis=0).astype(jnp.bfloat16)


def diagonal(size):
    return iota((size, size), 0) == iota((size, size), 1)


def own_norm_kernel(
    slices, group_ref, half_ref, near_hbm, far_hbm, gains_hbm, out_ref, factor_ref, near, far, gain, sems
):
    tiles, tile, features = near.shape
    width = out_ref.shape[2]
    first = near_hbm.shape[0] - tiles * tile
    half, group = half_ref[0], group_ref[0]
    copies = []
    for side in range(2):
        at = pl.multiple_of((half if side == 0 else 1 - half) * features, features)
        copies.append(
            pltpu.make_async_copy(gains_hbm.at[:, pl.ds(at, features)], gain.at[side], sems.at[side])
        )
    for i in range(tiles):
        at = pl.ds(first + i * tile, tile)
        for side, (hbm, vmem) in enumerate(((near_hbm, near), (far_hbm, far))):
            copies.append(
                pltpu.make_async_copy(hbm.at[at], vmem.at[i], sems.at[2 + 2 * i + side])
            )
    for copy in copies:
        copy.start()
    copies[0].wait()
    copies[1].wait()
    factors = []
    for i in range(tiles):
        copies[2 + 2 * i].wait()
        copies[3 + 2 * i].wait()
        total = 0.0
        for ref in (near, far):
            value = ref[i].astype(jnp.float32)
            total = total + jnp.sum(value * value, axis=1, keepdims=True)
        factor = lax.rsqrt(total * (1.0 / (2 * features)) + 1e-06)
        factors.append(jnp.sum(jnp.where(diagonal(tile), factor, 0.0), axis=0, keepdims=True))
        for side, ref in enumerate((near, far)):
            for j in range(slices // 2):
                at = pl.ds(pl.multiple_of((2 * j + group) * width, LANES), width)
                block = ref[i, :, at].astype(jnp.float32) * factor * gain[side, :, at]
                out_ref[side * (slices // 2) + j, pl.ds(i * tile, tile)] = block.astype(jnp.bfloat16)
    missing = factor_ref.shape[1] - tiles * tile
    if missing:
        factors.append(jnp.zeros((1, missing), jnp.float32))
    factor_ref[...] = jnp.concatenate(factors, axis=1)


def own_norm(slices, group, half, near, far, gains, rows):
    features = near.shape[1]
    tile = NORM_TILE
    held = pltpu.VMEM((rows // tile, tile, features), jnp.bfloat16)
    return pl.pallas_call(
        functools.partial(own_norm_kernel, slices),
        out_shape=(
            jax.ShapeDtypeStruct((slices, rows, features // slices), jnp.bfloat16),
            jax.ShapeDtypeStruct((1, near.shape[0]), jnp.float32),
        ),
        in_specs=[pl.BlockSpec(memory_space=pltpu.SMEM)] * 2
        + [pl.BlockSpec(memory_space=pltpu.HBM)] * 3,
        out_specs=[pl.BlockSpec(memory_space=pltpu.VMEM)] * 2,
        scratch_shapes=[
            held,
            held,
            pltpu.VMEM((2, 1, features), jnp.float32),
            pltpu.SemaphoreType.DMA((2 + 2 * (rows // tile),)),
        ],
        compiler_params=pltpu.CompilerParams(vmem_limit_bytes=VMEM),
        cost_estimate=cost(1.2e10, 1),
    )(group, half, near, far, gains)


def other_kernel(
    first_term, first, group_ref, half_ref, index_ref, base_ref, near_ref, far_ref, factor_ref, gains_ref, *refs
):
    *weights, out_ref = refs
    slices, rows = len(weights) // 2, out_ref.shape[0]
    half, width = slices // 2, near_ref.shape[1] // (slices // 2)
    terms = factor_ref[...].astype(jnp.float32)
    factor = terms[first_term : first_term + 1]
    for k in range(1, 3):
        factor = factor + terms[first_term + k : first_term + k + 1]
    factor = jnp.sum(jnp.where(diagonal(rows), factor[:, first : first + rows], 0.0), axis=1, keepdims=True)
    total = 0.0
    for k in range(slices):
        block = index_ref[base_ref[0] + k]
        far = (block >= half).astype(jnp.int32)
        side = half_ref[0] + far - 2 * far * half_ref[0]
        lane = (2 * (side * half + block - far * half) + group_ref[0]) * width
        at = pl.ds(pl.multiple_of((block - far * half) * width, LANES), width)
        at = pl.ds(first, rows), at
        value = jnp.where(far > 0, far_ref[at], near_ref[at]).astype(jnp.float32) * factor
        value = value * gains_ref[:, pl.ds(pl.multiple_of(lane, LANES), width)]
        value = value.astype(jnp.bfloat16)
        at = 0
        for weight in weights[2 * k : 2 * k + 2]:
            depth = weight.shape[0] // LANES * LANES
            total = total + jnp.dot(
                value[:, at : at + depth], weight[:depth], preferred_element_type=jnp.float32
            )
            at += depth
    out_ref[...] = total.astype(jnp.bfloat16)


NORM_TILE = 64


def norm_kernel(blocks, half_ref, near_hbm, far_hbm, gains_hbm, out_ref, done_ref, near, far, gain, sems):
    tiles, tile, features = near.shape
    width = out_ref.shape[2]
    half = half_ref[0]
    copies = []
    for side in range(2):
        at = pl.multiple_of((half if side == 0 else 1 - half) * features, features)
        copies.append(
            pltpu.make_async_copy(gains_hbm.at[:, pl.ds(at, features)], gain.at[side], sems.at[side])
        )
    for i in range(tiles):
        at = pl.ds(i * tile, tile)
        for side, (hbm, vmem) in enumerate(((near_hbm, near), (far_hbm, far))):
            copies.append(
                pltpu.make_async_copy(hbm.at[at], vmem.at[i], sems.at[2 + 2 * i + side])
            )
    for copy in copies:
        copy.start()
    done_ref[...] = jnp.zeros_like(done_ref)
    copies[0].wait()
    copies[1].wait()
    for i in range(tiles):
        copies[2 + 2 * i].wait()
        copies[3 + 2 * i].wait()
        total = 0.0
        for ref in (near, far):
            value = ref[i].astype(jnp.float32)
            total = total + jnp.sum(value * value, axis=1, keepdims=True)
        factor = lax.rsqrt(total * (1.0 / (2 * features)) + 1e-06)
        for side, ref in enumerate((near, far)):
            for j in range(blocks // 2):
                at = pl.ds(j * width, width)
                block = ref[i, :, at].astype(jnp.float32) * factor * gain[side, :, at]
                out_ref[side * (blocks // 2) + j, pl.ds(i * tile, tile)] = block.astype(jnp.bfloat16)


def normalize(blocks, half, near, far, gains):
    rows, features = near.shape
    tile = min(NORM_TILE, rows)
    held = pltpu.VMEM((rows // tile, tile, features), jnp.bfloat16)
    return pl.pallas_call(
        functools.partial(norm_kernel, blocks),
        out_shape=(
            jax.ShapeDtypeStruct((blocks, rows, 2 * features // blocks), jnp.bfloat16),
            jax.ShapeDtypeStruct((8, LANES), jnp.float32),
        ),
        in_specs=[pl.BlockSpec(memory_space=pltpu.SMEM)]
        + [pl.BlockSpec(memory_space=pltpu.HBM)] * 3,
        out_specs=[pl.BlockSpec(memory_space=pltpu.VMEM)] * 2,
        scratch_shapes=[
            held,
            held,
            pltpu.VMEM((2, 1, features), jnp.float32),
            pltpu.SemaphoreType.DMA((2 + 2 * (rows // tile),)),
        ],
        compiler_params=pltpu.CompilerParams(vmem_limit_bytes=VMEM),
        cost_estimate=cost(1, 1),
    )(half, near, far, gains)


def pool_rows(pool_ref):
    block_rows = pool_ref.shape[1]
    pool = pool_ref[...].astype(jnp.float32)
    return jnp.concatenate([pool[:, i, :] for i in range(block_rows)], axis=0).astype(jnp.bfloat16)


def positions_in_slots(sent, source, cape):
    sources = sent.shape[0]
    slots = sources * cape
    column = iota((sources, slots), 1)
    rank = column - jnp.floor((column.astype(jnp.float32) + 0.5) * (1.0 / cape)).astype(jnp.int32) * cape
    at_source = (column >= source * cape) & (column < source * cape + cape)
    at_rank = (iota((LANES, slots), 0) == rank[:1]).astype(jnp.bfloat16)
    wide = jnp.dot(sent.astype(jnp.bfloat16), at_rank, preferred_element_type=jnp.float32)
    return jnp.sum(jnp.where(at_source, wide, 0.0), axis=0, keepdims=True).astype(jnp.int32)


def pool_kernel(cape, message_ref, pool_ref, owner_ref, fill_ref, out_ref, position_ref):
    sections, heads = out_ref.shape[0], out_ref.shape[1]
    held, block_rows, _ = pool_ref.shape
    request = iota((sections * GROUP, held), 0)
    owner = owner_ref[...]
    owned = (request >= owner * GROUP) & (request < owner * GROUP + GROUP)
    mask = jnp.concatenate(
        [(owned & (fill_ref[...] > i)).astype(jnp.float32) for i in range(block_rows)], axis=1
    )
    pool = pool_rows(pool_ref)
    for h in range(heads // GROUP):
        query = message_ref[:, h * GROUP : (h + 1) * GROUP, :].astype(jnp.float32)
        query = query.reshape(sections * GROUP, HD).astype(jnp.bfloat16)
        key = pool[:, 2 * h * HD : (2 * h + 1) * HD]
        value = pool[:, (2 * h + 1) * HD : (2 * h + 2) * HD]
        top, total, acc = attend(query, key, value, mask > 0.0)
        lane = iota((sections * GROUP, LANES), 1)
        state = jnp.where(lane == 0, top, jnp.where(lane == 1, total, 0.0))
        out_ref[:, h * GROUP : (h + 1) * GROUP, :HD] = acc.reshape(sections, GROUP, HD)
        out_ref[:, h * GROUP : (h + 1) * GROUP, HD:] = state.reshape(sections, GROUP, LANES)
    sent = message_ref[:, heads : heads + 1, :].astype(jnp.float32).reshape(sections, LANES)
    position_ref[...] = positions_in_slots(sent, iota((sections, 1), 0), cape)


def ring_pool_kernel(sections, cape, index_ref, base_ref, *refs):
    told_refs = refs[:sections]
    pool_ref, owner_ref, fill_ref, slot_ref, out_ref, position_ref, place_ref = refs[sections:]
    place_ref[...] = (iota(place_ref.shape, 0) == slot_ref[...]).astype(jnp.bfloat16)
    sources = [index_ref[base_ref[0] + sections + j] for j in range(sections)]
    held, block_rows, _ = pool_ref.shape
    heads = out_ref.shape[1] // 2
    groups = heads // GROUP
    part = told_refs[0].shape[0] - GROUP - sections
    told = [ref[part:, :].astype(jnp.float32) for ref in told_refs]
    owner, fill = owner_ref[...], fill_ref[...]
    masks = []
    for j in range(sections):
        owned = owner == sources[j]
        mask = [(owned & (fill > i)).astype(jnp.float32) for i in range(block_rows)]
        masks.append(jnp.broadcast_to(jnp.concatenate(mask, axis=1), (GROUP, held * block_rows)))
    mask = jnp.concatenate(masks, axis=0) > 0.0
    pool = pool_rows(pool_ref)
    sums, states = [], []
    lane = iota((sections * GROUP, LANES), 1)
    for h in range(groups):
        query = jnp.concatenate([t[:GROUP, h * HD : (h + 1) * HD] for t in told], axis=0)
        key = pool[:, 2 * h * HD : (2 * h + 1) * HD]
        value = pool[:, (2 * h + 1) * HD : (2 * h + 2) * HD]
        top, total, acc = attend(query.astype(jnp.bfloat16), key, value, mask)
        terms = bf16_terms(top, 3) + bf16_terms(total, 2)
        state = jnp.zeros((sections * GROUP, LANES), jnp.float32)
        for k, term in enumerate(terms):
            state = jnp.where(lane == k, term, state)
        sums.append(acc)
        states.append(state)
    for j in range(sections):
        at = slice(j * GROUP, (j + 1) * GROUP)
        rows = jnp.concatenate([x[at] for x in sums] + [x[at] for x in states], axis=0)
        out_ref[sources[j]] = rows.astype(jnp.bfloat16)
    own = iota((sections, LANES), 0) == sources[0]
    sent = jnp.concatenate(
        [
            jnp.sum(jnp.where(own, t[GROUP:, :LANES], 0.0), axis=0, keepdims=True) for t in told
        ],
        axis=0,
    )
    source = jnp.zeros((sections, 1), jnp.int32)
    for j in range(sections):
        source = jnp.where(iota((sections, 1), 0) == j, sources[j], source)
    position_ref[...] = positions_in_slots(sent, source, cape)


def bf16_terms(value, count):
    terms = []
    for _ in range(count):
        term = value.astype(jnp.bfloat16).astype(jnp.float32)
        terms.append(term)
        value = value - term
    return terms


def attend(query, key, value, mask):
    scores = (
        lax.dot_general(query, key, (((1,), (1,)), ((), ())), preferred_element_type=jnp.float32)
        * SCALE
    )
    scores = jnp.where(mask, scores, NEG)
    top = jnp.max(scores, axis=1, keepdims=True)
    expo = jnp.where(mask, jnp.exp(scores - top), 0.0)
    total = jnp.sum(expo, axis=1, keepdims=True)
    acc = jnp.dot(expo.astype(jnp.bfloat16), value, preferred_element_type=jnp.float32)
    return top, total, acc


def dots_kernel(first, count, biased, index_ref, base_ref, *refs):
    bias = 0.0
    if biased:
        bias, refs = refs[0][...], refs[1:]
    weights, refs = refs[: 2 * count], refs[2 * count :]
    kinds = len(refs) // 3 if len(refs) % 3 == 0 else len(refs) // 2
    rows_refs, given, outs = refs[:kinds], refs[kinds:-kinds], refs[-kinds:]
    pieces = (rows_refs[0].shape[2] - weights[1].shape[0], weights[1].shape[0])
    for kind, (rows_ref, out) in enumerate(zip(rows_refs, outs)):
        total = given[kind][...] + bias if given else 0.0
        for k in range(count):
            block = index_ref[base_ref[0] + first + k]
            for p, at in enumerate((slice(0, pieces[0]), slice(pieces[0], sum(pieces)))):
                total = total + jnp.dot(
                    rows_ref[block, :, at],
                    weights[2 * k + p][: pieces[p]],
                    preferred_element_type=jnp.float32,
                )
        out[...] = total.astype(out.dtype)


def last_image_kernel(image_ref, other_ref, more_ref, place_ref, partial_ref, send_out):
    sections, cape, _ = send_out.shape
    width = image_ref.shape[1]
    other = [ref[...].astype(jnp.float32) for ref in (other_ref, more_ref)]
    image = image_ref[...] + jnp.concatenate(other, axis=0)
    send = jnp.dot(place_ref[...], image.astype(jnp.bfloat16), preferred_element_type=jnp.float32)
    send_out[:, :, :width] = send.astype(jnp.bfloat16).reshape(sections, cape, width)
    send_out[:, :, width:] = partial_ref[...]


def finish_kernel(text_ref, image_ref, bias_ref, slot_ref, text_out, send_out):
    text_out[...] = (text_ref[...] + bias_ref[...]).astype(jnp.bfloat16)
    image = (image_ref[...] + bias_ref[...]).astype(jnp.bfloat16)
    place = (iota((send_out.shape[0], image.shape[0]), 0) == slot_ref[...]).astype(jnp.bfloat16)
    send_out[...] = jnp.dot(place, image, preferred_element_type=jnp.float32).astype(jnp.bfloat16)


def place_kernel(
    split, text_ref, *refs
):
    arrived_ref, position_ref, slot_ref, count_ref, rows_ref, blocks_ref = refs[-6:]
    rows, width = rows_ref.shape
    text = text_ref[...].astype(jnp.float32)
    if split:
        text = (text + refs[0][...].astype(jnp.float32)).astype(jnp.bfloat16)
        lead = jnp.zeros((rows - text.shape[0], width), jnp.float32)
        text = jnp.concatenate([lead, text.astype(jnp.float32)], axis=0)
    sections, cape, _ = arrived_ref.shape
    row = iota((rows, sections * cape), 0)
    match = (row == position_ref[...]) & (row < count_ref[0])
    filled = jnp.max(match.astype(jnp.float32), axis=1, keepdims=True) > 0.0
    arrived = arrived_ref[:, :, :width].reshape(sections * cape, width)
    placed = jnp.dot(match.astype(jnp.bfloat16), arrived, preferred_element_type=jnp.float32)
    whole = jnp.where(filled, placed, text).astype(jnp.bfloat16)
    slots = (iota((blocks_ref.shape[0], rows), 0) == slot_ref[...]).astype(jnp.bfloat16)
    blocks_ref[...] = jnp.dot(slots, whole, preferred_element_type=jnp.float32).astype(jnp.bfloat16)
    rows_ref[...] = whole


def decode_kernel(packed, rows_ref, query_ref, partial_ref, length_ref, out_ref):
    rows = rows_ref.shape[0]
    heads = query_ref.shape[1] // HD
    mask = iota((GROUP, rows), 1) < length_ref[0]
    if packed:
        partial = partial_ref[:, : 2 * heads, rows_ref.shape[1] :].astype(jnp.float32)
    for h in range(heads // GROUP):
        at = slice(h * GROUP, (h + 1) * GROUP)
        key = rows_ref[:, 2 * h * HD : (2 * h + 1) * HD]
        value = rows_ref[:, (2 * h + 1) * HD : (2 * h + 2) * HD]
        query = query_group(query_ref, h).astype(jnp.bfloat16)
        top, total, acc = attend(query, key, value, mask)
        if packed:
            old_acc = partial[:, at, :]
            state = partial[:, heads + h * GROUP : heads + (h + 1) * GROUP, :]
            old_top = state[:, :, 0:1] + state[:, :, 1:2] + state[:, :, 2:3]
            old_total = state[:, :, 3:4] + state[:, :, 4:5]
        else:
            old_acc = partial_ref[:, at, :HD]
            old_top = partial_ref[:, at, HD : HD + 1]
            old_total = partial_ref[:, at, HD + 1 : HD + 2]
        best = jnp.maximum(top, jnp.max(old_top, axis=0))
        fresh_factor = jnp.exp(top - best)
        old_factor = jnp.exp(old_top - best[None])
        total = total * fresh_factor + jnp.sum(old_total * old_factor, axis=0)
        acc = acc * fresh_factor + jnp.sum(old_acc * old_factor, axis=0)
        result = (acc / total).astype(jnp.bfloat16)
        for j in range(GROUP):
            lane = (h * GROUP + j) * HD
            out_ref[:, lane : lane + HD] = result[j : j + 1]


def beside(x):
    return lax.ppermute(x, "tensor", [(0, 1), (1, 0)])


def exchange(x):
    return lax.all_to_all(x, "section", split_axis=0, concat_axis=0, tiled=True)


def ring_order(sections):
    return list(range(0, sections, 2)) + list(range(1, sections, 2))[::-1]


def ring_tables(sections, tensors):
    order = ring_order(sections)
    table = np.zeros((sections, tensors, 2 * sections), np.int32)
    distances = [0] + [s * d for d in range(1, sections // 2) for s in (1, -1)] + [sections // 2]
    for at, section in enumerate(order):
        for step, distance in enumerate(distances):
            source = order[(at - distance) % sections]
            for t in range(tensors):
                table[section, t, step] = (source - t * (sections // tensors)) % sections
            table[section, :, sections + step] = source
    return table


def after(values, others):
    return lax.optimization_barrier((tuple(values), tuple(others)))


def ring_path(
    text, image, target, weight, bias, gains, queries, pool, owner, fill, block_owner, half, cape, capr
):
    sections = lax.axis_size("section")
    tensors = lax.axis_size("tensor")
    order = ring_order(sections)
    ahead = [(order[i], order[(i + 1) % sections]) for i in range(sections)]
    back = [(b, a) for a, b in ahead]
    depth, width = weight.shape
    piece = depth // 4
    rows = text.shape[0]
    text_rows = rows - rows // LEAST_IMAGE
    heads = queries.shape[1] // HD
    group = lax.axis_index("groups").astype(jnp.int32).reshape(1)

    def up(x):
        return lax.ppermute(x, "section", ahead)

    def down(x):
        return lax.ppermute(x, "section", back)

    def across(x):
        return lax.ppermute(x, "groups", [(0, 1), (1, 0)])

    index = jnp.asarray(ring_tables(sections, tensors).reshape(-1))
    base = (lax.axis_index("section") * tensors + lax.axis_index("tensor")) * (2 * sections)
    base = base.astype(jnp.int32).reshape(1)

    def dots(first, count, inputs, states, dtype, *added):
        parts = [*added, *(p for pair in slices[first : first + count] for p in pair)]
        shapes = tuple(jax.ShapeDtypeStruct((x.shape[1], width), dtype) for x in inputs)
        return call(
            functools.partial(dots_kernel, first, count, len(added)),
            shapes, index, base, *parts, *inputs, *states,
            smem=(0, 1), cost=cost(1.2e10 if count == 5 else 1, 1),
            aliases={2 + len(parts) + len(inputs) + k: k for k in range(len(states))},
        )

    def other_rows(first_term, near, far, first, rows):
        parts = [p for pair in slices for p in pair]
        return pl.pallas_call(
            functools.partial(other_kernel, first_term, first),
            out_shape=jax.ShapeDtypeStruct((rows, width), jnp.bfloat16),
            in_specs=[pl.BlockSpec(memory_space=pltpu.SMEM)] * 4
            + [pl.BlockSpec(memory_space=pltpu.VMEM)] * (4 + len(parts)),
            out_specs=pl.BlockSpec(memory_space=pltpu.VMEM),
            compiler_params=pltpu.CompilerParams(vmem_limit_bytes=VMEM),
            cost_estimate=cost(1, 1),
        )(group, half, index, base, near, far, factors, gains, *parts)

    spaces = [pltpu.SMEM] * 3 + [pltpu.HBM] * 6
    own_a, own_b, image_slot, block_slot, picked = pl.pallas_call(
        functools.partial(open_kernel, sections, cape, capr, pool.shape[1]),
        out_shape=(
            jax.ShapeDtypeStruct((piece + GROUP + sections, width), jnp.bfloat16),
            jax.ShapeDtypeStruct((depth // 2 - piece, width), jnp.bfloat16),
            jax.ShapeDtypeStruct((1, rows), jnp.int32),
            jax.ShapeDtypeStruct((1, block_owner.shape[1] * pool.shape[1]), jnp.int32),
            jax.ShapeDtypeStruct((rows + text_rows, text.shape[1] // 2), jnp.bfloat16),
        ),
        in_specs=[pl.BlockSpec(memory_space=space) for space in spaces],
        out_specs=[pl.BlockSpec(memory_space=pltpu.VMEM)] * 5,
        scratch_shapes=[
            pltpu.VMEM(target.shape, jnp.int32),
            pltpu.VMEM(block_owner.shape, jnp.int32),
            pltpu.VMEM(queries.shape, jnp.bfloat16),
            pltpu.SemaphoreType.DMA((5 + sections,)),
        ],
        compiler_params=pltpu.CompilerParams(vmem_limit_bytes=VMEM_ALL),
    )(group, base, half, weight, target, block_owner, queries, image, text)
    near_a = [up(own_a), down(own_a)]
    others = across(picked)
    text_far, image_far = beside(text), beside(image)
    (own_b,), (text_far, image_far) = after((own_b,), (text_far, image_far))
    near_b = [up(own_b), down(own_b)]
    last = sections // 2 - 1
    slices = [(own_a, own_b)]
    normed_image, image_factor = own_norm(sections, group, half, image, image_far, gains, rows)
    waiting, late = [image_factor], text_far
    for step in range(1, last + 1):
        near_a, waiting = after(near_a, waiting)
        held_a = near_a
        near_a = [up(near_a[0])] + ([down(near_a[1])] if step < last else [])
        near_b, waiting = after(near_b, [*waiting, late])
        *waiting, late = waiting
        slices += list(zip(held_a, near_b))
        near_b = ([up(near_b[0])] if step < last else []) + [down(near_b[1])]
        if step == 1:
            image_factor = waiting[0]
            normed_text, text_factor = own_norm(
                sections, group, half, text, late, gains, text_rows
            )
            waiting, late = [image_factor, text_factor], image_factor
        elif step == 2:
            factors = call(
                factor_kernel,
                jax.ShapeDtypeStruct((FACTOR_ROWS, rows), jnp.bfloat16),
                *waiting,
            )
            state = dots(0, 2 * step + 1, (normed_text, normed_image), (), jnp.float32)
            waiting, late = [*state], factors
    state = waiting
    (other_image, other_text, factors), last_slice = after(
        (others[:rows], others[rows:], late), (*near_a, *near_b)
    )
    slices.append(last_slice)
    image_far, factors = beside(other_image), across(factors)
    told = [a for a, _ in slices]
    partial, position, place = call(
        functools.partial(ring_pool_kernel, sections, cape),
        (
            jax.ShapeDtypeStruct((sections, 2 * heads, HD), jnp.bfloat16),
            jax.ShapeDtypeStruct((1, sections * cape), jnp.int32),
            jax.ShapeDtypeStruct((sections * cape, rows), jnp.bfloat16),
        ),
        index, base, *told, pool, owner, fill, image_slot,
        smem=(0, 1),
    )
    done = 2 * last - 1
    sums = dots(done, sections - done, (normed_text, normed_image), state, jnp.float32, bias)
    (image_far, factors), sums = after((image_far, factors), sums)
    image_back = [
        across(other_rows(0, other_image, image_far, at, rows // 2)) for at in (0, rows // 2)
    ]
    text_back = other_rows(3, other_text, beside(other_text), 0, text_rows)
    image_back, (text_back, partial, place) = after(
        image_back, (text_back, partial, place)
    )
    text_back = across(text_back)
    send = call(
        last_image_kernel,
        jax.ShapeDtypeStruct((sections, cape, width + HD), jnp.bfloat16),
        sums[1], *image_back, place, partial,
    )
    arrived = exchange(send)
    return (sums[0], text_back), arrived, position, block_slot, arrived


def gather_path(
    text, image, target, weight, bias, gains, queries, pool, owner, fill, block_owner, half, cape, capr
):
    sections = lax.axis_size("section")
    rows, near = text.shape
    width = weight.shape[1]
    heads = queries.shape[1] // HD
    image_slot, block_slot, message = call(
        functools.partial(prep_kernel, sections, cape, capr, pool.shape[1]),
        (
            jax.ShapeDtypeStruct((1, rows), jnp.int32),
            jax.ShapeDtypeStruct((1, block_owner.shape[1] * pool.shape[1]), jnp.int32),
            jax.ShapeDtypeStruct((sections, 2 * heads, LANES), jnp.bfloat16),
        ),
        target, block_owner, queries,
    )
    partial, position = call(
        functools.partial(pool_kernel, cape),
        (
            jax.ShapeDtypeStruct((sections, heads, 2 * HD), jnp.float32),
            jax.ShapeDtypeStruct((1, sections * cape), jnp.int32),
        ),
        exchange(message), pool, owner, fill,
    )
    normed = [normalize(2, half, x, beside(x), gains)[0] for x in (text, image)]
    whole = lax.all_gather(weight, "section", axis=0, tiled=True)
    first = lax.dynamic_slice_in_dim(whole, half[0] * near, near, 0)
    second = lax.dynamic_slice_in_dim(whole, (1 - half[0]) * near, near, 0)
    text_sum, image_sum = (
        jnp.dot(n[0], first, preferred_element_type=jnp.float32)
        + jnp.dot(n[1], second, preferred_element_type=jnp.float32)
        for n in normed
    )
    text_rows, send = call(
        finish_kernel,
        (
            jax.ShapeDtypeStruct((rows, width), jnp.bfloat16),
            jax.ShapeDtypeStruct((sections * cape, width), jnp.bfloat16),
        ),
        text_sum, image_sum, bias, image_slot,
    )
    arrived = exchange(send.reshape(sections, cape, width))
    return (text_rows,), arrived, position, block_slot, exchange(partial)


def shards(
    text_embed,
    image_embed,
    image_count,
    prompt_len,
    embed_target,
    kv_weight,
    kv_bias,
    norm_gain,
    queries,
    old_pool,
    pool_owner,
    pool_fill,
    block_owner,
):
    sections, tensors = lax.axis_size("section"), lax.axis_size("tensor")
    rows = text_embed.shape[0]
    width = kv_weight.shape[1]
    heads = queries.shape[1] // HD
    cape = rows // sections
    block_rows = old_pool.shape[1]
    capr = (block_owner.shape[0] + sections - 1) // sections * block_rows
    ring = (
        sections == 8
        and tensors == 2
        and lax.axis_size("groups") == 2
        and kv_weight.shape[0] == 1024
        and rows == 2 * LANES
        and cape == 2 * heads
    )
    text_rows, arrived, position, block_slot, partial = (ring_path if ring else gather_path)(
        text_embed,
        image_embed,
        embed_target.reshape(1, -1),
        kv_weight,
        kv_bias.reshape(1, -1),
        norm_gain.reshape(1, -1),
        queries,
        old_pool,
        pool_owner.reshape(1, -1),
        pool_fill.reshape(1, -1),
        block_owner.reshape(1, -1),
        lax.axis_index("tensor").astype(jnp.int32).reshape(1),
        cape,
        capr,
    )
    whole_rows, block_data = call(
        functools.partial(place_kernel, ring),
        (
            jax.ShapeDtypeStruct((rows, width), jnp.bfloat16),
            jax.ShapeDtypeStruct((sections * capr, width), jnp.bfloat16),
        ),
        *text_rows,
        arrived,
        position,
        block_slot,
        image_count,
        smem=(len(text_rows) + 3,),
    )
    fresh = exchange(block_data.reshape(sections, capr, width)).reshape(sections * capr, width)
    decoded = call(
        functools.partial(decode_kernel, ring),
        jax.ShapeDtypeStruct((1, heads * HD), jnp.bfloat16),
        whole_rows,
        queries,
        partial,
        prompt_len,
        smem=(3,),
    )
    return decoded, fresh


def solution(mesh):
    return jax.shard_map(
        shards,
        mesh=mesh,
        in_specs=(
            P(("groups", "section"), "tensor"),
            P(("groups", "section"), "tensor"),
            P(("groups", "section")),
            P(("groups", "section")),
            P(("groups", "section")),
            P("section", "tensor"),
            P("tensor"),
            P(),
            P(("groups", "section"), "tensor"),
            P(("groups", "section"), None, "tensor"),
            P(("groups", "section")),
            P(("groups", "section")),
            P(("groups", "section")),
        ),
        out_specs=(P(("groups", "section"), "tensor"), P(("groups", "section"), "tensor")),
        check_vma=False,
    )
```
